32 devices in a mesh: narrow: 4 (over y, x), wide: 8 (over z, core).
Axes of the slice: x: 2, y: 2, z: 4, core: 2. Of those that a mesh axis runs over, the one named last changes fastest.
Arguments:
- tokens: bfloat16 [32768, 1024], P(('narrow', 'wide')), may hold values from -6 to 6
- norm_gains: float32 [2, 1024], replicated, may hold values from 0.25 to 1.75
- norm_biases: float32 [2, 1024], replicated, may hold values from -2 to 2
- w_qkv: bfloat16 [1024, 3072], replicated, may hold values from -0.25 to 0.25
- w_attn_out: bfloat16 [1024, 1024], replicated, may hold values from -0.75 to 0.75
- w_in: bfloat16 [8, 1024, 4096], P('wide'), may hold values from -0.1875 to 0.1875
- w_out: bfloat16 [8, 4096, 1024], P('wide'), may hold values from -0.09375 to 0.09375
- segment_ids: int32 [32, 1024], P(('narrow', 'wide')), may hold values from 0 to 3, never falling along the last dimension, each value on 1 to 512 neighbouring positions
- expert_ids: int32 [32768], P(('narrow', 'wide')), may hold values from 0 to 7, as said below
- slots: int32 [32768], P(('narrow', 'wide')), may hold values from 0 to 144, as said below
- cotangent: bfloat16 [32768, 1024], P(('narrow', 'wide')), may hold values from -6 to 6
Outputs:
- mixed: bfloat16 [32768, 1024], P(('narrow', 'wide'))
- d_tokens: float32 [32768, 1024], P(('narrow', 'wide'))
- d_norm_gains: float32 [2, 1024], P(None, ('narrow', 'wide'))
- d_norm_biases: float32 [2, 1024], P(None, ('narrow', 'wide'))
- d_w_qkv: float32 [1024, 3072], P(None, ('narrow', 'wide'))
- d_w_attn_out: float32 [1024, 1024], P(None, ('narrow', 'wide'))
- d_w_in: float32 [8, 1024, 4096], P('wide', None, 'narrow')
- d_w_out: float32 [8, 4096, 1024], P('wide', 'narrow')
The draws below stay inside these ranges and needn't reach their ends.
Inputs may be any that keep to these rules, and one draw needn't show every extreme that they name: `expert_ids`: each token's expert, from a hash of the token. The number of earlier tokens of the same device that have the same expert, or 144 where that number is 144 or more (the token is dropped); so the retained tokens of one device and expert hold slots 0, 1, 2, ... without gaps, and on every device some expert fills all 144 slots.
All inputs are finite; a program needn't handle non-finite values.
Results may differ from the reference program's by a relative error of at most 0.012.
The reference program's roundings to bfloat16 on the way count: a program that leaves them out, or rounds other values in their place, can miss the bound.
Values may be sent and summed in bfloat16 or wider, within the bound.
No kernel may reach another device: no remote copies, remote signals or barrier semaphores. Data moves between devices by JAX's collectives and lax.ppermute only.
A program may use at most 320 MiB of HBM per device.

```python
import math
import jax
import jax.numpy as jnp
import numpy as np
from jax import lax

D = 1024
HEADS = 16
HDIM = 64
FF = 4096
LEN = 1024
SEGS = 4
TOK_DEV = 1024
TOKENS = 32768
SEQS = 32
EXPERTS = 8
CAP = 144
HOT = 180


def routing_table(key):
    blocks = TOKENS // TOK_DEV
    base_key, hot_key, order_key = jax.random.split(key, 3)
    uniform_ids = jax.random.randint(base_key, (blocks, TOK_DEV), 0, EXPERTS)
    favoured = jax.random.randint(hot_key, (), 0, EXPERTS)
    shuffled = jax.vmap(lambda subkey: jax.random.permutation(subkey, TOK_DEV))(jax.random.split(order_key, blocks))
    chosen = jnp.where(shuffled < HOT, favoured, uniform_ids).astype(jnp.int32)
    onehot = (chosen[:, :, None] == jnp.arange(EXPERTS, dtype=jnp.int32)[None, None, :]).astype(jnp.int32)
    earlier = jnp.cumsum(onehot, axis=1) - onehot
    position = jnp.sum(earlier * onehot, axis=2)
    return (chosen.reshape(TOKENS), jnp.minimum(position, CAP).reshape(TOKENS).astype(jnp.int32))


def draw_expert_ids(key, part):
    return routing_table(key)[0]


def draw_slots(key, part):
    return routing_table(key)[1]


def with_spikes(entries, stream_key, source, target, shards_of, factor):
    owner, partner = [(jnp.arange(entries.shape[dim]) // (entries.shape[dim] // shards_of)).reshape([-1 if axis == dim else 1 for axis in range(entries.ndim)]) for dim in (source, target)]
    chosen = jax.random.permutation(stream_key, shards_of)[partner]
    strong = (owner == chosen) | (owner == (partner + shards_of // 2) % shards_of)
    return jnp.where(strong, factor * entries, entries)


def block_scale(stream_key, dims, pieces, smallest, top_value):
    def one(axis_at, parts):
        draws = jax.random.uniform(jax.random.fold_in(jax.random.fold_in(stream_key, 6), axis_at), (parts,), jnp.float32, smallest / len(pieces), top_value / len(pieces))
        return jnp.repeat(jnp.exp(draws), dims[axis_at] // parts).reshape((-1,) + (1,) * (len(dims) - axis_at - 1))

    gain = one(*pieces[0])
    for cut in pieces[1:]:
        gain = gain * one(*cut)
    return gain


def length_profile(count, total, reach, skew):
    weights = [(1 << 20) // math.isqrt(grade ** skew) + 1 for grade in range(2, count + 1)]
    rest, given = total - reach - (count - 1), [1] * (count - 1)
    while rest > 0:
        free = [i for i in range(count - 1) if given[i] < reach]
        mass, budget = sum([weights[i] for i in free]), rest
        for i in free:
            extra = min(reach - given[i], max(1, budget * weights[i] // mass), rest)
            given[i] = given[i] + extra
            rest = rest - extra
    return np.array([reach] + given)


def ragged(stream_key, count, total, reach, slope):
    if count == 2:
        one = jax.random.randint(stream_key, (), max(1, total - reach), min(reach, total - 1) + 1)
        return jnp.stack([one, total - one])
    sizes = jnp.asarray(length_profile(count, total, reach, slope), jnp.int32)
    twos = (count - 1) // 2
    source_of, sink = sizes[1:1 + 2 * twos:2], sizes[2:2 + 2 * twos:2]
    slack = jnp.minimum(source_of - 1, reach - sink)
    passed = jax.random.randint(jax.random.fold_in(stream_key, 1), (twos,), 0, 1 << 20) % (slack + 1)
    sizes = sizes.at[1:1 + 2 * twos:2].set(source_of - passed).at[2:2 + 2 * twos:2].set(sink + passed)
    return sizes[jax.random.permutation(jax.random.fold_in(stream_key, 2), count)]


def normal_values(rng, dims, spread, reach, cuts=(), held_as=jnp.bfloat16):
    drawn = spread * jax.random.normal(rng, dims, jnp.float32)
    if cuts:
        drawn = drawn * block_scale(rng, dims, cuts, -0.22, 0.18)
    return jnp.clip(drawn, -reach, reach).astype(held_as)


def gaussian_with(key, shape, width, most, cuts, heavy, kind=jnp.bfloat16):
    values = width * jax.random.normal(key, shape, jnp.float32)
    if cuts:
        values = values * block_scale(key, shape, cuts, -0.22, 0.18)
    return jnp.clip(with_spikes(values, jax.random.fold_in(key, 3), *heavy), -most, most).astype(kind)


def setup_inputs(seed: int = 0) -> dict:
    keys = jax.random.split(jax.random.key(seed), 12)
    return {
        "tokens": normal_values(keys[0], (TOKENS, D), 1.0, 6.0, ((0, 32),)),
        "norm_gains": jnp.clip(1.0 + 0.15 * jax.random.normal(keys[1], (2, D), jnp.float32), 0.25, 1.75),
        "norm_biases": normal_values(keys[2], (2, D), 0.3, 2.0, (), jnp.float32),
        "w_qkv": normal_values(keys[3], (D, 3 * D), (D // 2) ** -0.5, 0.25),
        "w_attn_out": normal_values(keys[4], (D, D), (D // 16) ** -0.5, 0.75),
        "w_in": normal_values(keys[5], (EXPERTS, D, FF), D ** -0.5, 0.1875, ((0, 8),)),
        "w_out": normal_values(keys[6], (EXPERTS, FF, D), FF ** -0.5, 0.09375, ((0, 8),)),
        "segment_ids": jax.vmap(lambda own: jnp.searchsorted(jnp.cumsum(ragged(own, SEGS, LEN, LEN // 2, 0)), jnp.arange(LEN), side="right"))(jax.random.split(keys[7], SEQS)).reshape((SEQS, LEN)).astype(jnp.int32),
        "expert_ids": draw_expert_ids(jax.random.fold_in(keys[11], 71), 0),
        "slots": draw_slots(jax.random.fold_in(keys[11], 71), 0),
        "cotangent": gaussian_with(keys[10], (TOKENS, D), 1.0, 6.0, ((0, 32),), (0, 1, 32, 2.75)),
    }


EPSILON = 1e-05
NEGATIVE = -1e+30

@jax.custom_vjp
def low(v):
    return lax.optimization_barrier(v.astype(jnp.bfloat16)).astype(jnp.float32)

@jax.custom_vjp
def low_back(v):
    return v

def low_keep(v):
    return (low(v), None)

def low_pass(kept, grad):
    return (grad,)

def back_keep(v):
    return (v, None)

def back_low(kept, grad):
    return (low(grad),)
low.defvjp(low_keep, low_pass)
low_back.defvjp(back_keep, back_low)

def layer_norm(stream, norm_gain, norm_bias):
    average = lax.optimization_barrier(jnp.mean(stream, axis=-1, keepdims=True))
    centered = stream - average
    inverse = lax.rsqrt(lax.optimization_barrier(jnp.mean(centered * centered, axis=-1, keepdims=True)) + EPSILON)
    return centered * inverse * norm_gain + norm_bias

def reference(tokens, norm_gains, norm_biases, w_qkv, w_attn_out, w_in, w_out, segment_ids, expert_ids, slots, cotangent):
    highest = lax.Precision.HIGHEST
    dev_count = TOKENS // TOK_DEV
    retained = slots < CAP
    owner_dev = jnp.arange(TOKENS, dtype=jnp.int32) // TOK_DEV
    flat_slot = jnp.where(retained, (owner_dev * EXPERTS + expert_ids) * CAP + slots, dev_count * EXPERTS * CAP).astype(jnp.int32)
    positions = jnp.arange(LEN, dtype=jnp.int32)
    causal = positions[None, :] <= positions[:, None]
    score_scale = HDIM ** (-0.5)

    def attend(query_seq, key_seq, value_seq, doc_ids):
        scores = low_back(jnp.einsum('qhd,khd->hqk', query_seq, key_seq, precision=highest) * score_scale)
        allowed = causal & (doc_ids[None, :] == doc_ids[:, None])
        scores = jnp.where(allowed[None], scores, NEGATIVE)
        row_max = lax.optimization_barrier(jnp.max(scores, axis=-1, keepdims=True))
        exponent = jnp.exp(scores - row_max)
        attn_prob = exponent / lax.optimization_barrier(jnp.sum(exponent, axis=-1, keepdims=True))
        return jnp.einsum('hqk,khd->qhd', low(attn_prob), value_seq, precision=highest)

    def expert(packed):
        rows_in, weight_in, weight_out = packed
        preact = low_back(jnp.dot(rows_in, weight_in, precision=highest))
        hidden = low(jax.nn.gelu(preact))
        return low_back(low(jnp.dot(hidden, weight_out, precision=highest)))

    def attend_step(running, packed):
        return (running, jax.checkpoint(attend)(*packed))

    def forward(stream, norm_gain, norm_bias, proj_in, proj_out, expert_in, expert_out):
        normed = low(layer_norm(stream, norm_gain[0], norm_bias[0]))
        projected = low_back(low(jnp.dot(normed, proj_in, precision=highest)))
        query_all, key_all, value_all = [part_rows.reshape(SEQS, LEN, HEADS, HDIM) for part_rows in jnp.split(projected, 3, axis=1)]
        _, head_out = lax.scan(attend_step, jnp.zeros((), jnp.float32), (query_all, key_all, value_all, segment_ids))
        mixed_heads = low_back(low(head_out.reshape(TOKENS, D)))
        middle = stream + low_back(jnp.dot(mixed_heads, proj_out, precision=highest))
        sent_rows = low_back(low(layer_norm(middle, norm_gain[1], norm_bias[1])))
        buffer_rows = jnp.zeros((dev_count * EXPERTS * CAP, D), jnp.float32).at[flat_slot].set(sent_rows, mode='drop')
        per_expert = buffer_rows.reshape(dev_count, EXPERTS, CAP, D).transpose(1, 0, 2, 3).reshape(EXPERTS, dev_count * CAP, D)
        produced = lax.map(jax.checkpoint(expert), (per_expert, expert_in, expert_out))
        returned = produced.reshape(EXPERTS, dev_count, CAP, D).transpose(1, 0, 2, 3).reshape(dev_count * EXPERTS * CAP, D)
        return middle + jnp.take(returned, flat_slot, axis=0, mode='fill', fill_value=0.0)
    primals = (tokens.astype(jnp.float32), norm_gains, norm_biases, w_qkv.astype(jnp.float32), w_attn_out.astype(jnp.float32), w_in.astype(jnp.float32), w_out.astype(jnp.float32))
    result, pullback = jax.vjp(forward, *primals)
    gradients = pullback(cotangent.astype(jnp.float32))
    return (result.astype(jnp.bfloat16), gradients[0], gradients[1], gradients[2], gradients[3], gradients[4], gradients[5], gradients[6])
```

```python
import functools

import jax
import jax.numpy as jnp
from jax import lax
from jax.experimental import pallas as pl
from jax.experimental.pallas import tpu as pltpu
from jax.sharding import PartitionSpec as P

HEADS = 16
EPSILON = 1e-05
NEGATIVE = -1e30
CHUNKS = 2
BAND = 512
BLOCK = 256
F32 = jnp.float32
BF = jnp.bfloat16
VMEM_BYTES = 50 * 1024 * 1024


def mm(a, b):
    return lax.dot_general(a, b, (((1,), (0,)), ((), ())), preferred_element_type=F32)


def mm_nt(a, b):
    return lax.dot_general(a, b, (((1,), (1,)), ((), ())), preferred_element_type=F32)


def mm_tn(a, b):
    return lax.dot_general(a, b, (((0,), (0,)), ((), ())), preferred_element_type=F32)


def call(kernel, grid, in_specs, out_specs, out_shape, scratch=(), prefetch=0, flops=0, nbytes=0):
    return pl.pallas_call(
        kernel,
        grid_spec=pltpu.PrefetchScalarGridSpec(
            num_scalar_prefetch=prefetch,
            grid=grid,
            in_specs=in_specs,
            out_specs=out_specs,
            scratch_shapes=list(scratch),
        ),
        out_shape=out_shape,
        compiler_params=pltpu.CompilerParams(vmem_limit_bytes=VMEM_BYTES),
        cost_estimate=pl.CostEstimate(flops=flops, bytes_accessed=nbytes, transcendentals=0),
    )


def whole(shape):
    return pl.BlockSpec(shape, lambda *_: (0,) * len(shape))


def normalize(stream):
    average = jnp.mean(stream, axis=-1, keepdims=True)
    centered = stream - average
    inverse = lax.rsqrt(jnp.mean(centered * centered, axis=-1, keepdims=True) + EPSILON)
    return centered * inverse, inverse


def norm_back(unit, inverse, gain, grad):
    scaled = grad * gain
    first = jnp.mean(scaled, axis=-1, keepdims=True)
    second = jnp.mean(scaled * unit, axis=-1, keepdims=True)
    return inverse * (scaled - first - unit * second)


def qkv_kernel(x_ref, g_ref, b_ref, w_ref, n_ref, p_ref):
    rows = x_ref.shape[0]

    @pl.when(pl.program_id(0) == 0)
    def _():
        def step(i, _):
            at = pl.ds(i * 128, 128)
            unit, _inv = normalize(x_ref[at, :].astype(F32))
            n_ref[at, :] = (unit * g_ref[0:1, :] + b_ref[0:1, :]).astype(BF)
            return 0

        lax.fori_loop(0, rows // 128, step, 0)

    p_ref[...] = mm(n_ref[...], w_ref[...]).astype(BF)


def qkv(tokens, gains, biases, w_qkv):
    rows, dim = tokens.shape
    cols = w_qkv.shape[1]
    tile = 512
    return call(
        qkv_kernel,
        (cols // tile,),
        [whole((rows, dim)), whole(gains.shape), whole(biases.shape), pl.BlockSpec((dim, tile), lambda j: (0, j))],
        [whole((rows, dim)), pl.BlockSpec((rows, tile), lambda j: (0, j))],
        [jax.ShapeDtypeStruct((rows, dim), BF), jax.ShapeDtypeStruct((rows, cols), BF)],
        flops=2 * rows * dim * cols,
        nbytes=2 * (2 * rows * dim + dim * cols + rows * cols),
    )(tokens, gains, biases, w_qkv)


def spans(length):
    out = []
    for q_first in range(0, length, BLOCK):
        out.append((q_first, max(0, q_first - BAND)))
    return out


def fill_bias(bias_ref, doc_row, doc_col, length):
    at = 0
    for q_first, k_first in spans(length):
        keys = q_first + BLOCK - k_first
        key_pos = k_first + lax.broadcasted_iota(jnp.int32, (keys, BLOCK), 0)
        query_pos = q_first + lax.broadcasted_iota(jnp.int32, (keys, BLOCK), 1)
        same = doc_col[k_first : k_first + keys, :] == doc_row[:, q_first : q_first + BLOCK]
        bias_ref[at : at + keys, :] = jnp.where((key_pos <= query_pos) & same, 0.0, NEGATIVE).astype(F32)
        at += keys


def bias_rows(length):
    return sum(q + BLOCK - k for q, k in spans(length))


def head_lanes(block, head, head_dim):
    lane = lax.broadcasted_iota(jnp.int32, block.shape, 1)
    inside = (lane >= head * head_dim) & (lane < (head + 1) * head_dim)
    return jnp.where(inside, block, jnp.zeros_like(block))


def attn_fwd_kernel(head_dim, row_ref, col_ref, q_ref, k_ref, v_ref, o_ref, lse_ref, bias_ref):
    length = q_ref.shape[0]
    pair = q_ref.shape[1]
    scale = head_dim**-0.5

    @pl.when(pl.program_id(0) == 0)
    def _():
        fill_bias(bias_ref, row_ref[...], col_ref[...], length)

    value_t = v_ref[...].T
    at = 0
    for q_first, k_first in spans(length):
        keys = q_first + BLOCK - k_first
        q_at = slice(q_first, q_first + BLOCK)
        k_at = slice(k_first, k_first + keys)
        query = q_ref[q_at, :] * BF(scale)
        bias = bias_ref[at : at + keys, :]
        outs = []
        for head in range(pair // head_dim):
            scores = mm_nt(k_ref[k_at, :], head_lanes(query, head, head_dim)) + bias
            top = jnp.max(scores, axis=0, keepdims=True)
            exponent = jnp.exp(scores - top)
            total = jnp.sum(exponent, axis=0, keepdims=True)
            part = mm(value_t[head * head_dim : (head + 1) * head_dim, k_at], exponent.astype(BF))
            outs.append(part / total)
            lse_ref[0, head : head + 1, q_at] = top + jnp.log(total)
        o_ref[q_at, :] = jnp.concatenate(outs, axis=0).T.astype(BF)
        at += keys


def attn_fwd(projected, doc_row, doc_col, head_dim):
    length = projected.shape[0]
    width = projected.shape[1] // 3
    pair = 128
    pairs = width // pair
    per = pair // head_dim
    specs = [pl.BlockSpec((length, pair), functools.partial(lambda s, j: (0, s * pairs + j), s)) for s in range(3)]
    return call(
        functools.partial(attn_fwd_kernel, head_dim),
        (pairs,),
        [whole(doc_row.shape), whole(doc_col.shape)] + specs,
        [pl.BlockSpec((length, pair), lambda j: (0, j)), pl.BlockSpec((1, per, length), lambda j: (j, 0, 0))],
        [jax.ShapeDtypeStruct((length, width), BF), jax.ShapeDtypeStruct((pairs, per, length), F32)],
        scratch=[pltpu.VMEM((bias_rows(length), BLOCK), F32)],
        flops=8 * bias_rows(length) * BLOCK * width,
        nbytes=8 * length * width,
    )(doc_row, doc_col, projected, projected, projected)


def attn_bwd_kernel(head_dim, row_ref, col_ref, q_ref, k_ref, v_ref, do_ref, lse_ref, dq_ref, dk_ref, dv_ref, bias_ref, dk_sum, dv_sum):
    length = q_ref.shape[0]
    pair = q_ref.shape[1]
    scale = head_dim**-0.5

    @pl.when(pl.program_id(0) == 0)
    def _():
        fill_bias(bias_ref, row_ref[...], col_ref[...], length)

    key_t = (k_ref[...] * BF(scale)).T
    dk_sum[...] = jnp.zeros_like(dk_sum)
    dv_sum[...] = jnp.zeros_like(dv_sum)
    at = 0
    for q_first, k_first in spans(length):
        keys = q_first + BLOCK - k_first
        q_at = slice(q_first, q_first + BLOCK)
        k_at = slice(k_first, k_first + keys)
        query = q_ref[q_at, :] * BF(scale)
        grad = do_ref[q_at, :]
        bias = bias_ref[at : at + keys, :]
        dq_parts = []
        dk_part = None
        dv_part = None
        for head in range(pair // head_dim):
            query_one = head_lanes(query, head, head_dim)
            grad_one = head_lanes(grad, head, head_dim)
            scores = mm_nt(k_ref[k_at, :], query_one) + bias
            prob = jnp.exp(scores - lse_ref[0, head : head + 1, q_at])
            prob_grad = mm_nt(v_ref[k_at, :], grad_one)
            inner = jnp.sum(prob * prob_grad, axis=0, keepdims=True)
            score_grad = (prob * (prob_grad - inner)).astype(BF)
            dv_one = mm(prob.astype(BF), grad_one)
            dk_one = mm(score_grad, query_one)
            dv_part = dv_one if dv_part is None else dv_part + dv_one
            dk_part = dk_one if dk_part is None else dk_part + dk_one
            dq_parts.append(mm(key_t[head * head_dim : (head + 1) * head_dim, k_at], score_grad))
        dk_sum[k_at, :] += dk_part
        dv_sum[k_at, :] += dv_part
        dq_ref[q_at, :] = jnp.concatenate(dq_parts, axis=0).T.astype(BF)
        at += keys
    dk_ref[...] = dk_sum[...].astype(BF)
    dv_ref[...] = dv_sum[...].astype(BF)


def attn_bwd(projected, grad_heads, log_total, doc_row, doc_col, head_dim):
    length = projected.shape[0]
    width = projected.shape[1] // 3
    pair = 128
    pairs = width // pair
    per = pair // head_dim
    specs = [pl.BlockSpec((length, pair), functools.partial(lambda s, j: (0, s * pairs + j), s)) for s in range(3)]
    one = pl.BlockSpec((length, pair), lambda j: (0, j))
    return call(
        functools.partial(attn_bwd_kernel, head_dim),
        (pairs,),
        [whole(doc_row.shape), whole(doc_col.shape)]
        + specs
        + [one, pl.BlockSpec((1, per, length), lambda j: (j, 0, 0))],
        [one, one, one],
        [jax.ShapeDtypeStruct((length, width), BF)] * 3,
        scratch=[
            pltpu.VMEM((bias_rows(length), BLOCK), F32),
            pltpu.VMEM((length, pair), F32),
            pltpu.VMEM((length, pair), F32),
        ],
        flops=20 * bias_rows(length) * BLOCK * width,
        nbytes=14 * length * width,
    )(doc_row, doc_col, projected, projected, projected, grad_heads, log_total)


def middle_kernel(x_ref, h_ref, w_ref, g_ref, b_ref, m_ref, s_ref):
    middle = x_ref[...].astype(F32) + mm(h_ref[...], w_ref[...])
    m_ref[...] = middle
    unit, _inv = normalize(middle)
    s_ref[...] = (unit * g_ref[1:2, :] + b_ref[1:2, :]).astype(BF)


def make_middle(tokens, mixed_heads, w_attn_out, gains, biases):
    rows, dim = tokens.shape
    tile = 256
    block = pl.BlockSpec((tile, dim), lambda i: (i, 0))
    return call(
        middle_kernel,
        (rows // tile,),
        [block, block, whole(w_attn_out.shape), whole(gains.shape), whole(biases.shape)],
        [block, block],
        [jax.ShapeDtypeStruct((rows, dim), F32), jax.ShapeDtypeStruct((rows, dim), BF)],
        flops=2 * rows * dim * dim,
        nbytes=12 * rows * dim,
    )(tokens, mixed_heads, w_attn_out, gains, biases)


def dispatch_kernel(place_ref, x_ref, o_ref):
    tile = o_ref.shape[0]
    slot = pl.program_id(0) * tile + lax.broadcasted_iota(jnp.int32, (tile, place_ref.shape[1]), 0)
    pick = jnp.where(slot == place_ref[...], 1.0, 0.0).astype(BF)
    o_ref[...] = mm(pick, x_ref[...]).astype(BF)


def dispatch_rows(place_row, rows, count):
    dim = rows.shape[1]
    tile = 384
    return call(
        dispatch_kernel,
        (count // tile,),
        [whole(place_row.shape), whole(rows.shape)],
        pl.BlockSpec((tile, dim), lambda i: (i, 0)),
        jax.ShapeDtypeStruct((count, dim), BF),
        flops=2 * rows.shape[0] * count * dim,
        nbytes=2 * dim * (rows.shape[0] + count),
    )(place_row, rows)


def pick_rows(place, back):
    slot = lax.broadcasted_iota(jnp.int32, (place.shape[0], back.shape[0]), 1)
    return mm(jnp.where(slot == place, 1.0, 0.0).astype(BF), back)


def mixed_kernel(place_ref, m_ref, r_ref, o_ref):
    o_ref[...] = (m_ref[...] + pick_rows(place_ref[...], r_ref[...])).astype(BF)


def make_mixed(place_col, middle, back):
    rows, dim = middle.shape
    tile = 256
    block = pl.BlockSpec((tile, dim), lambda i: (i, 0))
    return call(
        mixed_kernel,
        (rows // tile,),
        [pl.BlockSpec((tile, 1), lambda i: (i, 0)), block, whole(back.shape)],
        block,
        jax.ShapeDtypeStruct((rows, dim), BF),
        flops=2 * rows * back.shape[0] * dim,
        nbytes=8 * rows * dim,
    )(place_col, middle, back)


def second_back_kernel(place_ref, m_ref, c_ref, r_ref, w_ref, g_ref, gm_ref, ga_ref, gh_ref, sums_ref):
    grad_sent = pick_rows(place_ref[...], r_ref[...])
    unit, inverse = normalize(m_ref[...])
    grad_middle = c_ref[...].astype(F32) + norm_back(unit, inverse, g_ref[1:2, :], grad_sent)
    gm_ref[...] = grad_middle
    grad_attn = grad_middle.astype(BF)
    ga_ref[...] = grad_attn
    gh_ref[...] = mm_nt(grad_attn, w_ref[...]).astype(BF)
    sums = jnp.concatenate(
        [jnp.sum(grad_sent * unit, axis=0, keepdims=True), jnp.sum(grad_sent, axis=0, keepdims=True)], axis=0
    )

    @pl.when(pl.program_id(0) == 0)
    def _():
        sums_ref[...] = sums

    @pl.when(pl.program_id(0) > 0)
    def _():
        sums_ref[...] += sums


def second_back(place_col, middle, cotangent, back, w_attn_out, gains):
    rows, dim = middle.shape
    tile = 256
    block = pl.BlockSpec((tile, dim), lambda i: (i, 0))
    return call(
        second_back_kernel,
        (rows // tile,),
        [
            pl.BlockSpec((tile, 1), lambda i: (i, 0)),
            block,
            block,
            whole(back.shape),
            whole(w_attn_out.shape),
            whole(gains.shape),
        ],
        [block, block, block, whole((2, dim))],
        [
            jax.ShapeDtypeStruct((rows, dim), F32),
            jax.ShapeDtypeStruct((rows, dim), BF),
            jax.ShapeDtypeStruct((rows, dim), BF),
            jax.ShapeDtypeStruct((2, dim), F32),
        ],
        flops=2 * rows * (back.shape[0] + dim) * dim,
        nbytes=16 * rows * dim,
    )(place_col, middle, cotangent, back, w_attn_out, gains)


def first_back_kernel(x_ref, gm_ref, dq_ref, dk_ref, dv_ref, w_ref, g_ref, dx_ref, sums_ref):
    dim = x_ref.shape[1]
    grad_normed = mm_nt(dq_ref[...], w_ref[:, :dim])
    grad_normed += mm_nt(dk_ref[...], w_ref[:, dim : 2 * dim])
    grad_normed += mm_nt(dv_ref[...], w_ref[:, 2 * dim :])
    unit, inverse = normalize(x_ref[...].astype(F32))
    dx_ref[...] = gm_ref[...] + norm_back(unit, inverse, g_ref[0:1, :], grad_normed)
    sums = jnp.concatenate(
        [jnp.sum(grad_normed * unit, axis=0, keepdims=True), jnp.sum(grad_normed, axis=0, keepdims=True)], axis=0
    )

    @pl.when(pl.program_id(0) == 0)
    def _():
        sums_ref[...] = sums

    @pl.when(pl.program_id(0) > 0)
    def _():
        sums_ref[...] += sums


def first_back(tokens, grad_middle, grads, w_qkv, gains):
    rows, dim = tokens.shape
    tile = 256
    block = pl.BlockSpec((tile, dim), lambda i: (i, 0))
    return call(
        first_back_kernel,
        (rows // tile,),
        [block, block, block, block, block, whole(w_qkv.shape), whole(gains.shape)],
        [block, whole((2, dim))],
        [jax.ShapeDtypeStruct((rows, dim), F32), jax.ShapeDtypeStruct((2, dim), F32)],
        flops=6 * rows * dim * dim,
        nbytes=22 * rows * dim,
    )(tokens, grad_middle, *grads, w_qkv, gains)


def expert_kernel(x_ref, c_ref, wi_ref, wo_ref, h_ref, gp_ref, out_ref, gr_ref, out_sum, gr_sum):
    step = pl.program_id(0)
    preact = mm(x_ref[...], wi_ref[...])
    grad_hidden = mm_nt(c_ref[...], wo_ref[...])
    slope = 0.7978845608028654
    square = preact * preact
    tanh = jnp.tanh(preact * (slope + (slope * 0.044715) * square))
    half = 0.5 + 0.5 * tanh
    hidden = preact * half
    gate = half + hidden * (1.0 - tanh) * (slope + (3.0 * slope * 0.044715) * square)
    hidden_low = hidden.astype(BF)
    grad_low = (gate * grad_hidden).astype(BF)
    h_ref[...] = hidden_low
    gp_ref[...] = grad_low
    out_part = mm(hidden_low, wo_ref[...])
    gr_part = mm_nt(grad_low, wi_ref[...])

    @pl.when(step == 0)
    def _():
        out_sum[...] = out_part
        gr_sum[...] = gr_part

    @pl.when(step > 0)
    def _():
        out_sum[...] += out_part
        gr_sum[...] += gr_part

    @pl.when(step == pl.num_programs(0) - 1)
    def _():
        out_ref[...] = out_sum[...].astype(BF)
        gr_ref[...] = gr_sum[...].astype(BF)


def expert(rows, grads, w_in, w_out):
    count, dim = rows.shape
    units = w_in.shape[1]
    tile = 512
    act = pl.BlockSpec((count, tile), lambda j: (0, j))
    return call(
        expert_kernel,
        (units // tile,),
        [
            whole(rows.shape),
            whole(grads.shape),
            pl.BlockSpec((dim, tile), lambda j: (0, j)),
            pl.BlockSpec((tile, dim), lambda j: (j, 0)),
        ],
        [act, act, whole(rows.shape), whole(rows.shape)],
        [
            jax.ShapeDtypeStruct((count, units), BF),
            jax.ShapeDtypeStruct((count, units), BF),
            jax.ShapeDtypeStruct((count, dim), BF),
            jax.ShapeDtypeStruct((count, dim), BF),
        ],
        scratch=[pltpu.VMEM((count, dim), F32), pltpu.VMEM((count, dim), F32)],
        flops=8 * count * dim * units,
        nbytes=4 * dim * units + 4 * count * units,
    )(rows, grads, w_in, w_out)


def outer_kernel(count, *refs):
    o_ref = refs[-1]
    total = mm_tn(refs[1][...], refs[1 + count][...])
    for i in range(1, count):
        total += mm_tn(refs[1 + i][...], refs[1 + count + i][...])
    o_ref[0] = total.astype(BF)


def outer(first, second, table, first_tile, second_tile, steps):
    count = len(first)
    first_cols = first_tile or first[0].shape[1]
    second_cols = second_tile or second[0].shape[1]
    return call(
        functools.partial(outer_kernel, count),
        (steps,),
        [pl.BlockSpec((a.shape[0], first_cols), lambda i, t: (0, t[0, i])) for a in first]
        + [pl.BlockSpec((a.shape[0], second_cols), lambda i, t: (0, t[1, i])) for a in second],
        pl.BlockSpec((1, first_cols, second_cols), lambda i, t: (i, 0, 0)),
        jax.ShapeDtypeStruct((steps, first_cols, second_cols), BF),
        prefetch=1,
        flops=2 * steps * first_cols * second_cols * sum(a.shape[0] for a in first),
        nbytes=2 * steps * first_cols * second_cols,
    )(table, *first, *second)


def swap(value, axis, mask):
    size = lax.axis_size(axis)
    return lax.ppermute(value, axis, [(i, i ^ mask) for i in range(size)])


def exchange(rows, axis):
    size = lax.axis_size(axis)
    blocks = rows.reshape(size, rows.shape[0] // size, rows.shape[1])
    parts = [blocks[0]] + [swap(blocks[p], axis, p) for p in range(1, size)]
    return jnp.concatenate(parts, axis=0)


def split_sum(value, dim, axis, mask):
    bit = jnp.where((lax.axis_index(axis) & mask) > 0, 1, 0)
    mine = lax.dynamic_index_in_dim(value, bit, dim, keepdims=False)
    other = lax.dynamic_index_in_dim(value, 1 - bit, dim, keepdims=False)
    return (mine.astype(F32) + swap(other, axis, mask).astype(F32)).astype(value.dtype)


def bits_of(size):
    return [1 << i for i in range(size.bit_length() - 1)]


def on_device(
    tokens,
    norm_gains,
    norm_biases,
    w_qkv,
    w_attn_out,
    w_in,
    w_out,
    segment_ids,
    expert_ids,
    slots,
    cotangent,
):
    tok, dim = tokens.shape
    head_dim = dim // HEADS
    wide = lax.axis_size("wide")
    narrow = lax.axis_size("narrow")
    units = w_in.shape[2]
    me_wide = lax.axis_index("wide")
    me_narrow = lax.axis_index("narrow")
    capacity = tok * 9 // (8 * wide)
    count = wide * capacity
    part_slots = capacity // CHUNKS
    part_rows = wide * part_slots
    w_in = w_in[0]
    w_out = w_out[0]

    place = (slots // part_slots) * part_rows + (expert_ids ^ me_wide) * part_slots + slots % part_slots
    place = jnp.where(slots < capacity, place, count).astype(jnp.int32)
    place_row = place[None, :]
    place_col = place[:, None]
    doc_row = segment_ids
    doc_col = segment_ids.reshape(tok, 1)

    sent_grads = dispatch_rows(place_row, cotangent, count)
    expert_grads = [exchange(sent_grads[c * part_rows : (c + 1) * part_rows], "wide") for c in range(CHUNKS)]

    normed, projected = qkv(tokens, norm_gains, norm_biases, w_qkv)
    mixed_heads, log_total = attn_fwd(projected, doc_row, doc_col, head_dim)
    middle, sent = make_middle(tokens, mixed_heads, w_attn_out, norm_gains, norm_biases)
    sent_rows = dispatch_rows(place_row, sent, count)
    expert_rows = [exchange(sent_rows[c * part_rows : (c + 1) * part_rows], "wide") for c in range(CHUNKS)]

    done = [expert(expert_rows[c], expert_grads[c], w_in, w_out) for c in range(CHUNKS)]
    hidden = [d[0] for d in done]
    grad_preact = [d[1] for d in done]
    back_grads = jnp.concatenate([exchange(d[3], "wide") for d in done], axis=0)
    back_rows = jnp.concatenate([exchange(d[2], "wide") for d in done], axis=0)

    quarter = units // narrow
    half = quarter // 2
    half_dim = dim // 2
    order = [0, 2, 1, 3]

    def place_table(firsts, seconds):
        return jnp.stack([jnp.stack(firsts), jnp.stack(seconds)]).astype(jnp.int32)

    zero = jnp.int32(0)

    def out_tiles(side, positions):
        table = place_table([2 * (me_narrow ^ p) + side for p in positions], [zero for _ in positions])
        return outer(hidden, expert_grads, table, half, None, len(positions))

    def in_tiles(side, positions):
        table = place_table([zero + side for _ in positions], [me_narrow ^ p for p in positions])
        return outer(expert_rows, grad_preact, table, half_dim, quarter, len(positions))

    def narrow_sum(tiles, side):
        masks = [1, 2] if side == 0 else [2, 1]
        first, second = masks
        send = tiles(side, [first, 3])
        keep = tiles(side, [0, second])
        got = swap(send, "narrow", first)
        again = (keep[1].astype(F32) + got[1].astype(F32)).astype(BF)
        last = swap(again, "narrow", second)
        return keep[0].astype(F32) + got[0].astype(F32) + last.astype(F32)

    d_w_out = jnp.concatenate([narrow_sum(out_tiles, 0), narrow_sum(out_tiles, 1)], axis=0)
    d_w_in = jnp.concatenate([narrow_sum(in_tiles, 0), narrow_sum(in_tiles, 1)], axis=0)

    mixed = make_mixed(place_col, middle, back_rows)
    grad_middle, grad_attn, grad_heads, sums_two = second_back(
        place_col, middle, cotangent, back_grads, w_attn_out, norm_gains
    )
    grads = attn_bwd(projected, grad_heads, log_total, doc_row, doc_col, head_dim)
    d_tokens, sums_one = first_back(tokens, grad_middle, grads, w_qkv, norm_gains)

    owners = narrow * wide

    def transposed(first, second):
        steps = first.shape[1] // 512
        table = place_table([jnp.int32(i) for i in range(steps)], [zero for _ in range(steps)])
        return outer([first], [second], table, 512, None, steps).reshape(first.shape[1], second.shape[1])

    d_qkv_t = jnp.concatenate([transposed(g, normed) for g in grads], axis=0)
    d_out_t = transposed(grad_attn, mixed_heads)
    own_qkv = 3 * dim // owners
    own_out = dim // owners
    joined = jnp.concatenate(
        [d_qkv_t.reshape(owners, own_qkv, dim), d_out_t.reshape(owners, own_out, dim)], axis=1
    )
    n_bits = bits_of(narrow)
    w_bits = bits_of(wide)
    shape = (2,) * (len(n_bits) + len(w_bits)) + (own_qkv + own_out, dim)
    value = joined.reshape(shape)
    names = [("narrow", b) for b in reversed(n_bits)] + [("wide", b) for b in reversed(w_bits)]
    steps = [("wide", 1), ("narrow", 1), ("narrow", 2)] + [("wide", b) for b in w_bits[1:]]
    for step in steps:
        dim_at = names.index(step)
        value = split_sum(value, dim_at, *step)
        names.pop(dim_at)
    d_w_qkv = value[:own_qkv].T.astype(F32)
    d_w_attn_out = value[own_qkv:].T.astype(F32)

    sums = jnp.concatenate([sums_one[0:1], sums_two[0:1], sums_one[1:2], sums_two[1:2]], axis=0)
    sums = lax.psum_scatter(sums, ("narrow", "wide"), scatter_dimension=1, tiled=True)
    return (mixed, d_tokens, sums[:2], sums[2:], d_w_qkv, d_w_attn_out, d_w_in[None], d_w_out[None])


def solution(mesh):
    placed = (
        P(("narrow", "wide"), None),
        P(),
        P(),
        P(),
        P(),
        P("wide", None, None),
        P("wide", None, None),
        P(("narrow", "wide"), None),
        P(("narrow", "wide")),
        P(("narrow", "wide")),
        P(("narrow", "wide"), None),
    )
    return jax.shard_map(
        on_device,
        mesh=mesh,
        in_specs=placed,
        out_specs=(
            P(("narrow", "wide"), None),
            P(("narrow", "wide"), None),
            P(None, ("narrow", "wide")),
            P(None, ("narrow", "wide")),
            P(None, ("narrow", "wide")),
            P(None, ("narrow", "wide")),
            P("wide", None, "narrow"),
            P("wide", "narrow", None),
        ),
        check_vma=False,
    )
```

```python
import functools

import jax
import jax.numpy as jnp
from jax import lax
from jax.experimental import pallas as pl
from jax.experimental.pallas import tpu as pltpu
from jax.sharding import PartitionSpec as P

HEADS = 16
EPSILON = 1e-05
NEGATIVE = -1e30
BAND = 512
BLOCK = 256
SUB = 256
F32 = jnp.float32
BF = jnp.bfloat16
VMEM_BYTES = 60 * 1024 * 1024


def mm(a, b):
    return lax.dot_general(a, b, (((1,), (0,)), ((), ())), preferred_element_type=F32)


def mm_nt(a, b):
    return lax.dot_general(a, b, (((1,), (1,)), ((), ())), preferred_element_type=F32)


def mm_tn(a, b):
    return lax.dot_general(a, b, (((0,), (0,)), ((), ())), preferred_element_type=F32)


def call(kernel, grid, in_specs, out_specs, out_shape, scratch=(), prefetch=0, aliases=None, after=(), cost=0):
    count = prefetch + len(in_specs)
    extra = len(after)

    def body(*refs):
        kernel(*refs[:count], *refs[count + extra :])

    run = pl.pallas_call(
        body,
        grid_spec=pltpu.PrefetchScalarGridSpec(
            num_scalar_prefetch=prefetch,
            grid=grid,
            in_specs=list(in_specs) + [pl.BlockSpec(memory_space=pl.ANY)] * extra,
            out_specs=out_specs,
            scratch_shapes=list(scratch),
        ),
        out_shape=out_shape,
        input_output_aliases=aliases or {},
        compiler_params=pltpu.CompilerParams(vmem_limit_bytes=VMEM_BYTES),
        cost_estimate=pl.CostEstimate(flops=1 + int(cost * 1.15e9), bytes_accessed=0, transcendentals=0),
    )
    return lambda *args: run(*args, *after)


def whole(shape):
    return pl.BlockSpec(shape, lambda *_: (0,) * len(shape))


def normalize(stream):
    average = jnp.mean(stream, axis=-1, keepdims=True)
    centered = stream - average
    inverse = lax.rsqrt(jnp.mean(centered * centered, axis=-1, keepdims=True) + EPSILON)
    return centered * inverse, inverse


def norm_back(unit, inverse, gain, grad):
    scaled = grad * gain
    first = jnp.mean(scaled, axis=-1, keepdims=True)
    second = jnp.mean(scaled * unit, axis=-1, keepdims=True)
    return inverse * (scaled - first - unit * second)


def first_norm_kernel(x_ref, g_ref, b_ref, n_ref):
    unit, _inverse = normalize(x_ref[...].astype(F32))
    n_ref[...] = (unit * g_ref[0:1, :] + b_ref[0:1, :]).astype(BF)


def first_norm(tokens, gains, biases, after=(), cost=0):
    rows, dim = tokens.shape
    block = pl.BlockSpec((256, dim), lambda i: (i, 0))
    return call(
        first_norm_kernel,
        (rows // 256,),
        [block, whole(gains.shape), whole(biases.shape)],
        block,
        jax.ShapeDtypeStruct((rows, dim), BF),
        after=after,
        cost=cost,
    )(tokens, gains, biases)


def project_kernel(n_ref, w_ref, p_ref):
    p_ref[...] = mm(n_ref[...], w_ref[...]).astype(BF)


def project(normed, w_qkv, after=(), cost=0):
    rows, dim = normed.shape
    cols = w_qkv.shape[1]
    tile = 768
    return call(
        project_kernel,
        (cols // tile,),
        [whole((rows, dim)), pl.BlockSpec((dim, tile), lambda j: (0, j))],
        pl.BlockSpec((rows, tile), lambda j: (0, j)),
        jax.ShapeDtypeStruct((rows, cols), BF),
        after=after,
        cost=cost,
    )(normed, w_qkv)


def spans(length):
    out = []
    for q_first in range(0, length, BLOCK):
        out.append((q_first, max(0, q_first - BAND)))
    return out


def fill_bias(bias_ref, doc_row, doc_col, length):
    at = 0
    for q_first, k_first in spans(length):
        keys = q_first + BLOCK - k_first
        key_pos = k_first + lax.broadcasted_iota(jnp.int32, (keys, BLOCK), 0)
        query_pos = q_first + lax.broadcasted_iota(jnp.int32, (keys, BLOCK), 1)
        same = doc_col[k_first : k_first + keys, :] == doc_row[:, q_first : q_first + BLOCK]
        bias_ref[at : at + keys, :] = jnp.where((key_pos <= query_pos) & same, 0.0, NEGATIVE).astype(F32)
        at += keys


def bias_rows(length):
    return sum(q + BLOCK - k for q, k in spans(length))


def head_lanes(block, head, head_dim):
    lane = lax.broadcasted_iota(jnp.int32, block.shape, 1)
    inside = (lane >= head * head_dim) & (lane < (head + 1) * head_dim)
    return jnp.where(inside, block, jnp.zeros_like(block))


def attn_fwd_kernel(head_dim, row_ref, col_ref, q_ref, k_ref, v_ref, o_ref, lse_ref, bias_ref):
    length = q_ref.shape[0]
    pair = q_ref.shape[1]
    scale = head_dim**-0.5

    @pl.when(pl.program_id(0) == 0)
    def _():
        fill_bias(bias_ref, row_ref[...], col_ref[...], length)

    value_t = v_ref[...].T
    at = 0
    for q_first, k_first in spans(length):
        keys = q_first + BLOCK - k_first
        q_at = slice(q_first, q_first + BLOCK)
        k_at = slice(k_first, k_first + keys)
        query = q_ref[q_at, :] * BF(scale)
        bias = bias_ref[at : at + keys, :]
        outs = []
        for head in range(pair // head_dim):
            scores = mm_nt(k_ref[k_at, :], head_lanes(query, head, head_dim)) + bias
            top = jnp.max(scores, axis=0, keepdims=True)
            exponent = jnp.exp(scores - top)
            total = jnp.sum(exponent, axis=0, keepdims=True)
            part = mm(value_t[head * head_dim : (head + 1) * head_dim, k_at], exponent.astype(BF))
            outs.append(part / total)
            lse_ref[0, head : head + 1, q_at] = top + jnp.log(total)
        o_ref[q_at, :] = jnp.concatenate(outs, axis=0).T.astype(BF)
        at += keys


def attn_fwd(projected, doc_row, doc_col, head_dim, cost=0):
    length = projected.shape[0]
    width = projected.shape[1] // 3
    pair = 128
    pairs = width // pair
    per = pair // head_dim
    specs = [pl.BlockSpec((length, pair), functools.partial(lambda s, j: (0, s * pairs + j), s)) for s in range(3)]
    return call(
        functools.partial(attn_fwd_kernel, head_dim),
        (pairs,),
        [whole(doc_row.shape), whole(doc_col.shape)] + specs,
        [pl.BlockSpec((length, pair), lambda j: (0, j)), pl.BlockSpec((1, per, length), lambda j: (j, 0, 0))],
        [jax.ShapeDtypeStruct((length, width), BF), jax.ShapeDtypeStruct((pairs, per, length), F32)],
        scratch=[pltpu.VMEM((bias_rows(length), BLOCK), F32)],
        cost=cost,
    )(doc_row, doc_col, projected, projected, projected)


def attn_bwd_kernel(head_dim, row_ref, col_ref, q_ref, k_ref, v_ref, do_ref, lse_ref, g_ref, gt_ref, bias_ref, dk_sum, dv_sum):
    length = q_ref.shape[0]
    pair = q_ref.shape[1]
    scale = head_dim**-0.5

    @pl.when(pl.program_id(0) == 0)
    def _():
        fill_bias(bias_ref, row_ref[...], col_ref[...], length)

    key_t = (k_ref[...] * BF(scale)).T
    dk_sum[...] = jnp.zeros_like(dk_sum)
    dv_sum[...] = jnp.zeros_like(dv_sum)
    at = 0
    for q_first, k_first in spans(length):
        keys = q_first + BLOCK - k_first
        q_at = slice(q_first, q_first + BLOCK)
        k_at = slice(k_first, k_first + keys)
        query = q_ref[q_at, :] * BF(scale)
        grad = do_ref[q_at, :]
        bias = bias_ref[at : at + keys, :]
        dq_parts = []
        dk_part = None
        dv_part = None
        for head in range(pair // head_dim):
            query_one = head_lanes(query, head, head_dim)
            grad_one = head_lanes(grad, head, head_dim)
            scores = mm_nt(k_ref[k_at, :], query_one) + bias
            prob = jnp.exp(scores - lse_ref[0, head : head + 1, q_at])
            prob_grad = mm_nt(v_ref[k_at, :], grad_one)
            inner = jnp.sum(prob * prob_grad, axis=0, keepdims=True)
            score_grad = (prob * (prob_grad - inner)).astype(BF)
            dv_one = mm(prob.astype(BF), grad_one)
            dk_one = mm(score_grad, query_one)
            dv_part = dv_one if dv_part is None else dv_part + dv_one
            dk_part = dk_one if dk_part is None else dk_part + dk_one
            dq_parts.append(mm(key_t[head * head_dim : (head + 1) * head_dim, k_at], score_grad))
        dk_sum[k_at, :] += dk_part
        dv_sum[k_at, :] += dv_part
        dq_t = jnp.concatenate(dq_parts, axis=0)
        gt_ref[0, :, q_at] = dq_t.astype(BF)
        g_ref[0, q_at, :] = dq_t.T.astype(BF)
        at += keys
    for i, ref in ((1, dk_sum), (2, dv_sum)):
        low = ref[...].astype(BF)
        g_ref[i] = low
        gt_ref[i] = low.T


def attn_bwd(projected, grad_heads, log_total, doc_row, doc_col, head_dim, part, parts, held=(), after=(), cost=0):
    length = projected.shape[0]
    width = projected.shape[1] // 3
    pair = 128
    pairs = width // pair
    steps = pairs // parts
    first = part * steps
    per = pair // head_dim
    specs = [
        pl.BlockSpec((length, pair), functools.partial(lambda s, j: (0, s * pairs + first + j), s)) for s in range(3)
    ]
    held = list(held)
    count = len(held)
    kernel = functools.partial(attn_bwd_kernel, head_dim)
    return call(
        lambda *refs: kernel(*refs[:7], *refs[7 + count :]),
        (steps,),
        [whole(doc_row.shape), whole(doc_col.shape)]
        + specs
        + [
            pl.BlockSpec((length, pair), lambda j: (0, first + j)),
            pl.BlockSpec((1, per, length), lambda j: (first + j, 0, 0)),
        ]
        + [pl.BlockSpec(memory_space=pl.ANY)] * count,
        [
            pl.BlockSpec((3, length, pair), lambda j: (0, 0, first + j)),
            pl.BlockSpec((3, pair, length), lambda j: (0, first + j, 0)),
        ],
        [jax.ShapeDtypeStruct((3, length, width), BF), jax.ShapeDtypeStruct((3, width, length), BF)],
        scratch=[
            pltpu.VMEM((bias_rows(length), BLOCK), F32),
            pltpu.VMEM((length, pair), F32),
            pltpu.VMEM((length, pair), F32),
        ],
        aliases={7 + i: i for i in range(count)},
        after=after,
        cost=cost,
    )(doc_row, doc_col, projected, projected, projected, grad_heads, log_total, *held)


def middle_kernel(x_ref, h_ref, w_ref, g_ref, b_ref, *refs):
    m_ref, s_ref = refs[-2:]
    middle = x_ref[...].astype(F32) + mm(h_ref[...], w_ref[...])
    m_ref[...] = middle
    unit, _inverse = normalize(middle)
    s_ref[...] = (unit * g_ref[1:2, :] + b_ref[1:2, :]).astype(BF)


def make_middle(tokens, mixed_heads, w_attn_out, gains, biases, part, parts, held=(), after=(), cost=0):
    rows, dim = tokens.shape
    tile = 256
    steps = rows // tile // parts
    block = pl.BlockSpec((tile, dim), lambda i: (part * steps + i, 0))
    held = list(held)
    return call(
        middle_kernel,
        (steps,),
        [block, block, whole(w_attn_out.shape), whole(gains.shape), whole(biases.shape)]
        + [pl.BlockSpec(memory_space=pl.ANY)] * len(held),
        [block, pl.BlockSpec((tile, dim), lambda i: (i, 0))],
        [jax.ShapeDtypeStruct((rows, dim), F32), jax.ShapeDtypeStruct((rows // parts, dim), BF)],
        aliases={5: 0} if held else None,
        after=after,
        cost=cost,
    )(tokens, mixed_heads, w_attn_out, gains, biases, *held)


def dispatch_kernel(parts, slots, *refs):
    places = refs[:2]
    rows = [refs[2 : 2 + parts], refs[2 + parts : 2 + 2 * parts]]
    o_refs = refs[2 + 2 * parts :]
    count = slots * (o_refs[0].shape[0] // (2 * slots)) * len(o_refs)
    for side in range(2):
        total = None
        at = 0
        for ref in rows[side]:
            slot = lax.broadcasted_iota(jnp.int32, (count, ref.shape[0]), 0)
            pick = jnp.where(slot == places[side][:, at : at + ref.shape[0]], 1.0, 0.0).astype(BF)
            part = mm(pick, ref[...])
            total = part if total is None else total + part
            at += ref.shape[0]
        low = total.astype(BF)
        if len(o_refs) == 1:
            o_refs[0][side * count : (side + 1) * count, :] = low
        else:
            for i, ref in enumerate(o_refs):
                ref[side * slots : (side + 1) * slots, :] = low[i * slots : (i + 1) * slots]


def dispatch_rows(places, rows, positions, slots, after=(), cost=0):
    dim = rows[0][0].shape[1]
    parts = len(rows[0])
    apart = slots % 16 == 0
    count = positions if apart else 1
    shape = (2 * slots * (positions // count), dim)
    out = call(
        functools.partial(dispatch_kernel, parts, slots),
        (1,),
        [whole(p.shape) for p in places] + [whole(r.shape) for side in rows for r in side],
        [whole(shape)] * count,
        [jax.ShapeDtypeStruct(shape, BF)] * count,
        after=after,
        cost=cost,
    )(*places, *rows[0], *rows[1])
    if apart:
        return out
    sides = out[0].reshape(2, positions, slots, dim)
    return [sides[:, p].reshape(2 * slots, dim) for p in range(positions)]


def fill(joined_ref, block_refs):
    at = 0
    for ref in block_refs:
        joined_ref[at : at + ref.shape[0], :] = ref[...]
        at += ref.shape[0]


def pick_rows(place, back):
    slot = lax.broadcasted_iota(jnp.int32, (place.shape[0], back.shape[0]), 1)
    return mm(jnp.where(slot == place, 1.0, 0.0).astype(BF), back)


def mixed_kernel(count, place_ref, m_ref, *refs):
    o_ref, joined_ref = refs[count:]

    @pl.when(pl.program_id(0) == 0)
    def _():
        fill(joined_ref, refs[:count])

    o_ref[...] = (m_ref[...] + pick_rows(place_ref[...], joined_ref[...])).astype(BF)


def make_mixed(place_col, middle, back, after=(), cost=0):
    rows, dim = middle.shape
    tile = 256
    total = sum(n for _, n in back)
    block = pl.BlockSpec((tile, dim), lambda i: (i, 0))
    return call(
        functools.partial(mixed_kernel, len(back)),
        (rows // tile,),
        [pl.BlockSpec((tile, 1), lambda i: (i, 0)), block] + [whole((n, dim)) for _, n in back],
        block,
        jax.ShapeDtypeStruct((rows, dim), BF),
        scratch=[pltpu.VMEM((total, dim), BF)],
        after=after,
        cost=cost,
    )(place_col, middle, *[b for b, _ in back])


def second_back_kernel(count, place_ref, m_ref, c_ref, w_ref, g_ref, *refs):
    gm_ref, gat_ref, gh_ref, sums_ref, joined_ref = refs[count:]

    @pl.when(pl.program_id(0) == 0)
    def _():
        fill(joined_ref, refs[:count])

    grad_sent = pick_rows(place_ref[...], joined_ref[...])
    unit, inverse = normalize(m_ref[...])
    grad_middle = c_ref[...].astype(F32) + norm_back(unit, inverse, g_ref[1:2, :], grad_sent)
    gm_ref[...] = grad_middle
    grad_attn = grad_middle.astype(BF)
    gat_ref[...] = grad_attn.T
    gh_ref[...] = mm_nt(grad_attn, w_ref[...]).astype(BF)
    sums = jnp.concatenate(
        [jnp.sum(grad_sent * unit, axis=0, keepdims=True), jnp.sum(grad_sent, axis=0, keepdims=True)], axis=0
    )

    @pl.when(pl.program_id(0) == 0)
    def _():
        sums_ref[...] = sums

    @pl.when(pl.program_id(0) > 0)
    def _():
        sums_ref[...] += sums


def second_back(place_col, middle, cotangent, back, w_attn_out, gains, after=(), cost=0):
    rows, dim = middle.shape
    tile = 256
    total = sum(n for _, n in back)
    block = pl.BlockSpec((tile, dim), lambda i: (i, 0))
    return call(
        functools.partial(second_back_kernel, len(back)),
        (rows // tile,),
        [pl.BlockSpec((tile, 1), lambda i: (i, 0)), block, block, whole(w_attn_out.shape), whole(gains.shape)]
        + [whole((n, dim)) for _, n in back],
        [block, pl.BlockSpec((dim, tile), lambda i: (0, i)), block, whole((2, dim))],
        [
            jax.ShapeDtypeStruct((rows, dim), F32),
            jax.ShapeDtypeStruct((dim, rows), BF),
            jax.ShapeDtypeStruct((rows, dim), BF),
            jax.ShapeDtypeStruct((2, dim), F32),
        ],
        scratch=[pltpu.VMEM((total, dim), BF)],
        after=after,
        cost=cost,
    )(place_col, middle, cotangent, w_attn_out, gains, *[b for b, _ in back])


def first_back_kernel(x_ref, gm_ref, d_ref, w_ref, g_ref, dx_ref, sums_ref):
    dim = x_ref.shape[1]
    grad_normed = mm_nt(d_ref[0], w_ref[:, :dim])
    grad_normed += mm_nt(d_ref[1], w_ref[:, dim : 2 * dim])
    grad_normed += mm_nt(d_ref[2], w_ref[:, 2 * dim :])
    unit, inverse = normalize(x_ref[...].astype(F32))
    dx_ref[...] = gm_ref[...] + norm_back(unit, inverse, g_ref[0:1, :], grad_normed)
    sums = jnp.concatenate(
        [jnp.sum(grad_normed * unit, axis=0, keepdims=True), jnp.sum(grad_normed, axis=0, keepdims=True)], axis=0
    )

    @pl.when(pl.program_id(0) == 0)
    def _():
        sums_ref[...] = sums

    @pl.when(pl.program_id(0) > 0)
    def _():
        sums_ref[...] += sums


def first_back(tokens, grad_middle, grads, w_qkv, gains, after=(), cost=0):
    rows, dim = tokens.shape
    tile = 256
    block = pl.BlockSpec((tile, dim), lambda i: (i, 0))
    return call(
        first_back_kernel,
        (rows // tile,),
        [
            block,
            block,
            pl.BlockSpec((3, tile, dim), lambda i: (0, i, 0)),
            whole(w_qkv.shape),
            whole(gains.shape),
        ],
        [block, whole((2, dim))],
        [jax.ShapeDtypeStruct((rows, dim), F32), jax.ShapeDtypeStruct((2, dim), F32)],
        after=after,
        cost=cost,
    )(tokens, grad_middle, grads, w_qkv, gains)


def grad_hidden_kernel(count, wo_ref, *refs):
    gh_ref, turned_ref, joined_ref = refs[count:]

    @pl.when(pl.program_id(0) == 0)
    def _():
        fill(joined_ref, refs[:count])
        turned_ref[...] = joined_ref[...].T

    gh_ref[...] = mm_nt(joined_ref[...], wo_ref[...]).astype(BF)


def grad_hidden(grads, w_out, after=(), cost=0):
    total = sum(g.shape[0] for g in grads)
    units, dim = w_out.shape
    tile = 512
    return call(
        functools.partial(grad_hidden_kernel, len(grads)),
        (units // tile,),
        [pl.BlockSpec((tile, dim), lambda j: (j, 0))] + [whole(g.shape) for g in grads],
        [pl.BlockSpec((total, tile), lambda j: (0, j)), whole((dim, total))],
        [jax.ShapeDtypeStruct((total, units), BF), jax.ShapeDtypeStruct((dim, total), BF)],
        scratch=[pltpu.VMEM((total, dim), BF)],
        after=after,
        cost=cost,
    )(w_out, *grads)


def expert_kernel(count, aliased, wi_ref, gh_ref, *refs):
    blocks = refs[:count]
    outs = refs[count + aliased :]
    h_ref, gp_ref = outs[:2]
    gr_refs = outs[2:-2]
    joined_ref, gr_sum = outs[-2:]
    step = pl.program_id(0)

    @pl.when(step == 0)
    def _():
        fill(joined_ref, blocks)
        gr_sum[...] = jnp.zeros_like(gr_sum)

    slope = 0.7978845608028654
    for first in range(0, wi_ref.shape[1], SUB):
        cols = slice(first, first + SUB)
        preact = mm(joined_ref[...], wi_ref[:, cols])
        square = preact * preact
        tanh = jnp.tanh(preact * (slope + (slope * 0.044715) * square))
        half = 0.5 + 0.5 * tanh
        hidden = preact * half
        gate = half + hidden * (1.0 - tanh) * (slope + (3.0 * slope * 0.044715) * square)
        h_ref[:, cols] = hidden.astype(BF)
        grad_low = (gate * gh_ref[:, cols].astype(F32)).astype(BF)
        gp_ref[:, cols] = grad_low
        gr_sum[...] += mm_nt(grad_low, wi_ref[:, cols])

    @pl.when(step == pl.num_programs(0) - 1)
    def _():
        at = 0
        for ref in gr_refs:
            ref[...] = gr_sum[at : at + ref.shape[0], :].astype(BF)
            at += ref.shape[0]


def expert(blocks, gh, w_in, first, held=(), out_rows=None, after=(), cost=0):
    count = sum(b.shape[0] for b in blocks)
    dim, units = w_in.shape
    tile = 1024
    at = first // count
    act = pl.BlockSpec((count, tile), lambda j: (at, j))
    shape = jax.ShapeDtypeStruct(gh.shape, BF)
    held = list(held)
    pieces = out_rows or [b.shape[0] for b in blocks]
    return call(
        functools.partial(expert_kernel, len(blocks), len(held)),
        (units // tile,),
        [pl.BlockSpec((dim, tile), lambda j: (0, j)), act]
        + [whole(b.shape) for b in blocks]
        + [pl.BlockSpec(memory_space=pl.ANY)] * len(held),
        [act, act] + [whole((n, dim)) for n in pieces],
        [shape, shape] + [jax.ShapeDtypeStruct((n, dim), BF) for n in pieces],
        scratch=[pltpu.VMEM((count, dim), BF), pltpu.VMEM((count, dim), F32)],
        aliases={2 + len(blocks) + i: i for i in range(len(held))},
        after=after,
        cost=cost,
    )(w_in, gh, *blocks, *held)


def turn_kernel(count, *refs):
    o_ref, joined_ref = refs[count:]
    fill(joined_ref, refs[:count])
    o_ref[...] = joined_ref[...].T


def turned(blocks, after=(), cost=0):
    total = sum(b.shape[0] for b in blocks)
    dim = blocks[0].shape[1]
    return call(
        functools.partial(turn_kernel, len(blocks)),
        (1,),
        [whole(b.shape) for b in blocks],
        whole((dim, total)),
        jax.ShapeDtypeStruct((dim, total), BF),
        scratch=[pltpu.VMEM((total, dim), BF)],
        after=after,
        cost=cost,
    )(*blocks)


def produced_kernel(h_ref, wo_ref, *refs):
    o_refs, total_ref = refs[:-1], refs[-1]
    step = pl.program_id(0)
    part = mm(h_ref[...], wo_ref[...])

    @pl.when(step == 0)
    def _():
        total_ref[...] = part

    @pl.when(step > 0)
    def _():
        total_ref[...] += part

    @pl.when(step == pl.num_programs(0) - 1)
    def _():
        at = 0
        for ref in o_refs:
            ref[...] = total_ref[at : at + ref.shape[0], :].astype(BF)
            at += ref.shape[0]


def make_produced(hidden, w_out, pieces, after=(), cost=0):
    rows, units = hidden.shape
    dim = w_out.shape[1]
    tile = 512
    return call(
        produced_kernel,
        (units // tile,),
        [pl.BlockSpec((rows, tile), lambda j: (0, j)), pl.BlockSpec((tile, dim), lambda j: (j, 0))],
        [whole((n, dim)) for n in pieces],
        [jax.ShapeDtypeStruct((n, dim), BF) for n in pieces],
        scratch=[pltpu.VMEM((rows, dim), F32)],
        after=after,
        cost=cost,
    )(hidden, w_out)


def halves_kernel(count, slots, *refs):
    o_ref = refs[-1]
    for i in range(count):
        o_ref[i * slots : (i + 1) * slots, :] = refs[i][...]


def second_halves(blocks, slots, after=(), cost=0):
    dim = blocks[0].shape[1]
    count = len(blocks)
    return call(
        functools.partial(halves_kernel, count, slots),
        (1,),
        [pl.BlockSpec((slots, dim), lambda i: (1, 0))] * count,
        whole((count * slots, dim)),
        jax.ShapeDtypeStruct((count * slots, dim), BF),
        after=after,
        cost=cost,
    )(*blocks)


def add_kernel(k_ref, g_ref, o_ref):
    o_ref[...] = (k_ref[...].astype(F32) + g_ref[...].astype(F32)).astype(BF)


def add_second(keep, got, after=(), cost=0):
    _, rows, cols = keep.shape
    tile = 256
    block = pl.BlockSpec((1, tile, cols), lambda i: (1, i, 0))
    return call(
        add_kernel,
        (rows // tile,),
        [block, block],
        pl.BlockSpec((1, tile, cols), lambda i: (0, i, 0)),
        jax.ShapeDtypeStruct((1, rows, cols), BF),
        after=after,
        cost=cost,
    )(keep, got)


def stack_kernel(a_ref, b_ref, o_ref):
    o_ref[0:1, :] = a_ref[0:1, :]
    o_ref[1:2, :] = b_ref[0:1, :]
    o_ref[2:3, :] = a_ref[1:2, :]
    o_ref[3:4, :] = b_ref[1:2, :]


def stack_sums(first, second, after=(), cost=0):
    _, dim = first.shape
    return call(
        stack_kernel,
        (1,),
        [whole(first.shape), whole(second.shape)],
        whole((4, dim)),
        jax.ShapeDtypeStruct((4, dim), F32),
        after=after,
        cost=cost,
    )(first, second)


def tiles_kernel(_, a_ref, b_ref, o_ref):
    o_ref[0] = mm(a_ref[...], b_ref[...]).astype(BF)


def weight_tiles(first, second, table, first_tile, second_tile, after=(), cost=0):
    steps = table.shape[1]
    depth = first.shape[1]
    return call(
        tiles_kernel,
        (steps,),
        [
            pl.BlockSpec((first_tile, depth), lambda i, t: (t[0, i], 0)),
            pl.BlockSpec((depth, second_tile), lambda i, t: (0, t[1, i])),
        ],
        pl.BlockSpec((1, first_tile, second_tile), lambda i, t: (i, 0, 0)),
        jax.ShapeDtypeStruct((steps, first_tile, second_tile), BF),
        prefetch=1,
        after=after,
        cost=cost,
    )(table, first, second)


def joint_kernel(g_ref, ga_ref, n_ref, h_ref, o_ref):
    own = o_ref.shape[0]
    dim = o_ref.shape[2]
    qkv_part = mm(g_ref[...], n_ref[...]).reshape(own, g_ref.shape[0] // own, dim)
    out_part = mm(ga_ref[...], h_ref[...]).reshape(own, ga_ref.shape[0] // own, dim)
    o_ref[...] = jnp.concatenate([qkv_part, out_part], axis=1).astype(BF)


def joint(grads_t, grad_attn_t, normed, mixed_heads, owners, part, parts, after=(), cost=0):
    rows, dim = normed.shape
    steps = 8
    cols = dim // parts
    own = owners // steps
    qkv_rows = grads_t.shape[0] // steps
    out_rows = grad_attn_t.shape[0] // steps
    right = pl.BlockSpec((rows, cols), lambda i: (0, part))
    each = (qkv_rows + out_rows) // own
    return call(
        joint_kernel,
        (steps,),
        [
            pl.BlockSpec((qkv_rows, rows), lambda i: (i, 0)),
            pl.BlockSpec((out_rows, rows), lambda i: (i, 0)),
            right,
            right,
        ],
        pl.BlockSpec((own, each, cols), lambda i: (i, 0, 0)),
        jax.ShapeDtypeStruct((owners, each, cols), BF),
        after=after,
        cost=cost,
    )(grads_t, grad_attn_t, normed, mixed_heads)


def finish_kernel(turn, *refs):
    o_ref = refs[-1]
    total = refs[0][0].astype(F32) + refs[1][0].astype(F32) + refs[2][0].astype(F32)
    o_ref[...] = total.T if turn else total


def finish(keep, got, last, turn, side, held=None, after=(), cost=0):
    _, rows, cols = keep.shape
    tile = 256
    block = pl.BlockSpec((1, tile, cols), lambda i: (0, i, 0))
    steps = rows // tile
    shape = (cols, 2 * rows) if turn else (2 * rows, cols)
    out = (
        pl.BlockSpec((cols, tile), lambda i: (0, side * steps + i))
        if turn
        else pl.BlockSpec((tile, cols), lambda i: (side * steps + i, 0))
    )
    more = [] if held is None else [held]
    count = len(more)

    def body(*refs):
        finish_kernel(turn, *refs[:3], refs[3 + count])

    return call(
        body,
        (steps,),
        [block] * 3 + [pl.BlockSpec(memory_space=pl.ANY)] * count,
        out,
        jax.ShapeDtypeStruct(shape, F32),
        aliases={3: 0} if more else None,
        after=after,
        cost=cost,
    )(keep, got, last, *more)


def swap(value, axis, mask):
    size = lax.axis_size(axis)
    return lax.ppermute(value, axis, [(i, i ^ mask) for i in range(size)])


def split_sum(value, dim, axis, mask):
    bit = jnp.where((lax.axis_index(axis) & mask) > 0, 1, 0)
    mine = lax.dynamic_index_in_dim(value, bit, dim, keepdims=False)
    other = lax.dynamic_index_in_dim(value, 1 - bit, dim, keepdims=False)
    return (mine.astype(F32) + swap(other, axis, mask).astype(F32)).astype(value.dtype)


def bits_of(size):
    return [1 << i for i in range(size.bit_length() - 1)]


def on_device(
    tokens,
    norm_gains,
    norm_biases,
    w_qkv,
    w_attn_out,
    w_in,
    w_out,
    segment_ids,
    expert_ids,
    slots,
    cotangent,
):
    tok, dim = tokens.shape
    head_dim = dim // HEADS
    wide = lax.axis_size("wide")
    narrow = lax.axis_size("narrow")
    units = w_in.shape[2]
    me_wide = lax.axis_index("wide")
    me_narrow = lax.axis_index("narrow")
    capacity = tok * 9 // (8 * wide)
    w_in = w_in[0]
    w_out = w_out[0]
    zs = wide // 2
    slots_all = zs * capacity
    groups = [list(range(zs // 2)), list(range(zs // 2, 3 * zs // 4)), list(range(3 * zs // 4, zs))]
    apart = capacity % 16 == 0

    def joinable(blocks):
        return blocks if apart else [jnp.concatenate(blocks, axis=0)]

    def by_position(pieces):
        return list(pieces) if apart else [q for p in pieces for q in jnp.split(p, p.shape[0] // (2 * capacity))]

    def piece_rows(group):
        return [2 * capacity] * len(group) if apart else [2 * capacity * len(group)]

    away = expert_ids ^ me_wide
    kept = slots < capacity
    base = (away >> 1) * capacity + slots
    core = away & 1
    nowhere = 2 * slots_all
    place_own = jnp.where(kept & (core == 0), base, nowhere).astype(jnp.int32)[None, :]
    place_sent = jnp.where(kept & (core == 1), base, nowhere).astype(jnp.int32)[None, :]
    places = [place_own, swap(place_sent, "wide", 1)]
    place_col = jnp.where(kept, core * slots_all + base, nowhere).astype(jnp.int32)[:, None]
    doc_row = segment_ids
    doc_col = segment_ids.reshape(tok, 1)

    def exchange(blocks, positions):
        return [swap(blocks[z], "wide", 2 * z) if z else blocks[z] for z in positions]

    def bring_back(blocks, after):
        if not apart:
            theirs = jnp.concatenate([b[capacity:] for b in blocks], axis=0)
            ours = swap(theirs, "wide", 1)
            return [(jnp.concatenate([b[:capacity] for b in blocks], axis=0), slots_all), (ours, slots_all)]
        ours = swap(second_halves(blocks, capacity, after), "wide", 1)
        return [(b, capacity) for b in blocks] + [(ours, slots_all)]

    cotangent_other = swap(cotangent, "wide", 1)
    normed = first_norm(tokens, norm_gains, norm_biases)
    sent_grads = dispatch_rows(places, [[cotangent], [cotangent_other]], zs, capacity, after=[normed])
    expert_grads = exchange(sent_grads, range(zs))

    projected = project(normed, w_qkv, after=[sent_grads[0]])
    mixed_heads, log_total = attn_fwd(projected, doc_row, doc_col, head_dim)
    middle, sent_first = make_middle(tokens, mixed_heads, w_attn_out, norm_gains, norm_biases, 0, 2)
    other_first = swap(sent_first, "wide", 1)
    middle, sent_last = make_middle(
        tokens, mixed_heads, w_attn_out, norm_gains, norm_biases, 1, 2, [middle], after=expert_grads
    )
    other_last = swap(sent_last, "wide", 1)
    sent_rows = dispatch_rows(places, [[sent_first, sent_last], [other_first, other_last]], zs, capacity)
    expert_rows = exchange(sent_rows, range(zs))

    gh, grads_t = grad_hidden(joinable(expert_grads), w_out, after=[sent_rows[0]])
    held = ()
    back_grads = []
    before = [gh]
    for group in groups:
        blocks = joinable([expert_rows[z] for z in group])
        outs = expert(blocks, gh, w_in, 2 * group[0] * capacity, held, piece_rows(group), after=before)
        held = outs[:2]
        before = [outs[2]]
        pieces = by_position(outs[2:])
        back_grads += exchange({z: pieces[i] for i, z in enumerate(group)}, group)
    hidden, grad_preact = held

    quarter = units // narrow
    half_dim = dim // 2

    def tiles(turned_rows, right, side, positions, after):
        table = jnp.stack(
            [jnp.full((len(positions),), side, jnp.int32), jnp.stack([me_narrow ^ p for p in positions]).astype(jnp.int32)]
        )
        return weight_tiles(turned_rows, right, table, half_dim, quarter, after=after)

    masks = [(1, 2), (2, 1)]
    sides = range(2)

    def send(turned_rows, right, after):
        out = [tiles(turned_rows, right, side, [masks[side][0], 3], after) for side in sides]
        return out, [swap(out[side], "narrow", masks[side][0]) for side in sides]

    def keep(turned_rows, right, after):
        return [tiles(turned_rows, right, side, [0, masks[side][1]], after) for side in sides]

    def second_step(kept, got, after):
        again = [add_second(kept[side], got[side], after) for side in sides]
        return again, [swap(again[side], "narrow", masks[side][1]) for side in sides]

    send_out, got_out = send(grads_t, hidden, before)
    rows_t = turned(joinable(expert_rows), after=send_out)
    keep_out = keep(grads_t, hidden, [rows_t])
    produced = make_produced(hidden, w_out, piece_rows(range(zs)), after=keep_out)
    back_rows = exchange(by_position(produced), range(zs))
    back_grads = bring_back(back_grads, [produced[0]])
    send_in, got_in = send(rows_t, grad_preact, [back_grads[0][0], produced[0]])
    grad_middle, grad_attn_t, grad_heads, sums_two = second_back(
        place_col, middle, cotangent, back_grads, w_attn_out, norm_gains, after=send_in + got_out
    )
    attn = functools.partial(attn_bwd, projected, grad_heads, log_total, doc_row, doc_col, head_dim)
    held = attn(0, 2)
    back_rows = bring_back(back_rows, [held[0]])
    again_out, last_out = second_step(keep_out, got_out, [held[0]])
    grads, grads_all_t = attn(1, 2, held, after=again_out)
    grads_all_t = grads_all_t.reshape(3 * dim, tok)

    owners = narrow * wide
    own_qkv = 3 * dim // owners
    n_bits = bits_of(narrow)
    w_bits = bits_of(wide)
    joints = []
    for side in sides:
        joints.append(joint(grads_all_t, grad_attn_t, normed, mixed_heads, owners, side, 2, after=joints))
    keep_in = keep(rows_t, grad_preact, joints)
    again_in, last_in = second_step(keep_in, got_in, keep_in)
    values = []
    for side in sides:
        value = joints[side].reshape((2,) * (len(n_bits) + len(w_bits)) + joints[side].shape[1:])
        names = [("narrow", b) for b in reversed(n_bits)] + [("wide", b) for b in reversed(w_bits)]
        steps = [("wide", 1)] + [("narrow", b) for b in masks[side]] + [("wide", b) for b in w_bits[1:]]
        for step in steps:
            at = names.index(step)
            value = split_sum(value, at, *step)
            names.pop(at)
        values.append(value)
    d_tokens, sums_one = first_back(tokens, grad_middle, grads, w_qkv, norm_gains, after=again_in)
    mixed = make_mixed(place_col, middle, back_rows, after=[sums_one])
    value = jnp.concatenate(values, axis=1)
    d_w_qkv = value[:own_qkv].T.astype(F32)
    d_w_attn_out = value[own_qkv:].T.astype(F32)

    d_w_out = finish(keep_out[0], got_out[0], last_out[0], True, 0, after=[mixed])
    d_w_out = finish(keep_out[1], got_out[1], last_out[1], True, 1, d_w_out)
    d_w_in = finish(keep_in[0], got_in[0], last_in[0], False, 0, after=[d_w_out])
    d_w_in = finish(keep_in[1], got_in[1], last_in[1], False, 1, d_w_in)

    sums = stack_sums(sums_one, sums_two, after=[d_w_in])
    for axis, bits in (("narrow", n_bits), ("wide", w_bits)):
        for bit in bits:
            sums = sums + swap(sums, axis, bit)
    own = dim // owners
    sums = lax.dynamic_slice_in_dim(sums, (me_narrow * wide + me_wide) * own, own, 1)
    return (mixed, d_tokens, sums[:2], sums[2:], d_w_qkv, d_w_attn_out, d_w_in[None], d_w_out[None])


def solution(mesh):
    placed = (
        P(("narrow", "wide"), None),
        P(),
        P(),
        P(),
        P(),
        P("wide", None, None),
        P("wide", None, None),
        P(("narrow", "wide"), None),
        P(("narrow", "wide")),
        P(("narrow", "wide")),
        P(("narrow", "wide"), None),
    )
    return jax.shard_map(
        on_device,
        mesh=mesh,
        in_specs=placed,
        out_specs=(
            P(("narrow", "wide"), None),
            P(("narrow", "wide"), None),
            P(None, ("narrow", "wide")),
            P(None, ("narrow", "wide")),
            P(None, ("narrow", "wide")),
            P(None, ("narrow", "wide")),
            P("wide", None, "narrow"),
            P("wide", "narrow", None),
        ),
        check_vma=False,
    )
```

```python
import functools
import itertools

import jax
import jax.numpy as jnp
from jax import lax
from jax.experimental import pallas as pl
from jax.experimental.pallas import tpu as pltpu
from jax.sharding import PartitionSpec as P

HEADS = 16
EPSILON = 1e-05
NEGATIVE = -1e30
BAND = 512
BLOCK = 256
SUB = 256
F32 = jnp.float32
BF = jnp.bfloat16
COST_GATE = 6
VMEM_BYTES = 48 * 1024 * 1024


def mm(a, b):
    return lax.dot_general(a, b, (((1,), (0,)), ((), ())), preferred_element_type=F32)


def mm_nt(a, b):
    return lax.dot_general(a, b, (((1,), (1,)), ((), ())), preferred_element_type=F32)


def mm_tn(a, b):
    return lax.dot_general(a, b, (((0,), (0,)), ((), ())), preferred_element_type=F32)


def call(kernel, grid, in_specs, out_specs, out_shape, scratch=(), prefetch=0, aliases=None, after=(), cost=0):
    count = prefetch + len(in_specs)
    extra = len(after)

    def body(*refs):
        kernel(*refs[:count], *refs[count + extra :])

    run = pl.pallas_call(
        body,
        grid_spec=pltpu.PrefetchScalarGridSpec(
            num_scalar_prefetch=prefetch,
            grid=grid,
            in_specs=list(in_specs) + [pl.BlockSpec(memory_space=pl.ANY)] * extra,
            out_specs=out_specs,
            scratch_shapes=list(scratch),
        ),
        out_shape=out_shape,
        input_output_aliases=aliases or {},
        compiler_params=pltpu.CompilerParams(vmem_limit_bytes=VMEM_BYTES),
        cost_estimate=pl.CostEstimate(flops=1 + int(cost * 1.15e9), bytes_accessed=0, transcendentals=0),
    )
    return lambda *args: run(*args, *after)


def whole(shape):
    return pl.BlockSpec(shape, lambda *_: (0,) * len(shape))


def normalize(stream):
    average = jnp.mean(stream, axis=-1, keepdims=True)
    centered = stream - average
    inverse = lax.rsqrt(jnp.mean(centered * centered, axis=-1, keepdims=True) + EPSILON)
    return centered * inverse, inverse


def norm_back(unit, inverse, gain, grad):
    scaled = grad * gain
    first = jnp.mean(scaled, axis=-1, keepdims=True)
    second = jnp.mean(scaled * unit, axis=-1, keepdims=True)
    return inverse * (scaled - first - unit * second)


def first_norm_kernel(x_ref, g_ref, b_ref, n_ref):
    unit, _inverse = normalize(x_ref[...].astype(F32))
    n_ref[...] = (unit * g_ref[0:1, :] + b_ref[0:1, :]).astype(BF)


def first_norm(tokens, gains, biases, after=(), cost=0):
    rows, dim = tokens.shape
    block = pl.BlockSpec((256, dim), lambda i: (i, 0))
    return call(
        first_norm_kernel,
        (rows // 256,),
        [block, whole(gains.shape), whole(biases.shape)],
        block,
        jax.ShapeDtypeStruct((rows, dim), BF),
        after=after,
        cost=cost,
    )(tokens, gains, biases)


def project_kernel(n_ref, w_ref, p_ref):
    p_ref[...] = mm(n_ref[...], w_ref[...]).astype(BF)


def project(normed, w_qkv, after=(), cost=0):
    rows, dim = normed.shape
    cols = w_qkv.shape[1]
    tile = 768
    return call(
        project_kernel,
        (cols // tile,),
        [whole((rows, dim)), pl.BlockSpec((dim, tile), lambda j: (0, j))],
        pl.BlockSpec((rows, tile), lambda j: (0, j)),
        jax.ShapeDtypeStruct((rows, cols), BF),
        after=after,
        cost=cost,
    )(normed, w_qkv)


def fill_masks(col_ref, fq_ref, fk_ref, tri_ref, head_dim):
    length = col_ref.shape[0]
    doc = lax.broadcasted_iota(jnp.int32, fq_ref.shape, 1) % head_dim
    same = doc == col_ref[...]
    fq_ref[...] = jnp.where(same, 1.0, 0.0).astype(BF)
    fk_ref[...] = jnp.where(same, 0.0, NEGATIVE).astype(BF)
    key_pos = lax.broadcasted_iota(jnp.int32, tri_ref.shape, 0)
    query_pos = lax.broadcasted_iota(jnp.int32, tri_ref.shape, 1)
    tri_ref[...] = jnp.where(key_pos <= query_pos, 0.0, NEGATIVE).astype(F32)


def lanes_of(shape, head, head_dim):
    lane = lax.broadcasted_iota(jnp.int32, shape, 1)
    return (lane >= head * head_dim) & (lane < (head + 1) * head_dim)


def attn_fwd_kernel(head_dim, col_ref, q_ref, k_ref, v_ref, o_ref, lse_ref, fq_ref, fk_ref, tri_ref, vt_ref, qh_ref, kh_ref):
    length, pair = q_ref.shape
    scale = head_dim**-0.5
    per = pair // head_dim

    @pl.when(pl.program_id(0) == 0)
    def _():
        fill_masks(col_ref, fq_ref, fk_ref, tri_ref, head_dim)
        vt_ref[...] = jnp.ones_like(vt_ref)

    value_t = v_ref[...].T
    query = q_ref[...] * BF(scale)
    for head in range(per):
        inside = lanes_of(query.shape, head, head_dim)
        vt_ref[head, :head_dim, :] = value_t[head * head_dim : (head + 1) * head_dim, :]
        qh_ref[head] = jnp.where(inside, query, fq_ref[...])
        kh_ref[head] = jnp.where(inside, k_ref[...], fk_ref[...])
    def first_stage(q_first):
        k_first = max(0, q_first - BAND)
        allparts = [[] for _ in range(per)]
        for k_at in range(k_first, q_first + BLOCK, BLOCK):
            for head in range(per):
                scores = mm_nt(kh_ref[head, k_at : k_at + BLOCK, :], qh_ref[head, q_first : q_first + BLOCK, :])
                if k_at == q_first:
                    scores = scores + tri_ref[...]
                allparts[head].append(scores)
        tops = [functools.reduce(jnp.maximum, [jnp.max(p, axis=0, keepdims=True) for p in parts]) for parts in allparts]
        return allparts, tops

    def second_stage(q_first, allparts, tops):
        k_first = max(0, q_first - BAND)
        q_at = slice(q_first, q_first + BLOCK)
        totals = [None] * per
        for i in range(len(allparts[0])):
            k_at = k_first + i * BLOCK
            for head in range(per):
                prob = jnp.exp(allparts[head][i] - tops[head]).astype(BF)
                part = mm(vt_ref[head, :, k_at : k_at + BLOCK], prob)
                totals[head] = part if totals[head] is None else totals[head] + part
        outs = []
        for head in range(per):
            total = totals[head]
            sums = total[head_dim : head_dim + 1, :]
            outs.append(total[:head_dim, :] / sums)
            lse_ref[0, head : head + 1, q_at] = tops[head] + jnp.log(sums)
        o_ref[q_at, :] = jnp.concatenate(outs, axis=0).T.astype(BF)

    firsts = list(range(0, length, BLOCK))
    ahead = first_stage(firsts[0])
    for i, q_first in enumerate(firsts):
        now = ahead
        if i + 1 < len(firsts):
            ahead = first_stage(firsts[i + 1])
        second_stage(q_first, *now)


def attn_fwd(projected, doc_col, head_dim, cost=0):
    length = projected.shape[0]
    width = projected.shape[1] // 3
    pair = 128
    pairs = width // pair
    per = pair // head_dim
    specs = [pl.BlockSpec((length, pair), functools.partial(lambda s, j: (0, s * pairs + j), s)) for s in range(3)]
    return call(
        functools.partial(attn_fwd_kernel, head_dim),
        (pairs,),
        [whole(doc_col.shape)] + specs,
        [pl.BlockSpec((length, pair), lambda j: (0, j)), pl.BlockSpec((1, per, length), lambda j: (j, 0, 0))],
        [jax.ShapeDtypeStruct((length, width), BF), jax.ShapeDtypeStruct((pairs, per, length), F32)],
        scratch=[
            pltpu.VMEM((length, pair), BF),
            pltpu.VMEM((length, pair), BF),
            pltpu.VMEM((BLOCK, BLOCK), F32),
            pltpu.VMEM((per, head_dim + 16, length), BF),
            pltpu.VMEM((per, length, pair), BF),
            pltpu.VMEM((per, length, pair), BF),
        ],
        cost=cost,
    )(doc_col, projected, projected, projected)


def two_parts(x):
    hi = x.astype(BF)
    return hi, (x - hi.astype(F32)).astype(BF)


def attn_bwd_kernel(head_dim, col_ref, q_ref, k_ref, v_ref, o_ref, do_ref, lse_ref, g_ref, gt_ref,
                    fq_ref, fk_ref, tri_ref, qx, kx, vx, dox, qm, dom, dk_sum, dv_sum):
    length, pair = q_ref.shape
    scale = head_dim**-0.5
    per = pair // head_dim

    @pl.when(pl.program_id(0) == 0)
    def _():
        fill_masks(col_ref, fq_ref, fk_ref, tri_ref, head_dim)

    key_t = (k_ref[...] * BF(scale)).T
    query = q_ref[...] * BF(scale)
    grad = do_ref[...]
    lane = lax.broadcasted_iota(jnp.int32, (length, pair), 1)
    zero = jnp.zeros_like(query)
    one = jnp.ones_like(query)
    lse_rows = jnp.concatenate([lse_ref[0], jnp.zeros((8 - per, length), F32)], axis=0)
    lse_cols = lse_rows.T
    product = grad.astype(F32) * o_ref[...].astype(F32)
    for head in range(per):
        inside = lanes_of(query.shape, head, head_dim)
        slot = (1 - head) * head_dim + head_dim // 2
        first = lane == slot
        second = lane == slot + 1
        lse_hi, lse_lo = two_parts(-lse_cols[:, head : head + 1])
        delta = -jnp.sum(jnp.where(inside, product, 0.0), axis=1, keepdims=True)
        delta_hi, delta_lo = two_parts(delta)
        qm[head] = jnp.where(inside, query, zero)
        dom[head] = jnp.where(inside, grad, zero)
        qx[head] = jnp.where(inside, query, jnp.where(first, lse_hi, jnp.where(second, lse_lo, fq_ref[...])))
        kx[head] = jnp.where(inside, k_ref[...], jnp.where(first | second, one, fk_ref[...]))
        vx[head] = jnp.where(inside, v_ref[...], jnp.where(first | second, one, zero))
        dox[head] = jnp.where(inside, grad, jnp.where(first, delta_hi, jnp.where(second, delta_lo, zero)))
    dk_sum[...] = jnp.zeros_like(dk_sum)
    dv_sum[...] = jnp.zeros_like(dv_sum)
    for q_first in range(0, length, BLOCK):
        q_at = slice(q_first, q_first + BLOCK)
        dq_parts = [None] * per
        for k_first in range(max(0, q_first - BAND), q_first + BLOCK, BLOCK):
            k_at = slice(k_first, k_first + BLOCK)
            scores = [mm_nt(kx[h, k_at, :], qx[h, q_at, :]) for h in range(per)]
            prob_grads = [mm_nt(vx[h, k_at, :], dox[h, q_at, :]) for h in range(per)]
            if k_first == q_first:
                scores = [s + tri_ref[...] for s in scores]
            probs = [jnp.exp(s) for s in scores]
            score_grads = [(p * d).astype(BF) for p, d in zip(probs, prob_grads)]
            probs = [p.astype(BF) for p in probs]
            dv_sum[k_at, :] += mm(
                jnp.concatenate(probs, axis=1), jnp.concatenate([dom[h, q_at, :] for h in range(per)], axis=0)
            )
            dk_sum[k_at, :] += mm(
                jnp.concatenate(score_grads, axis=1), jnp.concatenate([qm[h, q_at, :] for h in range(per)], axis=0)
            )
            for h in range(per):
                one = mm(key_t[h * head_dim : (h + 1) * head_dim, k_at], score_grads[h])
                dq_parts[h] = one if dq_parts[h] is None else dq_parts[h] + one
        dq_t = jnp.concatenate(dq_parts, axis=0)
        gt_ref[0, :, q_at] = dq_t.astype(BF)
        g_ref[0, q_at, :] = dq_t.T.astype(BF)
    for i, ref in ((1, dk_sum), (2, dv_sum)):
        low = ref[...].astype(BF)
        g_ref[i] = low
        gt_ref[i] = low.T


def attn_bwd(projected, mixed_heads, grad_heads, log_total, doc_col, head_dim, part, parts, held=(), after=(), cost=0):
    length = projected.shape[0]
    width = projected.shape[1] // 3
    pair = 128
    pairs = width // pair
    steps = pairs // parts
    first = part * steps
    per = pair // head_dim
    specs = [
        pl.BlockSpec((length, pair), functools.partial(lambda s, j: (0, s * pairs + first + j), s)) for s in range(3)
    ]
    held = list(held)
    count = len(held)
    kernel = functools.partial(attn_bwd_kernel, head_dim)
    one = pl.BlockSpec((length, pair), lambda j: (0, first + j))
    return call(
        lambda *refs: kernel(*refs[:7], *refs[7 + count :]),
        (steps,),
        [whole(doc_col.shape)] + specs + [one, one, pl.BlockSpec((1, per, length), lambda j: (first + j, 0, 0))]
        + [pl.BlockSpec(memory_space=pl.ANY)] * count,
        [
            pl.BlockSpec((3, length, pair), lambda j: (0, 0, first + j)),
            pl.BlockSpec((3, pair, length), lambda j: (0, first + j, 0)),
        ],
        [jax.ShapeDtypeStruct((3, length, width), BF), jax.ShapeDtypeStruct((3, width, length), BF)],
        scratch=[
            pltpu.VMEM((length, pair), BF),
            pltpu.VMEM((length, pair), BF),
            pltpu.VMEM((BLOCK, BLOCK), F32),
        ]
        + [pltpu.VMEM((per, length, pair), BF)] * 6
        + [pltpu.VMEM((length, pair), F32)] * 2,
        aliases={7 + i: i for i in range(count)},
        after=after,
        cost=cost,
    )(doc_col, projected, projected, projected, mixed_heads, grad_heads, log_total, *held)


def middle_kernel(x_ref, h_ref, w_ref, g_ref, b_ref, *refs):
    m_ref, s_ref = refs[-2:]
    middle = x_ref[...].astype(F32) + mm(h_ref[...], w_ref[...])
    m_ref[...] = middle
    unit, _inverse = normalize(middle)
    s_ref[...] = (unit * g_ref[1:2, :] + b_ref[1:2, :]).astype(BF)


def make_middle(tokens, mixed_heads, w_attn_out, gains, biases, part, parts, held=(), after=(), cost=0):
    rows, dim = tokens.shape
    tile = 256
    steps = rows // tile // parts
    block = pl.BlockSpec((tile, dim), lambda i: (part * steps + i, 0))
    held = list(held)
    return call(
        middle_kernel,
        (steps,),
        [block, block, whole(w_attn_out.shape), whole(gains.shape), whole(biases.shape)]
        + [pl.BlockSpec(memory_space=pl.ANY)] * len(held),
        [block, pl.BlockSpec((tile, dim), lambda i: (i, 0))],
        [jax.ShapeDtypeStruct((rows, dim), F32), jax.ShapeDtypeStruct((rows // parts, dim), BF)],
        aliases={5: 0} if held else None,
        after=after,
        cost=cost,
    )(tokens, mixed_heads, w_attn_out, gains, biases, *held)


def dispatch_kernel(parts, slots, *refs):
    places = refs[:2]
    rows = [refs[2 : 2 + parts], refs[2 + parts : 2 + 2 * parts]]
    o_refs = refs[2 + 2 * parts :]
    count = slots * (o_refs[0].shape[0] // (2 * slots)) * len(o_refs)
    for side in range(2):
        total = None
        at = 0
        for ref in rows[side]:
            slot = lax.broadcasted_iota(jnp.int32, (count, ref.shape[0]), 0)
            pick = jnp.where(slot == places[side][:, at : at + ref.shape[0]], 1.0, 0.0).astype(BF)
            part = mm(pick, ref[...])
            total = part if total is None else total + part
            at += ref.shape[0]
        low = total.astype(BF)
        if len(o_refs) == 1:
            o_refs[0][side * count : (side + 1) * count, :] = low
        else:
            for i, ref in enumerate(o_refs):
                ref[side * slots : (side + 1) * slots, :] = low[i * slots : (i + 1) * slots]


def dispatch_rows(places, rows, positions, slots, after=(), cost=0):
    dim = rows[0][0].shape[1]
    parts = len(rows[0])
    apart = slots % 16 == 0
    count = positions if apart else 1
    shape = (2 * slots * (positions // count), dim)
    out = call(
        functools.partial(dispatch_kernel, parts, slots),
        (1,),
        [whole(p.shape) for p in places] + [whole(r.shape) for side in rows for r in side],
        [whole(shape)] * count,
        [jax.ShapeDtypeStruct(shape, BF)] * count,
        after=after,
        cost=cost,
    )(*places, *rows[0], *rows[1])
    if apart:
        return out
    sides = out[0].reshape(2, positions, slots, dim)
    return [sides[:, p].reshape(2 * slots, dim) for p in range(positions)]


def fill(joined_ref, block_refs):
    at = 0
    for ref in block_refs:
        joined_ref[at : at + ref.shape[0], :] = ref[...]
        at += ref.shape[0]


def pick_rows(place, back):
    slot = lax.broadcasted_iota(jnp.int32, (place.shape[0], back.shape[0]), 1)
    return mm(jnp.where(slot == place, 1.0, 0.0).astype(BF), back)


def mixed_kernel(count, place_ref, m_ref, *refs):
    o_ref, joined_ref = refs[count:]

    @pl.when(pl.program_id(0) == 0)
    def _():
        fill(joined_ref, refs[:count])

    o_ref[...] = (m_ref[...] + pick_rows(place_ref[...], joined_ref[...])).astype(BF)


def make_mixed(place_col, middle, back, after=(), cost=0):
    rows, dim = middle.shape
    tile = 256
    total = sum(n for _, n in back)
    block = pl.BlockSpec((tile, dim), lambda i: (i, 0))
    return call(
        functools.partial(mixed_kernel, len(back)),
        (rows // tile,),
        [pl.BlockSpec((tile, 1), lambda i: (i, 0)), block] + [whole((n, dim)) for _, n in back],
        block,
        jax.ShapeDtypeStruct((rows, dim), BF),
        scratch=[pltpu.VMEM((total, dim), BF)],
        after=after,
        cost=cost,
    )(place_col, middle, *[b for b, _ in back])


def second_back_kernel(count, place_ref, m_ref, c_ref, w_ref, g_ref, *refs):
    gm_ref, gat_ref, gh_ref, sums_ref, joined_ref = refs[count:]

    @pl.when(pl.program_id(0) == 0)
    def _():
        fill(joined_ref, refs[:count])

    grad_sent = pick_rows(place_ref[...], joined_ref[...])
    unit, inverse = normalize(m_ref[...])
    grad_middle = c_ref[...].astype(F32) + norm_back(unit, inverse, g_ref[1:2, :], grad_sent)
    gm_ref[...] = grad_middle
    grad_attn = grad_middle.astype(BF)
    gat_ref[...] = grad_attn.T
    gh_ref[...] = mm_nt(grad_attn, w_ref[...]).astype(BF)
    sums = jnp.concatenate(
        [jnp.sum(grad_sent * unit, axis=0, keepdims=True), jnp.sum(grad_sent, axis=0, keepdims=True)], axis=0
    )

    @pl.when(pl.program_id(0) == 0)
    def _():
        sums_ref[...] = sums

    @pl.when(pl.program_id(0) > 0)
    def _():
        sums_ref[...] += sums


def second_back(place_col, middle, cotangent, back, w_attn_out, gains, after=(), cost=0):
    rows, dim = middle.shape
    tile = 256
    total = sum(n for _, n in back)
    block = pl.BlockSpec((tile, dim), lambda i: (i, 0))
    return call(
        functools.partial(second_back_kernel, len(back)),
        (rows // tile,),
        [pl.BlockSpec((tile, 1), lambda i: (i, 0)), block, block, whole(w_attn_out.shape), whole(gains.shape)]
        + [whole((n, dim)) for _, n in back],
        [block, pl.BlockSpec((dim, tile), lambda i: (0, i)), block, whole((2, dim))],
        [
            jax.ShapeDtypeStruct((rows, dim), F32),
            jax.ShapeDtypeStruct((dim, rows), BF),
            jax.ShapeDtypeStruct((rows, dim), BF),
            jax.ShapeDtypeStruct((2, dim), F32),
        ],
        scratch=[pltpu.VMEM((total, dim), BF)],
        after=after,
        cost=cost,
    )(place_col, middle, cotangent, w_attn_out, gains, *[b for b, _ in back])


def first_back_kernel(x_ref, gm_ref, d_ref, w_ref, g_ref, dx_ref, sums_ref):
    dim = x_ref.shape[1]
    grad_normed = mm_nt(d_ref[0], w_ref[:, :dim])
    grad_normed += mm_nt(d_ref[1], w_ref[:, dim : 2 * dim])
    grad_normed += mm_nt(d_ref[2], w_ref[:, 2 * dim :])
    unit, inverse = normalize(x_ref[...].astype(F32))
    dx_ref[...] = gm_ref[...] + norm_back(unit, inverse, g_ref[0:1, :], grad_normed)
    sums = jnp.concatenate(
        [jnp.sum(grad_normed * unit, axis=0, keepdims=True), jnp.sum(grad_normed, axis=0, keepdims=True)], axis=0
    )

    @pl.when(pl.program_id(0) == 0)
    def _():
        sums_ref[...] = sums

    @pl.when(pl.program_id(0) > 0)
    def _():
        sums_ref[...] += sums


def first_back(tokens, grad_middle, grads, w_qkv, gains, after=(), cost=0):
    rows, dim = tokens.shape
    tile = 256
    block = pl.BlockSpec((tile, dim), lambda i: (i, 0))
    return call(
        first_back_kernel,
        (rows // tile,),
        [
            block,
            block,
            pl.BlockSpec((3, tile, dim), lambda i: (0, i, 0)),
            whole(w_qkv.shape),
            whole(gains.shape),
        ],
        [block, whole((2, dim))],
        [jax.ShapeDtypeStruct((rows, dim), F32), jax.ShapeDtypeStruct((2, dim), F32)],
        after=after,
        cost=cost,
    )(tokens, grad_middle, grads, w_qkv, gains)


def grad_hidden_kernel(count, wo_ref, *refs):
    gh_ref, turned_ref, joined_ref = refs[count:]

    @pl.when(pl.program_id(0) == 0)
    def _():
        fill(joined_ref, refs[:count])
        turned_ref[...] = joined_ref[...].T

    gh_ref[...] = mm_nt(joined_ref[...], wo_ref[...]).astype(BF)


def grad_hidden(grads, w_out, after=(), cost=0):
    total = sum(g.shape[0] for g in grads)
    units, dim = w_out.shape
    tile = 512
    return call(
        functools.partial(grad_hidden_kernel, len(grads)),
        (units // tile,),
        [pl.BlockSpec((tile, dim), lambda j: (j, 0))] + [whole(g.shape) for g in grads],
        [pl.BlockSpec((total, tile), lambda j: (0, j)), whole((dim, total))],
        [jax.ShapeDtypeStruct((total, units), BF), jax.ShapeDtypeStruct((dim, total), BF)],
        scratch=[pltpu.VMEM((total, dim), BF)],
        after=after,
        cost=cost,
    )(w_out, *grads)


def expert_kernel(count, aliased, wi_ref, gh_ref, *refs):
    blocks = refs[:count]
    outs = refs[count + aliased :]
    h_ref, gp_ref = outs[:2]
    gr_refs = outs[2:-2]
    joined_ref, gr_sum = outs[-2:]
    step = pl.program_id(0)

    @pl.when(step == 0)
    def _():
        fill(joined_ref, blocks)
        gr_sum[...] = jnp.zeros_like(gr_sum)

    slope = 0.7978845608028654
    for first in range(0, wi_ref.shape[1], SUB):
        cols = slice(first, first + SUB)
        preact = mm(joined_ref[...], wi_ref[:, cols])
        square = preact * preact
        tanh = jnp.tanh(preact * (slope + (slope * 0.044715) * square))
        half = 0.5 + 0.5 * tanh
        hidden = preact * half
        gate = half + hidden * (1.0 - tanh) * (slope + (3.0 * slope * 0.044715) * square)
        h_ref[:, cols] = hidden.astype(BF)
        grad_low = (gate * gh_ref[:, cols].astype(F32)).astype(BF)
        gp_ref[:, cols] = grad_low
        gr_sum[...] += mm_nt(grad_low, wi_ref[:, cols])

    @pl.when(step == pl.num_programs(0) - 1)
    def _():
        at = 0
        for ref in gr_refs:
            ref[...] = gr_sum[at : at + ref.shape[0], :].astype(BF)
            at += ref.shape[0]


def expert(blocks, gh, w_in, first, held=(), out_rows=None, after=(), cost=0):
    count = sum(b.shape[0] for b in blocks)
    dim, units = w_in.shape
    tile = 1024
    at = first // count
    act = pl.BlockSpec((count, tile), lambda j: (at, j))
    shape = jax.ShapeDtypeStruct(gh.shape, BF)
    held = list(held)
    pieces = out_rows or [b.shape[0] for b in blocks]
    return call(
        functools.partial(expert_kernel, len(blocks), len(held)),
        (units // tile,),
        [pl.BlockSpec((dim, tile), lambda j: (0, j)), act]
        + [whole(b.shape) for b in blocks]
        + [pl.BlockSpec(memory_space=pl.ANY)] * len(held),
        [act, act] + [whole((n, dim)) for n in pieces],
        [shape, shape] + [jax.ShapeDtypeStruct((n, dim), BF) for n in pieces],
        scratch=[pltpu.VMEM((count, dim), BF), pltpu.VMEM((count, dim), F32)],
        aliases={2 + len(blocks) + i: i for i in range(len(held))},
        after=after,
        cost=cost,
    )(w_in, gh, *blocks, *held)


def turn_kernel(count, *refs):
    o_ref, joined_ref = refs[count:]
    fill(joined_ref, refs[:count])
    o_ref[...] = joined_ref[...].T


def turned(blocks, after=(), cost=0):
    total = sum(b.shape[0] for b in blocks)
    dim = blocks[0].shape[1]
    return call(
        functools.partial(turn_kernel, len(blocks)),
        (1,),
        [whole(b.shape) for b in blocks],
        whole((dim, total)),
        jax.ShapeDtypeStruct((dim, total), BF),
        scratch=[pltpu.VMEM((total, dim), BF)],
        after=after,
        cost=cost,
    )(*blocks)


def produced_kernel(h_ref, wo_ref, *refs):
    o_refs, total_ref = refs[:-1], refs[-1]
    step = pl.program_id(0)
    part = mm(h_ref[...], wo_ref[...])

    @pl.when(step == 0)
    def _():
        total_ref[...] = part

    @pl.when(step > 0)
    def _():
        total_ref[...] += part

    @pl.when(step == pl.num_programs(0) - 1)
    def _():
        at = 0
        for ref in o_refs:
            ref[...] = total_ref[at : at + ref.shape[0], :].astype(BF)
            at += ref.shape[0]


def make_produced(hidden, w_out, pieces, after=(), cost=0):
    rows, units = hidden.shape
    dim = w_out.shape[1]
    tile = 512
    return call(
        produced_kernel,
        (units // tile,),
        [pl.BlockSpec((rows, tile), lambda j: (0, j)), pl.BlockSpec((tile, dim), lambda j: (j, 0))],
        [whole((n, dim)) for n in pieces],
        [jax.ShapeDtypeStruct((n, dim), BF) for n in pieces],
        scratch=[pltpu.VMEM((rows, dim), F32)],
        after=after,
        cost=cost,
    )(hidden, w_out)


def halves_kernel(count, slots, *refs):
    o_ref = refs[-1]
    for i in range(count):
        o_ref[i * slots : (i + 1) * slots, :] = refs[i][...]


def second_halves(blocks, slots, after=(), cost=0):
    dim = blocks[0].shape[1]
    count = len(blocks)
    return call(
        functools.partial(halves_kernel, count, slots),
        (1,),
        [pl.BlockSpec((slots, dim), lambda i: (1, 0))] * count,
        whole((count * slots, dim)),
        jax.ShapeDtypeStruct((count * slots, dim), BF),
        after=after,
        cost=cost,
    )(*blocks)


def add_kernel(*refs):
    o_ref = refs[-1]
    for i in range(o_ref.shape[0]):
        o_ref[i] = (refs[2 * i][0].astype(F32) + refs[2 * i + 1][0].astype(F32)).astype(BF)


def add_second(pairs, after=(), cost=0):
    _, rows, cols = pairs[0][0].shape
    tile = 256
    block = pl.BlockSpec((1, tile, cols), lambda i: (1, i, 0))
    return call(
        add_kernel,
        (rows // tile,),
        [block] * (2 * len(pairs)),
        pl.BlockSpec((len(pairs), tile, cols), lambda i: (0, i, 0)),
        jax.ShapeDtypeStruct((len(pairs), rows, cols), BF),
        after=after,
        cost=cost,
    )(*[a for pair in pairs for a in pair])


def stack_kernel(a_ref, b_ref, o_ref):
    o_ref[0:1, :] = a_ref[0:1, :]
    o_ref[1:2, :] = b_ref[0:1, :]
    o_ref[2:3, :] = a_ref[1:2, :]
    o_ref[3:4, :] = b_ref[1:2, :]


def stack_sums(first, second, after=(), cost=0):
    _, dim = first.shape
    return call(
        stack_kernel,
        (1,),
        [whole(first.shape), whole(second.shape)],
        whole((4, dim)),
        jax.ShapeDtypeStruct((4, dim), F32),
        after=after,
        cost=cost,
    )(first, second)


def weights_kernel(table_ref, l_ref, r_ref, send_a, send_b, keep_a, keep_b):
    half = l_ref.shape[0] // 2

    def put(step, first_ref, last_ref):
        @pl.when(pl.program_id(0) == step)
        def _():
            first_ref[0] = mm(l_ref[:half, :], r_ref[...]).astype(BF)
            last_ref[0] = mm(l_ref[half:, :], r_ref[...]).astype(BF)

    put(0, send_a, send_b)
    put(1, send_a, keep_b)
    put(2, keep_a, send_b)
    put(3, keep_a, keep_b)


def weight_parts(left, right, table, after=(), cost=0):
    dim, depth = left.shape
    quarter = right.shape[1] // 4
    half = jax.ShapeDtypeStruct((2, dim // 2, quarter), BF)

    def part(until):
        return pl.BlockSpec((1, dim // 2, quarter), lambda i, t: (jnp.where(i <= until, 1, 0), 0, 0))

    send_a, send_b, keep_a, keep_b = call(
        weights_kernel,
        (4,),
        [whole(left.shape), pl.BlockSpec((depth, quarter), lambda i, t: (0, t[i]))],
        [part(0), part(1), part(2), part(2)],
        [half] * 4,
        prefetch=1,
        after=after,
        cost=cost,
    )(table, left, right)
    return [send_a, send_b], [keep_a, keep_b]


def joint_kernel(bit_ref, g_ref, ga_ref, n_ref, h_ref, *out_refs):
    low = bit_ref[0] == 0
    for side in range(2):
        keep_ref, send_ref = out_refs[2 * side : 2 * side + 2]
        own = 2 * keep_ref.shape[0]
        cols = keep_ref.shape[2]
        at = slice(side * cols, (side + 1) * cols)
        qkv_part = mm(g_ref[...], n_ref[:, at]).reshape(own, g_ref.shape[0] // own, cols)
        out_part = mm(ga_ref[...], h_ref[:, at]).reshape(own, ga_ref.shape[0] // own, cols)
        both = jnp.concatenate([qkv_part, out_part], axis=1).astype(BF)
        both = both.reshape(own // 2, 2, *both.shape[1:])
        keep_ref[...] = jnp.where(low, both[:, 0], both[:, 1])
        send_ref[...] = jnp.where(low, both[:, 1], both[:, 0])


def joint(grads_t, grad_attn_t, normed, mixed_heads, bit, owners, after=(), cost=0):
    rows, dim = normed.shape
    steps = 8
    cols = dim // 2
    own = owners // steps
    qkv_rows = grads_t.shape[0] // steps
    out_rows = grad_attn_t.shape[0] // steps
    each = (qkv_rows + out_rows) // own
    block = pl.BlockSpec((own // 2, each, cols), lambda i, _: (i, 0, 0))
    return call(
        joint_kernel,
        (steps,),
        [
            pl.BlockSpec((qkv_rows, rows), lambda i, _: (i, 0)),
            pl.BlockSpec((out_rows, rows), lambda i, _: (i, 0)),
            whole((rows, dim)),
            whole((rows, dim)),
        ],
        [block] * 4,
        [jax.ShapeDtypeStruct((owners // 2, each, cols), BF)] * 4,
        prefetch=1,
        after=after,
        cost=cost,
    )(bit, grads_t, grad_attn_t, normed, mixed_heads)


def add_split_kernel(parts, _, *refs):
    keep_ref, send_ref = refs[4 * parts :]
    cols = refs[0].shape[2]
    for i in range(parts):
        mine_keep, got_keep, mine_send, got_send = refs[4 * i : 4 * i + 4]
        at = slice(i * cols, (i + 1) * cols)
        keep_ref[:, :, at] = (mine_keep[...].astype(F32) + got_keep[...].astype(F32)).astype(BF)
        send_ref[:, :, at] = (mine_send[...].astype(F32) + got_send[...].astype(F32)).astype(BF)


def add_split(pairs, bit, inner, after=(), cost=0):
    count, rows, cols = pairs[0][0].shape
    parts = len(pairs)
    outer = count // (2 * inner)
    each = min(inner, 2)
    steps = inner // each
    block = (each, rows, cols)
    keep = pl.BlockSpec(block, lambda i, j, b: ((2 * i + b[0]) * steps + j, 0, 0))
    send = pl.BlockSpec(block, lambda i, j, b: ((2 * i + 1 - b[0]) * steps + j, 0, 0))
    out = pl.BlockSpec((each, rows, parts * cols), lambda i, j, b: (i * steps + j, 0, 0))
    return call(
        functools.partial(add_split_kernel, parts),
        (outer, steps),
        [keep, keep, send, send] * parts,
        [out, out],
        [jax.ShapeDtypeStruct((count // 2, rows, parts * cols), BF)] * 2,
        prefetch=1,
        after=after,
        cost=cost,
    )(bit, *[a for mine, got in pairs for a in (mine, got, mine, got)])


def add_rows_kernel(count, *refs):
    total = refs[0][...]
    for i in range(1, count):
        total += refs[i][...]
    refs[count][...] = total


def add_rows(values, after=(), cost=0):
    shape = values[0].shape
    return call(
        functools.partial(add_rows_kernel, len(values)),
        (1,),
        [whole(shape)] * len(values),
        whole(shape),
        jax.ShapeDtypeStruct(shape, F32),
        after=after,
        cost=cost,
    )(*values)


def finish_kernel(turn, *refs):
    o_ref = refs[-1]
    total = refs[0][0].astype(F32) + refs[1][0].astype(F32) + refs[2][0].astype(F32)
    o_ref[...] = total.T if turn else total


def finish(keep, got, last, which, turn, side, held=None, after=(), cost=0):
    _, rows, cols = keep.shape
    tile = 256
    block = pl.BlockSpec((1, tile, cols), lambda i: (0, i, 0))
    steps = rows // tile
    shape = (cols, 2 * rows) if turn else (2 * rows, cols)
    out = (
        pl.BlockSpec((cols, tile), lambda i: (0, side * steps + i))
        if turn
        else pl.BlockSpec((tile, cols), lambda i: (side * steps + i, 0))
    )
    more = [] if held is None else [held]
    count = len(more)

    def body(*refs):
        finish_kernel(turn, *refs[:3], refs[3 + count])

    return call(
        body,
        (steps,),
        [block] * 2
        + [pl.BlockSpec((1, tile, cols), lambda i: (which, i, 0))]
        + [pl.BlockSpec(memory_space=pl.ANY)] * count,
        out,
        jax.ShapeDtypeStruct(shape, F32),
        aliases={3: 0} if more else None,
        after=after,
        cost=cost,
    )(keep, got, last, *more)


def swap(value, axis, mask):
    size = lax.axis_size(axis)
    return lax.ppermute(value, axis, [(i, i ^ mask) for i in range(size)])


def bit_of(axis, mask):
    return jnp.where((lax.axis_index(axis) & mask) > 0, 1, 0).astype(jnp.int32).reshape(1)


def bits_of(size):
    return [1 << i for i in range(size.bit_length() - 1)]


def on_device(
    tokens,
    norm_gains,
    norm_biases,
    w_qkv,
    w_attn_out,
    w_in,
    w_out,
    segment_ids,
    expert_ids,
    slots,
    cotangent,
):
    tok, dim = tokens.shape
    head_dim = dim // HEADS
    wide = lax.axis_size("wide")
    narrow = lax.axis_size("narrow")
    units = w_in.shape[2]
    me_wide = lax.axis_index("wide")
    me_narrow = lax.axis_index("narrow")
    capacity = tok * 9 // (8 * wide)
    w_in = w_in[0]
    w_out = w_out[0]
    zs = wide // 2
    slots_all = zs * capacity
    groups = [list(range(zs // 2)), list(range(zs // 2, 3 * zs // 4)), list(range(3 * zs // 4, zs))]
    apart = capacity % 16 == 0

    def joinable(blocks):
        return blocks if apart else [jnp.concatenate(blocks, axis=0)]

    def by_position(pieces):
        return list(pieces) if apart else [q for p in pieces for q in jnp.split(p, p.shape[0] // (2 * capacity))]

    def piece_rows(group):
        return [2 * capacity] * len(group) if apart else [2 * capacity * len(group)]

    away = expert_ids ^ me_wide
    kept = slots < capacity
    base = (away >> 1) * capacity + slots
    core = away & 1
    nowhere = 2 * slots_all
    place_own = jnp.where(kept & (core == 0), base, nowhere).astype(jnp.int32)[None, :]
    place_sent = jnp.where(kept & (core == 1), base, nowhere).astype(jnp.int32)[None, :]
    places = [place_own, swap(place_sent, "wide", 1)]
    place_col = jnp.where(kept, core * slots_all + base, nowhere).astype(jnp.int32)[:, None]
    doc_col = segment_ids.reshape(tok, 1)

    def exchange(blocks, positions):
        return [swap(blocks[z], "wide", 2 * z) if z else blocks[z] for z in positions]

    def bring_back(blocks, after, cost=0):
        if not apart:
            theirs = jnp.concatenate([b[capacity:] for b in blocks], axis=0)
            own = [(jnp.concatenate([b[:capacity] for b in blocks], axis=0), slots_all)]
        else:
            theirs = second_halves(blocks, capacity, after, cost)
            own = [(b, capacity) for b in blocks]
        return own + [(swap(theirs, "wide", 1), slots_all)], theirs

    cotangent_other = swap(cotangent, "wide", 1)
    normed = first_norm(tokens, norm_gains, norm_biases)
    sent_grads = dispatch_rows(places, [[cotangent], [cotangent_other]], zs, capacity, after=[normed])
    expert_grads = exchange(sent_grads, range(zs))

    projected = project(normed, w_qkv, after=[sent_grads[0]])
    mixed_heads, log_total = attn_fwd(projected, doc_col, head_dim)
    middle, sent_first = make_middle(tokens, mixed_heads, w_attn_out, norm_gains, norm_biases, 0, 2)
    other_first = swap(sent_first, "wide", 1)
    middle, sent_last = make_middle(
        tokens, mixed_heads, w_attn_out, norm_gains, norm_biases, 1, 2, [middle], after=expert_grads
    )
    other_last = swap(sent_last, "wide", 1)
    sent_rows = dispatch_rows(places, [[sent_first, sent_last], [other_first, other_last]], zs, capacity)
    expert_rows = exchange(sent_rows, range(zs))

    gh, grads_t = grad_hidden(joinable(expert_grads), w_out, after=[sent_rows[0]])
    held = ()
    back_grads = []
    before = [gh]
    for group in groups:
        blocks = joinable([expert_rows[z] for z in group])
        outs = expert(blocks, gh, w_in, 2 * group[0] * capacity, held, piece_rows(group), after=before)
        held = outs[:2]
        before = [outs[2]]
        pieces = by_position(outs[2:])
        back_grads += exchange({z: pieces[i] for i, z in enumerate(group)}, group)
    hidden, grad_preact = held

    masks = [(1, 2), (2, 1)]
    sides = range(2)
    table = jnp.array([3, 1, 2, 0], jnp.int32) ^ me_narrow

    def first_step(send):
        return [swap(send[side], "narrow", masks[side][0]) for side in sides]

    send_out, keep_out = weight_parts(grads_t, hidden, table, after=before)
    got_out = first_step(send_out)
    produced = make_produced(hidden, w_out, piece_rows(range(zs)), after=send_out)
    back_rows = exchange(by_position(produced), range(zs))
    rows_t = turned(joinable(expert_rows), after=[produced[0]])
    send_in, keep_in = weight_parts(rows_t, grad_preact, table)
    got_in = first_step(send_in)
    back_grads, _ = bring_back(back_grads, [send_in[0]], COST_GATE)
    grad_middle, grad_attn_t, grad_heads, sums_two = second_back(
        place_col, middle, cotangent, back_grads, w_attn_out, norm_gains, after=send_in + got_out
    )
    grads, grads_all_t = attn_bwd(projected, mixed_heads, grad_heads, log_total, doc_col, head_dim, 0, 1)
    back_rows, sent = bring_back(back_rows, [grads])
    last = []
    before = [grads, sent]
    for side in sides:
        again = add_second([(keep_out[side], got_out[side]), (keep_in[side], got_in[side])], after=before)
        before = [again]
        last.append(swap(again, "narrow", masks[side][1]))
    grads_all_t = grads_all_t.reshape(3 * dim, tok)

    owners = narrow * wide
    own_qkv = 3 * dim // owners
    n_bits = bits_of(narrow)
    w_bits = bits_of(wide)
    names = [("narrow", b) for b in reversed(n_bits)] + [("wide", b) for b in reversed(w_bits)]
    core_bit = ("wide", 1)
    orders = [[("narrow", b) for b in masks[side]] + [("wide", b) for b in w_bits[1:]] for side in sides]
    bits = {name: bit_of(*name) for name in names}
    kept_a, sent_a, kept_b, sent_b = joint(
        grads_all_t, grad_attn_t, normed, mixed_heads, bits[core_bit], owners, after=before
    )
    got_a, got_b = [swap(sent, *core_bit) for sent in (sent_a, sent_b)]
    state = [(kept_a, got_a, names[:-1]), (kept_b, got_b, names[:-1])]

    def narrow_step(after, number):
        for side in sides:
            kept, got, left = state[side]
            step = orders[side][number]
            at = left.index(step)
            kept, sent = add_split([(kept, got)], bits[step], 1 << (len(left) - 1 - at), after=after)
            state[side] = (kept, swap(sent, *step), left[:at] + left[at + 1 :])
        return [state[side][0] for side in sides]

    d_tokens, sums_one = first_back(tokens, grad_middle, grads, w_qkv, norm_gains, after=[kept_a])
    sums = stack_sums(sums_one, sums_two, after=last, cost=2)
    reached = narrow_step([sums], 0)
    mixed = make_mixed(place_col, middle, back_rows, after=reached)
    reached = narrow_step([mixed], 1)
    rounds = [("narrow", n_bits)] + [("wide", w_bits[i : i + 2]) for i in range(0, len(w_bits), 2)]

    def sum_round(sums, number, after):
        axis, some = rounds[number]
        others = sorted({sum(c) for c in itertools.product(*[(0, b) for b in some])} - {0})
        return add_rows([sums] + [swap(sums, axis, m) for m in others], after=after)

    d_w_out = finish(keep_out[0], got_out[0], last[0], 0, True, 0, after=reached)
    d_w_out = finish(keep_out[1], got_out[1], last[1], 0, True, 1, d_w_out)
    d_w_in = finish(keep_in[0], got_in[0], last[0], 1, False, 0, after=[d_w_out])
    d_w_in = finish(keep_in[1], got_in[1], last[1], 1, False, 1, d_w_in)
    pairs = [state[side][:2] for side in sides]
    left = state[0][2]
    before = [d_w_in]
    for number, step in enumerate(("wide", b) for b in w_bits[1:]):
        at = left.index(step)
        kept, sent = add_split(pairs, bits[step], 1 << (len(left) - 1 - at), after=before)
        pairs = [(kept, swap(sent, *step))]
        left = left[:at] + left[at + 1 :]
        sums = sum_round(sums, number, [kept])
        before = []
    for number in range(len(w_bits) - 1, len(rounds)):
        sums = sum_round(sums, number, ())
    value = pairs[0][0][0].astype(F32) + pairs[0][1][0].astype(F32)
    d_w_qkv = value[:own_qkv].T
    d_w_attn_out = value[own_qkv:].T
    own = dim // owners
    sums = lax.dynamic_slice_in_dim(sums, (me_narrow * wide + me_wide) * own, own, 1)
    return (mixed, d_tokens, sums[:2], sums[2:], d_w_qkv, d_w_attn_out, d_w_in[None], d_w_out[None])


def solution(mesh):
    placed = (
        P(("narrow", "wide"), None),
        P(),
        P(),
        P(),
        P(),
        P("wide", None, None),
        P("wide", None, None),
        P(("narrow", "wide"), None),
        P(("narrow", "wide")),
        P(("narrow", "wide")),
        P(("narrow", "wide"), None),
    )
    return jax.shard_map(
        on_device,
        mesh=mesh,
        in_specs=placed,
        out_specs=(
            P(("narrow", "wide"), None),
            P(("narrow", "wide"), None),
            P(None, ("narrow", "wide")),
            P(None, ("narrow", "wide")),
            P(None, ("narrow", "wide")),
            P(None, ("narrow", "wide")),
            P("wide", None, "narrow"),
            P("wide", "narrow", None),
        ),
        check_vma=False,
    )
```

```python
import functools
import itertools

import jax
import jax.numpy as jnp
from jax import lax
from jax.experimental import pallas as pl
from jax.experimental.pallas import tpu as pltpu
from jax.sharding import PartitionSpec as P

HEADS = 16
EPSILON = 1e-05
NEGATIVE = -1e30
BAND = 512
BLOCK = 256
SUB = 256
TILE = 256
SPARE = 16
PARTS = 3
F32 = jnp.float32
BF = jnp.bfloat16
LAST_ROWS = 128
COST_GATE = 6
COST_MIDDLE = 25
PAIRS_FIRST = 5
VMEM_BYTES = 48 * 1024 * 1024


def mm(a, b):
    return lax.dot_general(a, b, (((1,), (0,)), ((), ())), preferred_element_type=F32)


def mm_nt(a, b):
    return lax.dot_general(a, b, (((1,), (1,)), ((), ())), preferred_element_type=F32)


def mm_tn(a, b):
    return lax.dot_general(a, b, (((0,), (0,)), ((), ())), preferred_element_type=F32)


ORDER = []


def call(kernel, grid, in_specs, out_specs, out_shape, scratch=(), prefetch=0, aliases=None, after=(), cost=0):
    count = prefetch + len(in_specs)
    after = [*after, *ORDER]
    extra = len(after)
    several = isinstance(out_specs, list)
    outs = len(out_specs) if several else 1

    def body(*refs):
        rest = refs[count + extra :]
        kernel(*refs[:count], *rest[:outs], *rest[outs + 1 :])
        rest[outs][...] = jnp.zeros_like(rest[outs])

    run = pl.pallas_call(
        body,
        grid_spec=pltpu.PrefetchScalarGridSpec(
            num_scalar_prefetch=prefetch,
            grid=grid,
            in_specs=list(in_specs) + [pl.BlockSpec(memory_space=pl.ANY)] * extra,
            out_specs=[*(out_specs if several else [out_specs]), whole((8, 128))],
            scratch_shapes=list(scratch),
        ),
        out_shape=[*(out_shape if several else [out_shape]), jax.ShapeDtypeStruct((8, 128), F32)],
        input_output_aliases=aliases or {},
        compiler_params=pltpu.CompilerParams(vmem_limit_bytes=VMEM_BYTES),
        cost_estimate=pl.CostEstimate(flops=1 + int(cost * 1.15e9), bytes_accessed=0, transcendentals=0),
    )

    def apply(*args):
        *results, token = run(*args, *after)
        ORDER[:] = [token]
        return results if several else results[0]

    return apply


def whole(shape):
    return pl.BlockSpec(shape, lambda *_: (0,) * len(shape))


def normalize(stream):
    average = jnp.mean(stream, axis=-1, keepdims=True)
    centered = stream - average
    inverse = lax.rsqrt(jnp.mean(centered * centered, axis=-1, keepdims=True) + EPSILON)
    return centered * inverse, inverse


def norm_back(unit, inverse, gain, grad):
    scaled = grad * gain
    first = jnp.mean(scaled, axis=-1, keepdims=True)
    second = jnp.mean(scaled * unit, axis=-1, keepdims=True)
    return inverse * (scaled - first - unit * second)


def first_norm_kernel(x_ref, g_ref, b_ref, n_ref):
    unit, _inverse = normalize(x_ref[...].astype(F32))
    n_ref[...] = (unit * g_ref[0:1, :] + b_ref[0:1, :]).astype(BF)


def first_norm(tokens, gains, biases, after=(), cost=0):
    rows, dim = tokens.shape
    block = pl.BlockSpec((256, dim), lambda i: (i, 0))
    return call(
        first_norm_kernel,
        (rows // 256,),
        [block, whole(gains.shape), whole(biases.shape)],
        block,
        jax.ShapeDtypeStruct((rows, dim), BF),
        after=after,
        cost=cost,
    )(tokens, gains, biases)


def project_kernel(n_ref, w_ref, p_ref):
    p_ref[...] = mm(n_ref[...], w_ref[...]).astype(BF)


def project(normed, w_qkv, after=(), cost=0):
    rows, dim = normed.shape
    cols = w_qkv.shape[1]
    tile = 768
    return call(
        project_kernel,
        (cols // tile,),
        [whole((rows, dim)), pl.BlockSpec((dim, tile), lambda j: (0, j))],
        pl.BlockSpec((rows, tile), lambda j: (0, j)),
        jax.ShapeDtypeStruct((rows, cols), BF),
        after=after,
        cost=cost,
    )(normed, w_qkv)


def fill_masks(col_ref, fq_ref, fk_ref, tri_ref, head_dim):
    length = col_ref.shape[0]
    doc = lax.broadcasted_iota(jnp.int32, fq_ref.shape, 1) % head_dim
    same = doc == col_ref[...]
    fq_ref[...] = jnp.where(same, 1.0, 0.0).astype(BF)
    fk_ref[...] = jnp.where(same, 0.0, NEGATIVE).astype(BF)
    key_pos = lax.broadcasted_iota(jnp.int32, tri_ref.shape, 0)
    query_pos = lax.broadcasted_iota(jnp.int32, tri_ref.shape, 1)
    tri_ref[...] = jnp.where(key_pos <= query_pos, 0.0, NEGATIVE).astype(F32)


def lanes_of(shape, head, head_dim):
    lane = lax.broadcasted_iota(jnp.int32, shape, 1)
    return (lane >= head * head_dim) & (lane < (head + 1) * head_dim)


def attn_fwd_kernel(head_dim, col_ref, q_ref, k_ref, v_ref, o_ref, ol_ref, lse_ref, fq_ref, fk_ref, tri_ref, vt_ref, qh_ref, kh_ref):
    length, pair = q_ref.shape
    scale = head_dim**-0.5
    per = pair // head_dim

    @pl.when(pl.program_id(0) == 0)
    def _():
        fill_masks(col_ref, fq_ref, fk_ref, tri_ref, head_dim)
        vt_ref[...] = jnp.ones_like(vt_ref)

    value_t = v_ref[...].T
    query = q_ref[...] * BF(scale)
    for head in range(per):
        inside = lanes_of(query.shape, head, head_dim)
        vt_ref[head, :head_dim, :] = value_t[head * head_dim : (head + 1) * head_dim, :]
        qh_ref[head] = jnp.where(inside, query, fq_ref[...])
        kh_ref[head] = jnp.where(inside, k_ref[...], fk_ref[...])
    def first_stage(q_first):
        k_first = max(0, q_first - BAND)
        allparts = [[] for _ in range(per)]
        for k_at in range(k_first, q_first + BLOCK, BLOCK):
            for head in range(per):
                scores = mm_nt(kh_ref[head, k_at : k_at + BLOCK, :], qh_ref[head, q_first : q_first + BLOCK, :])
                if k_at == q_first:
                    scores = scores + tri_ref[...]
                allparts[head].append(scores)
        tops = [functools.reduce(jnp.maximum, [jnp.max(p, axis=0, keepdims=True) for p in parts]) for parts in allparts]
        return allparts, tops

    def second_stage(q_first, allparts, tops):
        k_first = max(0, q_first - BAND)
        q_at = slice(q_first, q_first + BLOCK)
        totals = [None] * per
        for i in range(len(allparts[0])):
            k_at = k_first + i * BLOCK
            for head in range(per):
                prob = jnp.exp(allparts[head][i] - tops[head]).astype(BF)
                part = mm(vt_ref[head, :, k_at : k_at + BLOCK], prob)
                totals[head] = part if totals[head] is None else totals[head] + part
        outs = []
        for head in range(per):
            total = totals[head]
            sums = total[head_dim : head_dim + 1, :]
            outs.append(total[:head_dim, :] / sums)
            lse_ref[0, head : head + 1, q_at] = tops[head] + jnp.log(sums)
        o_ref[q_at, :], ol_ref[q_at, :] = in_parts(jnp.concatenate(outs, axis=0).T, 2)

    firsts = list(range(0, length, BLOCK))
    ahead = first_stage(firsts[0])
    for i, q_first in enumerate(firsts):
        now = ahead
        if i + 1 < len(firsts):
            ahead = first_stage(firsts[i + 1])
        second_stage(q_first, *now)


def attn_fwd(projected, doc_col, head_dim, cost=0):
    length = projected.shape[0]
    width = projected.shape[1] // 3
    pair = 128
    pairs = width // pair
    per = pair // head_dim
    specs = [pl.BlockSpec((length, pair), functools.partial(lambda s, j: (0, s * pairs + j), s)) for s in range(3)]
    return call(
        functools.partial(attn_fwd_kernel, head_dim),
        (pairs,),
        [whole(doc_col.shape)] + specs,
        [pl.BlockSpec((length, pair), lambda j: (0, j))] * 2 + [pl.BlockSpec((1, per, length), lambda j: (j, 0, 0))],
        [jax.ShapeDtypeStruct((length, width), BF)] * 2 + [jax.ShapeDtypeStruct((pairs, per, length), F32)],
        scratch=[
            pltpu.VMEM((length, pair), BF),
            pltpu.VMEM((length, pair), BF),
            pltpu.VMEM((BLOCK, BLOCK), F32),
            pltpu.VMEM((per, head_dim + 16, length), BF),
            pltpu.VMEM((per, length, pair), BF),
            pltpu.VMEM((per, length, pair), BF),
        ],
        cost=cost,
    )(doc_col, projected, projected, projected)


def in_parts(x, count):
    parts = []
    for _ in range(count):
        parts.append(x.astype(BF))
        x = x - parts[-1].astype(F32)
    return parts


def attn_bwd_kernel(head_dim, col_ref, q_ref, k_ref, v_ref, o_ref, ol_ref, do_ref, lse_ref, g_ref, gt_ref,
                    fq_ref, fk_ref, tri_ref, qx, kx, vx, dox, qm, dom, dk_sum, dv_sum):
    length, pair = q_ref.shape
    scale = head_dim**-0.5
    per = pair // head_dim

    @pl.when(pl.program_id(0) == 0)
    def _():
        fill_masks(col_ref, fq_ref, fk_ref, tri_ref, head_dim)

    key_t = (k_ref[...] * BF(scale)).T
    query = q_ref[...] * BF(scale)
    grad = do_ref[...]
    lane = lax.broadcasted_iota(jnp.int32, (length, pair), 1)
    zero = jnp.zeros_like(query)
    one = jnp.ones_like(query)
    lse_rows = jnp.concatenate([lse_ref[0], jnp.zeros((8 - per, length), F32)], axis=0)
    lse_cols = lse_rows.T
    product = grad.astype(F32) * (o_ref[...].astype(F32) + ol_ref[...].astype(F32))
    for head in range(per):
        inside = lanes_of(query.shape, head, head_dim)
        slots = [lane == (1 - head) * head_dim + head_dim // 2 + i for i in range(PARTS)]
        some = functools.reduce(jnp.logical_or, slots)
        delta = jnp.sum(jnp.where(inside, product, 0.0), axis=1, keepdims=True)

        def spread(column, rest):
            for slot, part in zip(slots, in_parts(-column, PARTS)):
                rest = jnp.where(slot, part, rest)
            return rest

        qm[head] = jnp.where(inside, query, zero)
        dom[head] = jnp.where(inside, grad, zero)
        qx[head] = jnp.where(inside, query, spread(lse_cols[:, head : head + 1], fq_ref[...]))
        kx[head] = jnp.where(inside, k_ref[...], jnp.where(some, one, fk_ref[...]))
        vx[head] = jnp.where(inside, v_ref[...], jnp.where(some, one, zero))
        dox[head] = jnp.where(inside, grad, spread(delta, zero))
    dk_sum[...] = jnp.zeros_like(dk_sum)
    dv_sum[...] = jnp.zeros_like(dv_sum)
    for q_first in range(0, length, BLOCK):
        q_at = slice(q_first, q_first + BLOCK)
        dq_parts = [None] * per
        for k_first in range(max(0, q_first - BAND), q_first + BLOCK, BLOCK):
            k_at = slice(k_first, k_first + BLOCK)
            scores = [mm_nt(kx[h, k_at, :], qx[h, q_at, :]) for h in range(per)]
            prob_grads = [mm_nt(vx[h, k_at, :], dox[h, q_at, :]) for h in range(per)]
            if k_first == q_first:
                scores = [s + tri_ref[...] for s in scores]
            probs = [jnp.exp(s) for s in scores]
            score_grads = [(p * d).astype(BF) for p, d in zip(probs, prob_grads)]
            probs = [p.astype(BF) for p in probs]
            dv_sum[k_at, :] += mm(
                jnp.concatenate(probs, axis=1), jnp.concatenate([dom[h, q_at, :] for h in range(per)], axis=0)
            )
            dk_sum[k_at, :] += mm(
                jnp.concatenate(score_grads, axis=1), jnp.concatenate([qm[h, q_at, :] for h in range(per)], axis=0)
            )
            for h in range(per):
                one = mm(key_t[h * head_dim : (h + 1) * head_dim, k_at], score_grads[h])
                dq_parts[h] = one if dq_parts[h] is None else dq_parts[h] + one
        dq_t = jnp.concatenate(dq_parts, axis=0)
        gt_ref[0, :, q_at] = dq_t.astype(BF)
        g_ref[0, q_at, :] = dq_t.T.astype(BF)
    for i, ref in ((1, dk_sum), (2, dv_sum)):
        low = ref[...].astype(BF)
        g_ref[i] = low
        gt_ref[i] = low.T


def attn_bwd(projected, mixed_heads, mixed_low, grad_heads, log_total, doc_col, head_dim, first, steps, held=(), after=(), cost=0):
    length = projected.shape[0]
    width = projected.shape[1] // 3
    pair = 128
    pairs = width // pair
    per = pair // head_dim
    specs = [
        pl.BlockSpec((length, pair), functools.partial(lambda s, j: (0, s * pairs + first + j), s)) for s in range(3)
    ]
    held = list(held)
    count = len(held)
    kernel = functools.partial(attn_bwd_kernel, head_dim)
    one = pl.BlockSpec((length, pair), lambda j: (0, first + j))
    return call(
        lambda *refs: kernel(*refs[:8], *refs[8 + count :]),
        (steps,),
        [whole(doc_col.shape)] + specs + [one, one, one, pl.BlockSpec((1, per, length), lambda j: (first + j, 0, 0))]
        + [pl.BlockSpec(memory_space=pltpu.HBM)] * count,
        [
            pl.BlockSpec((3, length, pair), lambda j: (0, 0, first + j)),
            pl.BlockSpec((3, pair, length), lambda j: (0, first + j, 0)),
        ],
        [pltpu.HBM((3, length, width), BF), pltpu.HBM((3, width, length), BF)],
        scratch=[
            pltpu.VMEM((length, pair), BF),
            pltpu.VMEM((length, pair), BF),
            pltpu.VMEM((BLOCK, BLOCK), F32),
        ]
        + [pltpu.VMEM((per, length, pair), BF)] * 6
        + [pltpu.VMEM((length, pair), F32)] * 2,
        aliases={8 + i: i for i in range(count)},
        after=after,
        cost=cost,
    )(doc_col, projected, projected, projected, mixed_heads, mixed_low, grad_heads, log_total, *held)


def middle_kernel(x_ref, h_ref, w_ref, g_ref, b_ref, *refs):
    m_ref, s_ref = refs[-2:]
    middle = x_ref[...].astype(F32) + mm(h_ref[...], w_ref[...])
    m_ref[...] = middle
    unit, _inverse = normalize(middle)
    s_ref[...] = (unit * g_ref[1:2, :] + b_ref[1:2, :]).astype(BF)


def make_middle(tokens, mixed_heads, w_attn_out, gains, biases, first, count, held=(), after=(), cost=0):
    rows, dim = tokens.shape
    tile = min(count, 448)
    at = first // tile
    block = pl.BlockSpec((tile, dim), lambda i: (at + i, 0))
    held = list(held)
    return call(
        middle_kernel,
        (count // tile,),
        [block, block, whole(w_attn_out.shape), whole(gains.shape), whole(biases.shape)]
        + [pl.BlockSpec(memory_space=pltpu.HBM)] * len(held),
        [block, pl.BlockSpec((tile, dim), lambda i: (i, 0))],
        [pltpu.HBM((rows, dim), F32), jax.ShapeDtypeStruct((count, dim), BF)],
        aliases={5: 0} if held else None,
        after=after,
        cost=cost,
    )(tokens, mixed_heads, w_attn_out, gains, biases, *held)


def dispatch_kernel(slots, added, *refs):
    o_refs = refs[4 + added :]
    count = slots * (o_refs[0].shape[0] // (2 * slots)) * len(o_refs)
    for side in range(2):
        place, rows = refs[side], refs[2 + side]
        slot = lax.broadcasted_iota(jnp.int32, (count, rows.shape[0]), 0)
        low = mm(jnp.where(slot == place[...], 1.0, 0.0).astype(BF), rows[...]).astype(BF)
        for i, ref in enumerate(o_refs):
            each = count // len(o_refs)
            at = slice(side * each, (side + 1) * each)
            part = low[i * each : (i + 1) * each]
            ref[at, :] = part + refs[4 + i][at, :] if added else part


def dispatch_rows(places, rows, positions, slots, added=(), after=(), cost=0):
    dim = rows[0].shape[1]
    count = positions if slots % 16 == 0 else 1
    shape = (2 * slots * (positions // count), dim)
    return call(
        functools.partial(dispatch_kernel, slots, len(added)),
        (1,),
        [whole(a.shape) for a in [*places, *rows]] + [whole(shape)] * len(added),
        [whole(shape)] * count,
        [jax.ShapeDtypeStruct(shape, BF)] * count,
        after=after,
        cost=cost,
    )(*places, *rows, *added)


def separate(out, positions, slots):
    if len(out) > 1:
        return out
    sides = out[0].reshape(2, positions, slots, out[0].shape[1])
    return [sides[:, p].reshape(2 * slots, out[0].shape[1]) for p in range(positions)]


def fill(joined_ref, block_refs):
    at = 0
    for ref in block_refs:
        joined_ref[at : at + ref.shape[0], :] = ref[...]
        at += ref.shape[0]


def pick_rows(place, back):
    slot = lax.broadcasted_iota(jnp.int32, (place.shape[0], back.shape[0]), 1)
    return mm(jnp.where(slot == place, 1.0, 0.0).astype(BF), back)


def mixed_kernel(count, place_ref, m_ref, *refs):
    o_ref, joined_ref = refs[count:]

    @pl.when(pl.program_id(0) == 0)
    def _():
        fill(joined_ref, refs[:count])

    o_ref[...] = (m_ref[...] + pick_rows(place_ref[...], joined_ref[...])).astype(BF)


def make_mixed(place_col, middle, back, after=(), cost=0):
    rows, dim = middle.shape
    tile = 256
    total = sum(n for _, n in back)
    block = pl.BlockSpec((tile, dim), lambda i: (i, 0))
    return call(
        functools.partial(mixed_kernel, len(back)),
        (rows // tile,),
        [pl.BlockSpec((tile, 1), lambda i: (i, 0)), block] + [whole((n, dim)) for _, n in back],
        block,
        jax.ShapeDtypeStruct((rows, dim), BF),
        scratch=[pltpu.VMEM((total, dim), BF)],
        after=after,
        cost=cost,
    )(place_col, middle, *[b for b, _ in back])


def second_back_kernel(count, place_ref, m_ref, c_ref, w_ref, g_ref, *refs):
    gm_ref, gat_ref, gh_ref, sums_ref, joined_ref = refs[count:]

    @pl.when(pl.program_id(0) == 0)
    def _():
        fill(joined_ref, refs[:count])

    grad_sent = pick_rows(place_ref[...], joined_ref[...])
    unit, inverse = normalize(m_ref[...])
    grad_middle = c_ref[...].astype(F32) + norm_back(unit, inverse, g_ref[1:2, :], grad_sent)
    gm_ref[...] = grad_middle
    grad_attn = grad_middle.astype(BF)
    gat_ref[...] = grad_attn.T
    gh_ref[...] = mm_nt(grad_attn, w_ref[...]).astype(BF)
    sums = jnp.concatenate(
        [jnp.sum(grad_sent * unit, axis=0, keepdims=True), jnp.sum(grad_sent, axis=0, keepdims=True)], axis=0
    )

    @pl.when(pl.program_id(0) == 0)
    def _():
        sums_ref[...] = sums

    @pl.when(pl.program_id(0) > 0)
    def _():
        sums_ref[...] += sums


def second_back(place_col, middle, cotangent, back, w_attn_out, gains, after=(), cost=0):
    rows, dim = middle.shape
    tile = 256
    total = sum(n for _, n in back)
    block = pl.BlockSpec((tile, dim), lambda i: (i, 0))
    return call(
        functools.partial(second_back_kernel, len(back)),
        (rows // tile,),
        [pl.BlockSpec((tile, 1), lambda i: (i, 0)), block, block, whole(w_attn_out.shape), whole(gains.shape)]
        + [whole((n, dim)) for _, n in back],
        [block, pl.BlockSpec((dim, tile), lambda i: (0, i)), block, whole((2, dim))],
        [
            jax.ShapeDtypeStruct((rows, dim), F32),
            jax.ShapeDtypeStruct((dim, rows), BF),
            jax.ShapeDtypeStruct((rows, dim), BF),
            jax.ShapeDtypeStruct((2, dim), F32),
        ],
        scratch=[pltpu.VMEM((total, dim), BF)],
        after=after,
        cost=cost,
    )(place_col, middle, cotangent, w_attn_out, gains, *[b for b, _ in back])


def first_back_kernel(x_ref, gm_ref, d_ref, w_ref, g_ref, dx_ref, sums_ref):
    dim = x_ref.shape[1]
    grad_normed = mm_nt(d_ref[0], w_ref[:, :dim])
    grad_normed += mm_nt(d_ref[1], w_ref[:, dim : 2 * dim])
    grad_normed += mm_nt(d_ref[2], w_ref[:, 2 * dim :])
    unit, inverse = normalize(x_ref[...].astype(F32))
    dx_ref[...] = gm_ref[...] + norm_back(unit, inverse, g_ref[0:1, :], grad_normed)
    sums = jnp.concatenate(
        [jnp.sum(grad_normed * unit, axis=0, keepdims=True), jnp.sum(grad_normed, axis=0, keepdims=True)], axis=0
    )

    @pl.when(pl.program_id(0) == 0)
    def _():
        sums_ref[...] = sums

    @pl.when(pl.program_id(0) > 0)
    def _():
        sums_ref[...] += sums


def first_back(tokens, grad_middle, grads, w_qkv, gains, after=(), cost=0):
    rows, dim = tokens.shape
    tile = 256
    block = pl.BlockSpec((tile, dim), lambda i: (i, 0))
    return call(
        first_back_kernel,
        (rows // tile,),
        [
            block,
            block,
            pl.BlockSpec((3, tile, dim), lambda i: (0, i, 0)),
            whole(w_qkv.shape),
            whole(gains.shape),
        ],
        [block, whole((2, dim))],
        [jax.ShapeDtypeStruct((rows, dim), F32), jax.ShapeDtypeStruct((2, dim), F32)],
        after=after,
        cost=cost,
    )(tokens, grad_middle, grads, w_qkv, gains)


def grad_hidden_kernel(count, wo_ref, *refs):
    gh_ref, turned_ref, joined_ref = refs[count:]

    @pl.when(pl.program_id(0) == 0)
    def _():
        fill(joined_ref, refs[:count])
        turned_ref[...] = joined_ref[...].T

    gh_ref[...] = mm_nt(joined_ref[...], wo_ref[...]).astype(BF)


def grad_hidden(grads, w_out, after=(), cost=0):
    total = sum(g.shape[0] for g in grads)
    units, dim = w_out.shape
    tile = 512
    return call(
        functools.partial(grad_hidden_kernel, len(grads)),
        (units // tile,),
        [pl.BlockSpec((tile, dim), lambda j: (j, 0))] + [whole(g.shape) for g in grads],
        [pl.BlockSpec((total, tile), lambda j: (0, j)), whole((dim, total))],
        [jax.ShapeDtypeStruct((total, units), BF), jax.ShapeDtypeStruct((dim, total), BF)],
        scratch=[pltpu.VMEM((total, dim), BF)],
        after=after,
        cost=cost,
    )(w_out, *grads)


def expert_kernel(count, aliased, wi_ref, gh_ref, *refs):
    blocks = refs[:count]
    outs = refs[count + aliased :]
    h_ref, gp_ref = outs[:2]
    gr_refs = outs[2:-2]
    joined_ref, gr_sum = outs[-2:]
    step = pl.program_id(0)

    @pl.when(step == 0)
    def _():
        fill(joined_ref, blocks)
        gr_sum[...] = jnp.zeros_like(gr_sum)

    slope = 0.7978845608028654
    for first in range(0, wi_ref.shape[1], SUB):
        cols = slice(first, first + SUB)
        preact = mm(joined_ref[...], wi_ref[:, cols])
        square = preact * preact
        tanh = jnp.tanh(preact * (slope + (slope * 0.044715) * square))
        half = 0.5 + 0.5 * tanh
        hidden = preact * half
        gate = half + hidden * (1.0 - tanh) * (slope + (3.0 * slope * 0.044715) * square)
        h_ref[:, cols] = hidden.astype(BF)
        grad_low = (gate * gh_ref[:, cols].astype(F32)).astype(BF)
        gp_ref[:, cols] = grad_low
        gr_sum[...] += mm_nt(grad_low, wi_ref[:, cols])

    @pl.when(step == pl.num_programs(0) - 1)
    def _():
        at = 0
        for ref in gr_refs:
            ref[...] = gr_sum[at : at + ref.shape[0], :].astype(BF)
            at += ref.shape[0]


def expert(blocks, gh, w_in, first, held=(), out_rows=None, after=(), cost=0):
    count = sum(b.shape[0] for b in blocks)
    dim, units = w_in.shape
    tile = 1024
    at = first // count
    act = pl.BlockSpec((count, tile), lambda j: (at, j))
    shape = pltpu.HBM(gh.shape, BF)
    held = list(held)
    pieces = out_rows or [b.shape[0] for b in blocks]
    return call(
        functools.partial(expert_kernel, len(blocks), len(held)),
        (units // tile,),
        [pl.BlockSpec((dim, tile), lambda j: (0, j)), act]
        + [whole(b.shape) for b in blocks]
        + [pl.BlockSpec(memory_space=pltpu.HBM)] * len(held),
        [act, act] + [whole((n, dim)) for n in pieces],
        [shape, shape] + [jax.ShapeDtypeStruct((n, dim), BF) for n in pieces],
        scratch=[pltpu.VMEM((count, dim), BF), pltpu.VMEM((count, dim), F32)],
        aliases={2 + len(blocks) + i: i for i in range(len(held))},
        after=after,
        cost=cost,
    )(w_in, gh, *blocks, *held)


def turn_kernel(count, *refs):
    o_ref, joined_ref = refs[count:]
    fill(joined_ref, refs[:count])
    o_ref[...] = joined_ref[...].T


def turned(blocks, after=(), cost=0):
    total = sum(b.shape[0] for b in blocks)
    dim = blocks[0].shape[1]
    return call(
        functools.partial(turn_kernel, len(blocks)),
        (1,),
        [whole(b.shape) for b in blocks],
        whole((dim, total)),
        jax.ShapeDtypeStruct((dim, total), BF),
        scratch=[pltpu.VMEM((total, dim), BF)],
        after=after,
        cost=cost,
    )(*blocks)


def produced_kernel(h_ref, wo_ref, *refs):
    o_refs, total_ref = refs[:-1], refs[-1]
    step = pl.program_id(0)
    part = mm(h_ref[...], wo_ref[...])

    @pl.when(step == 0)
    def _():
        total_ref[...] = part

    @pl.when(step > 0)
    def _():
        total_ref[...] += part

    @pl.when(step == pl.num_programs(0) - 1)
    def _():
        at = 0
        for ref in o_refs:
            ref[...] = total_ref[at : at + ref.shape[0], :].astype(BF)
            at += ref.shape[0]


def make_produced(hidden, w_out, pieces, after=(), cost=0):
    rows, units = hidden.shape
    dim = w_out.shape[1]
    tile = 512
    return call(
        produced_kernel,
        (units // tile,),
        [pl.BlockSpec((rows, tile), lambda j: (0, j)), pl.BlockSpec((tile, dim), lambda j: (j, 0))],
        [whole((n, dim)) for n in pieces],
        [jax.ShapeDtypeStruct((n, dim), BF) for n in pieces],
        scratch=[pltpu.VMEM((rows, dim), F32)],
        after=after,
        cost=cost,
    )(hidden, w_out)


def halves_kernel(count, slots, *refs):
    o_ref = refs[-1]
    for i in range(count):
        o_ref[i * slots : (i + 1) * slots, :] = refs[i][...]


def second_halves(blocks, slots, after=(), cost=0):
    dim = blocks[0].shape[1]
    count = len(blocks)
    return call(
        functools.partial(halves_kernel, count, slots),
        (1,),
        [pl.BlockSpec((slots, dim), lambda i: (1, 0))] * count,
        whole((count * slots, dim)),
        jax.ShapeDtypeStruct((count * slots, dim), BF),
        after=after,
        cost=cost,
    )(*blocks)


def add_kernel(*refs):
    o_ref = refs[-1]
    rows = refs[0].shape[1]
    for i in range(o_ref.shape[0]):
        o_ref[i, :rows, :] = (refs[2 * i][0].astype(F32) + refs[2 * i + 1][0].astype(F32)).astype(BF)
        o_ref[i, rows:, :] = jnp.zeros((o_ref.shape[1] - rows, o_ref.shape[2]), BF)


def add_second(pairs, after=(), cost=0):
    _, rows, cols = pairs[0][0].shape
    steps = rows // TILE
    each = TILE + SPARE
    block = pl.BlockSpec((1, TILE, cols), lambda i: (1, i, 0))
    return call(
        add_kernel,
        (steps,),
        [block] * (2 * len(pairs)),
        pl.BlockSpec((len(pairs), each, cols), lambda i: (0, i, 0)),
        jax.ShapeDtypeStruct((len(pairs), steps * each, cols), BF),
        after=after,
        cost=cost,
    )(*[a for pair in pairs for a in pair])


def stack_kernel(a_ref, b_ref, o_ref):
    o_ref[0:1, :] = a_ref[0:1, :]
    o_ref[1:2, :] = b_ref[0:1, :]
    o_ref[2:3, :] = a_ref[1:2, :]
    o_ref[3:4, :] = b_ref[1:2, :]


def stack_sums(first, second, after=(), cost=0):
    _, dim = first.shape
    return call(
        stack_kernel,
        (1,),
        [whole(first.shape), whole(second.shape)],
        whole((4, dim)),
        jax.ShapeDtypeStruct((4, dim), F32),
        after=after,
        cost=cost,
    )(first, second)


def weights_kernel(count, puts, table_ref, l_ref, r_ref, *refs):
    half = l_ref.shape[0] // 2
    outs = refs[count:]

    for step, (first, last) in enumerate(puts):

        @pl.when(pl.program_id(0) == step)
        def _(first=first, last=last):
            outs[first][0] = mm(l_ref[:half, :], r_ref[...]).astype(BF)
            outs[last][0] = mm(l_ref[half:, :], r_ref[...]).astype(BF)


def weight_parts(left, right, table, count=4, held=(), after=(), cost=0):
    dim, depth = left.shape
    quarter = right.shape[1] // 4
    half = pltpu.HBM((2, dim // 2, quarter), BF)
    held = list(held)

    def part(until):
        return pl.BlockSpec((1, dim // 2, quarter), lambda i, t: (jnp.where(i <= until, 1, 0), 0, 0))

    if held:
        puts, specs = [(0, 1)], [part(-1), part(-1)]
    else:
        puts, specs = [(0, 1), (0, 3), (2, 1), (2, 3)][:count], [part(0), part(1), part(2), part(2)]
    steps = len(puts)
    return call(
        functools.partial(weights_kernel, len(held), puts),
        (steps,),
        [whole(left.shape), pl.BlockSpec((depth, quarter), lambda i, t: (0, t[i + (3 if held else 0)]))]
        + [pl.BlockSpec(memory_space=pltpu.HBM)] * len(held),
        specs,
        [half] * len(specs),
        prefetch=1,
        aliases={3 + i: i for i in range(len(held))},
        after=after,
        cost=cost,
    )(table, left, right, *held)


def joint_kernel(bit_ref, g_ref, ga_ref, n_ref, h_ref, *out_refs):
    low = bit_ref[0] == 0
    for side in range(2):
        keep_ref, send_ref = out_refs[2 * side : 2 * side + 2]
        own = 2 * keep_ref.shape[0]
        cols = keep_ref.shape[2]
        at = slice(side * cols, (side + 1) * cols)
        qkv_part = mm(g_ref[...], n_ref[:, at]).reshape(own, g_ref.shape[0] // own, cols)
        out_part = mm(ga_ref[...], h_ref[:, at]).reshape(own, ga_ref.shape[0] // own, cols)
        both = jnp.concatenate([qkv_part, out_part], axis=1).astype(BF)
        both = both.reshape(own // 2, 2, *both.shape[1:])
        keep_ref[...] = jnp.where(low, both[:, 0], both[:, 1])
        send_ref[...] = jnp.where(low, both[:, 1], both[:, 0])


def joint(grads_t, grad_attn_t, normed, mixed_heads, bit, owners, after=(), cost=0):
    rows, dim = normed.shape
    steps = 8
    cols = dim // 2
    own = owners // steps
    qkv_rows = grads_t.shape[0] // steps
    out_rows = grad_attn_t.shape[0] // steps
    each = (qkv_rows + out_rows) // own
    block = pl.BlockSpec((own // 2, each, cols), lambda i, _: (i, 0, 0))
    return call(
        joint_kernel,
        (steps,),
        [
            pl.BlockSpec((qkv_rows, rows), lambda i, _: (i, 0)),
            pl.BlockSpec((out_rows, rows), lambda i, _: (i, 0)),
            whole((rows, dim)),
            whole((rows, dim)),
        ],
        [block] * 4,
        [jax.ShapeDtypeStruct((owners // 2, each, cols), BF)] * 4,
        prefetch=1,
        after=after,
        cost=cost,
    )(bit, grads_t, grad_attn_t, normed, mixed_heads)


def add_split_kernel(parts, _, *refs):
    keep_ref, send_ref = refs[4 * parts :]
    cols = refs[0].shape[2]
    for i in range(parts):
        mine_keep, got_keep, mine_send, got_send = refs[4 * i : 4 * i + 4]
        at = slice(i * cols, (i + 1) * cols)
        keep_ref[:, :, at] = (mine_keep[...].astype(F32) + got_keep[...].astype(F32)).astype(BF)
        send_ref[:, :, at] = (mine_send[...].astype(F32) + got_send[...].astype(F32)).astype(BF)


def add_split(pairs, bit, inner, after=(), cost=0):
    count, rows, cols = pairs[0][0].shape
    parts = len(pairs)
    outer = count // (2 * inner)
    each = min(inner, 2)
    steps = inner // each
    block = (each, rows, cols)
    keep = pl.BlockSpec(block, lambda i, j, b: ((2 * i + b[0]) * steps + j, 0, 0))
    send = pl.BlockSpec(block, lambda i, j, b: ((2 * i + 1 - b[0]) * steps + j, 0, 0))
    out = pl.BlockSpec((each, rows, parts * cols), lambda i, j, b: (i * steps + j, 0, 0))
    return call(
        functools.partial(add_split_kernel, parts),
        (outer, steps),
        [keep, keep, send, send] * parts,
        [out, out],
        [jax.ShapeDtypeStruct((count // 2, rows, parts * cols), BF)] * 2,
        prefetch=1,
        after=after,
        cost=cost,
    )(bit, *[a for mine, got in pairs for a in (mine, got, mine, got)])


def add_rows_kernel(count, *refs):
    total = refs[0][...]
    for i in range(1, count):
        total += refs[i][...]
    refs[count][...] = total


def add_rows(values, after=(), cost=0):
    shape = values[0].shape
    return call(
        functools.partial(add_rows_kernel, len(values)),
        (1,),
        [whole(shape)] * len(values),
        whole(shape),
        jax.ShapeDtypeStruct(shape, F32),
        after=after,
        cost=cost,
    )(*values)


def finish_kernel(turn, *refs):
    o_ref = refs[-1]
    rows = refs[0].shape[1]
    total = refs[0][0].astype(F32) + refs[1][0].astype(F32) + refs[2][0, :rows].astype(F32)
    o_ref[...] = total.T if turn else total


def finish(keep, got, last, which, turn, side, held=None, after=(), cost=0):
    _, rows, cols = keep.shape
    tile = TILE
    block = pl.BlockSpec((1, tile, cols), lambda i: (0, i, 0))
    steps = rows // tile
    shape = (cols, 2 * rows) if turn else (2 * rows, cols)
    out = (
        pl.BlockSpec((cols, tile), lambda i: (0, side * steps + i))
        if turn
        else pl.BlockSpec((tile, cols), lambda i: (side * steps + i, 0))
    )
    more = [] if held is None else [held]
    count = len(more)

    def body(*refs):
        finish_kernel(turn, *refs[:3], refs[3 + count])

    return call(
        body,
        (steps,),
        [block] * 2
        + [pl.BlockSpec((1, tile + SPARE, cols), lambda i: (which, i, 0))]
        + [pl.BlockSpec(memory_space=pltpu.HBM)] * count,
        out,
        pltpu.HBM(shape, F32),
        aliases={3: 0} if more else None,
        after=after,
        cost=cost,
    )(keep, got, last, *more)


def swap(value, axis, mask):
    size = lax.axis_size(axis)
    return lax.ppermute(value, axis, [(i, i ^ mask) for i in range(size)])


def bit_of(axis, mask):
    return jnp.where((lax.axis_index(axis) & mask) > 0, 1, 0).astype(jnp.int32).reshape(1)


def bits_of(size):
    return [1 << i for i in range(size.bit_length() - 1)]


def on_device(
    tokens,
    norm_gains,
    norm_biases,
    w_qkv,
    w_attn_out,
    w_in,
    w_out,
    segment_ids,
    expert_ids,
    slots,
    cotangent,
):
    ORDER.clear()
    tok, dim = tokens.shape
    head_dim = dim // HEADS
    wide = lax.axis_size("wide")
    narrow = lax.axis_size("narrow")
    units = w_in.shape[2]
    me_wide = lax.axis_index("wide")
    me_narrow = lax.axis_index("narrow")
    capacity = tok * 9 // (8 * wide)
    w_in = w_in[0]
    w_out = w_out[0]
    zs = wide // 2
    slots_all = zs * capacity
    groups = [list(range(zs // 2)), list(range(zs // 2, 3 * zs // 4)), list(range(3 * zs // 4, zs))]
    apart = capacity % 16 == 0

    def joinable(blocks):
        return blocks if apart else [jnp.concatenate(blocks, axis=0)]

    def by_position(pieces):
        return list(pieces) if apart else [q for p in pieces for q in jnp.split(p, p.shape[0] // (2 * capacity))]

    def piece_rows(group):
        return [2 * capacity] * len(group) if apart else [2 * capacity * len(group)]

    away = expert_ids ^ me_wide
    kept = slots < capacity
    base = (away >> 1) * capacity + slots
    core = away & 1
    nowhere = 2 * slots_all
    place_own = jnp.where(kept & (core == 0), base, nowhere).astype(jnp.int32)[None, :]
    place_sent = jnp.where(kept & (core == 1), base, nowhere).astype(jnp.int32)[None, :]
    places = [place_own, swap(place_sent, "wide", 1)]
    place_col = jnp.where(kept, core * slots_all + base, nowhere).astype(jnp.int32)[:, None]
    doc_col = segment_ids.reshape(tok, 1)

    def exchange(blocks, positions):
        return [swap(blocks[z], "wide", 2 * z) if z else blocks[z] for z in positions]

    def bring_back(blocks, cost=0):
        if not apart:
            theirs = jnp.concatenate([b[capacity:] for b in blocks], axis=0)
            own = [(jnp.concatenate([b[:capacity] for b in blocks], axis=0), slots_all)]
        else:
            theirs = second_halves(blocks, capacity, cost=cost)
            own = [(b, capacity) for b in blocks]
        return own + [(swap(theirs, "wide", 1), slots_all)]

    cotangent_other = swap(cotangent, "wide", 1)
    normed = first_norm(tokens, norm_gains, norm_biases)
    sent_grads = dispatch_rows(places, [cotangent, cotangent_other], zs, capacity)
    expert_grads = exchange(separate(sent_grads, zs, capacity), range(zs))

    projected = project(normed, w_qkv)
    mixed_heads, mixed_low, log_total = attn_fwd(projected, doc_col, head_dim)
    many = tok - LAST_ROWS
    middle_of = functools.partial(make_middle, tokens, mixed_heads, w_attn_out, norm_gains, norm_biases)
    middle, sent_first = middle_of(0, many)
    other_first = swap(sent_first, "wide", 1)
    middle, sent_last = middle_of(many, LAST_ROWS, [middle], after=expert_grads, cost=COST_MIDDLE)
    other_last = swap(sent_last, "wide", 1)
    sent_rows = dispatch_rows([p[:, :many] for p in places], [sent_first, other_first], zs, capacity)
    sent_rows = dispatch_rows([p[:, many:] for p in places], [sent_last, other_last], zs, capacity, sent_rows)
    expert_rows = exchange(separate(sent_rows, zs, capacity), range(zs))

    gh, grads_t = grad_hidden(joinable(expert_grads), w_out)
    held = ()
    back_grads = []
    for group in groups:
        blocks = joinable([expert_rows[z] for z in group])
        outs = expert(blocks, gh, w_in, 2 * group[0] * capacity, held, piece_rows(group))
        held = outs[:2]
        pieces = by_position(outs[2:])
        back_grads += exchange({z: pieces[i] for i, z in enumerate(group)}, group)
    hidden, grad_preact = held

    masks = [(1, 2), (2, 1)]
    sides = range(2)
    table = jnp.array([3, 1, 2, 0], jnp.int32) ^ me_narrow

    def first_step(send):
        return [swap(send[side], "narrow", masks[side][0]) for side in sides]

    send_a, send_b, *keep_out = weight_parts(grads_t, hidden, table, 3)
    got_out = first_step([send_a, send_b])
    keep_out = weight_parts(grads_t, hidden, table, 1, keep_out)
    produced = make_produced(hidden, w_out, piece_rows(range(zs)))
    back_rows = exchange(by_position(produced), range(zs))
    rows_t = turned(joinable(expert_rows))
    send_a, send_b, *keep_in = weight_parts(rows_t, grad_preact, table)
    got_in = first_step([send_a, send_b])
    back_grads = bring_back(back_grads, COST_GATE)
    grad_middle, grad_attn_t, grad_heads, sums_two = second_back(
        place_col, middle, cotangent, back_grads, w_attn_out, norm_gains, after=got_out
    )
    attn = functools.partial(
        attn_bwd, projected, mixed_heads, mixed_low, grad_heads, log_total, doc_col, head_dim
    )
    pairs = dim // 128
    held = attn(0, PAIRS_FIRST)
    again = [add_second([(keep_out[side], got_out[side]), (keep_in[side], got_in[side])]) for side in sides]
    last = [swap(again[side], "narrow", masks[side][1]) for side in sides]
    grads, grads_all_t = attn(PAIRS_FIRST, pairs - PAIRS_FIRST, held)
    back_rows = bring_back(back_rows)
    grads_all_t = grads_all_t.reshape(3 * dim, tok)

    owners = narrow * wide
    own_qkv = 3 * dim // owners
    n_bits = bits_of(narrow)
    w_bits = bits_of(wide)
    names = [("narrow", b) for b in reversed(n_bits)] + [("wide", b) for b in reversed(w_bits)]
    core_bit = ("wide", 1)
    near = ("wide", w_bits[1])
    orders = [[near, ("narrow", 1), ("narrow", 2)], [("narrow", 1), ("narrow", 2), near]]
    bits = {name: bit_of(*name) for name in names}
    kept_a, sent_a, kept_b, sent_b = joint(
        grads_all_t, grad_attn_t, normed, mixed_heads, bits[core_bit], owners
    )
    got_a, got_b = [swap(sent, *core_bit) for sent in (sent_a, sent_b)]
    state = [(kept_a, got_a, names[:-1]), (kept_b, got_b, names[:-1])]

    def one_step(number):
        for side in sides:
            kept, got, left = state[side]
            step = orders[side][number]
            at = left.index(step)
            kept, sent = add_split([(kept, got)], bits[step], 1 << (len(left) - 1 - at))
            state[side] = (kept, swap(sent, *step), left[:at] + left[at + 1 :])

    rounds = [("narrow", n_bits)] + [("wide", w_bits[i : i + 2]) for i in range(0, len(w_bits), 2)]

    def send_sums(number):
        axis, some = rounds[number]
        others = sorted({sum(c) for c in itertools.product(*[(0, b) for b in some])} - {0})
        return [swap(sums, axis, m) for m in others]

    d_tokens, sums_one = first_back(tokens, grad_middle, grads, w_qkv, norm_gains)
    one_step(0)
    sums = stack_sums(sums_one, sums_two, after=last)
    sums_got = send_sums(0)
    mixed = make_mixed(place_col, middle, back_rows, cost=12)
    sums = add_rows([sums, *sums_got])
    one_step(1)
    sums_got = send_sums(1)
    d_w_out = finish(keep_out[0], got_out[0], last[0], 0, True, 0)
    d_w_out = finish(keep_out[1], got_out[1], last[1], 0, True, 1, d_w_out)
    sums = add_rows([sums, *sums_got])
    one_step(2)
    for number in range(2, len(rounds)):
        sums_got = send_sums(number)
        if number == 2:
            d_w_in = finish(keep_in[0], got_in[0], last[0], 1, False, 0)
            d_w_in = finish(keep_in[1], got_in[1], last[1], 1, False, 1, d_w_in)
        sums = add_rows([sums, *sums_got])
    pairs = [state[side][:2] for side in sides]
    left = state[0][2]
    for step in [("wide", b) for b in w_bits[2:]]:
        at = left.index(step)
        kept, sent = add_split(pairs, bits[step], 1 << (len(left) - 1 - at))
        pairs = [(kept, swap(sent, *step))]
        left = left[:at] + left[at + 1 :]
    value = pairs[0][0][0].astype(F32) + pairs[0][1][0].astype(F32)
    d_w_qkv = value[:own_qkv].T
    d_w_attn_out = value[own_qkv:].T
    own = dim // owners
    sums = lax.dynamic_slice_in_dim(sums, (me_narrow * wide + me_wide) * own, own, 1)
    return (mixed, d_tokens, sums[:2], sums[2:], d_w_qkv, d_w_attn_out, d_w_in[None], d_w_out[None])


def solution(mesh):
    placed = (
        P(("narrow", "wide"), None),
        P(),
        P(),
        P(),
        P(),
        P("wide", None, None),
        P("wide", None, None),
        P(("narrow", "wide"), None),
        P(("narrow", "wide")),
        P(("narrow", "wide")),
        P(("narrow", "wide"), None),
    )
    return jax.shard_map(
        on_device,
        mesh=mesh,
        in_specs=placed,
        out_specs=(
            P(("narrow", "wide"), None),
            P(("narrow", "wide"), None),
            P(None, ("narrow", "wide")),
            P(None, ("narrow", "wide")),
            P(None, ("narrow", "wide")),
            P(None, ("narrow", "wide")),
            P("wide", None, "narrow"),
            P("wide", "narrow", None),
        ),
        check_vma=False,
    )
```

```python
import functools
import itertools

import jax
import jax.numpy as jnp
from jax import lax
from jax.experimental import pallas as pl
from jax.experimental.pallas import tpu as pltpu
from jax.sharding import PartitionSpec as P

HEADS = 16
EPSILON = 1e-05
NEGATIVE = -1e30
BAND = 512
BLOCK = 256
SUB = 512
TILE = 256
SPARE = 16
PARTS = 3
F32 = jnp.float32
BF = jnp.bfloat16
LAST_ROWS = 128
COST_GATE = 6
COST_MIDDLE = 25
PAIRS_FIRST = 4
VMEM_BYTES = 48 * 1024 * 1024


def mm(a, b):
    return lax.dot_general(a, b, (((1,), (0,)), ((), ())), preferred_element_type=F32)


def mm_nt(a, b):
    return lax.dot_general(a, b, (((1,), (1,)), ((), ())), preferred_element_type=F32)


def mm_tn(a, b):
    return lax.dot_general(a, b, (((0,), (0,)), ((), ())), preferred_element_type=F32)


ORDER = []


def call(kernel, grid, in_specs, out_specs, out_shape, scratch=(), prefetch=0, aliases=None, after=(), cost=0):
    count = prefetch + len(in_specs)
    extra = len(after) + len(ORDER)
    order = list(ORDER)
    several = isinstance(out_specs, list)
    outs = len(out_specs) if several else 1

    def body(*refs):
        rest = refs[count + extra :]
        kernel(*refs[:count], *rest[:outs], *rest[outs + 1 :])
        rest[outs][...] = jnp.zeros_like(rest[outs])

    run = pl.pallas_call(
        body,
        grid_spec=pltpu.PrefetchScalarGridSpec(
            num_scalar_prefetch=prefetch,
            grid=grid,
            in_specs=list(in_specs)
            + [pl.BlockSpec(memory_space=pltpu.HBM)] * len(after)
            + [pl.BlockSpec(memory_space=pl.ANY)] * len(ORDER),
            out_specs=[*(out_specs if several else [out_specs]), whole((8, 128))],
            scratch_shapes=list(scratch),
        ),
        out_shape=[*(out_shape if several else [out_shape]), jax.ShapeDtypeStruct((8, 128), F32)],
        input_output_aliases=aliases or {},
        compiler_params=pltpu.CompilerParams(vmem_limit_bytes=VMEM_BYTES),
        cost_estimate=pl.CostEstimate(flops=1 + int(cost * 1.15e9), bytes_accessed=0, transcendentals=0),
    )

    def apply(*args):
        *results, token = run(*args, *[far(a) for a in after], *order)
        ORDER[:] = [token]
        return results if several else results[0]

    return apply


def far(value):
    return pltpu.with_memory_space_constraint(value, pltpu.HBM)


def whole(shape):
    return pl.BlockSpec(shape, lambda *_: (0,) * len(shape))


def normalize(stream):
    average = jnp.mean(stream, axis=-1, keepdims=True)
    centered = stream - average
    inverse = lax.rsqrt(jnp.mean(centered * centered, axis=-1, keepdims=True) + EPSILON)
    return centered * inverse, inverse


def norm_back(unit, inverse, gain, grad):
    scaled = grad * gain
    first = jnp.mean(scaled, axis=-1, keepdims=True)
    second = jnp.mean(scaled * unit, axis=-1, keepdims=True)
    return inverse * (scaled - first - unit * second)


def first_norm_kernel(x_ref, g_ref, b_ref, n_ref):
    unit, _inverse = normalize(x_ref[...].astype(F32))
    n_ref[...] = (unit * g_ref[0:1, :] + b_ref[0:1, :]).astype(BF)


def first_norm(tokens, gains, biases, after=(), cost=0):
    rows, dim = tokens.shape
    block = pl.BlockSpec((256, dim), lambda i: (i, 0))
    return call(
        first_norm_kernel,
        (rows // 256,),
        [block, whole(gains.shape), whole(biases.shape)],
        block,
        pltpu.HBM((rows, dim), BF),
        after=after,
        cost=cost,
    )(far(tokens), far(gains), far(biases))


def project_kernel(n_ref, w_ref, p_ref):
    p_ref[...] = mm(n_ref[...], w_ref[...]).astype(BF)


def project(normed, w_qkv, after=(), cost=0):
    rows, dim = normed.shape
    cols = w_qkv.shape[1]
    tile = 768
    return call(
        project_kernel,
        (cols // tile,),
        [whole((rows, dim)), pl.BlockSpec((dim, tile), lambda j: (0, j))],
        pl.BlockSpec((rows, tile), lambda j: (0, j)),
        jax.ShapeDtypeStruct((rows, cols), BF),
        after=after,
        cost=cost,
    )(far(normed), far(w_qkv))


def fill_masks(col_ref, fq_ref, fk_ref, tri_ref, head_dim):
    length = col_ref.shape[0]
    doc = lax.broadcasted_iota(jnp.int32, fq_ref.shape, 1) % head_dim
    same = doc == col_ref[...]
    fq_ref[...] = jnp.where(same, 1.0, 0.0).astype(BF)
    fk_ref[...] = jnp.where(same, 0.0, NEGATIVE).astype(BF)
    key_pos = lax.broadcasted_iota(jnp.int32, tri_ref.shape, 0)
    query_pos = lax.broadcasted_iota(jnp.int32, tri_ref.shape, 1)
    tri_ref[...] = jnp.where(key_pos <= query_pos, 0.0, NEGATIVE).astype(F32)


def lanes_of(shape, head, head_dim):
    lane = lax.broadcasted_iota(jnp.int32, shape, 1)
    return (lane >= head * head_dim) & (lane < (head + 1) * head_dim)


def attn_fwd_kernel(head_dim, col_ref, q_ref, k_ref, v_ref, o_ref, ol_ref, lse_ref, fq_ref, fk_ref, tri_ref, vt_ref, qh_ref, kh_ref):
    length, pair = q_ref.shape
    scale = head_dim**-0.5
    per = pair // head_dim

    @pl.when(pl.program_id(0) == 0)
    def _():
        fill_masks(col_ref, fq_ref, fk_ref, tri_ref, head_dim)
        vt_ref[...] = jnp.ones_like(vt_ref)

    value_t = v_ref[...].T
    query = q_ref[...] * BF(scale)
    for head in range(per):
        inside = lanes_of(query.shape, head, head_dim)
        vt_ref[head, :head_dim, :] = value_t[head * head_dim : (head + 1) * head_dim, :]
        qh_ref[head] = jnp.where(inside, query, fq_ref[...])
        kh_ref[head] = jnp.where(inside, k_ref[...], fk_ref[...])
    def first_stage(q_first):
        k_first = max(0, q_first - BAND)
        allparts = [[] for _ in range(per)]
        for k_at in range(k_first, q_first + BLOCK, BLOCK):
            for head in range(per):
                scores = mm_nt(kh_ref[head, k_at : k_at + BLOCK, :], qh_ref[head, q_first : q_first + BLOCK, :])
                if k_at == q_first:
                    scores = scores + tri_ref[...]
                allparts[head].append(scores)
        tops = [functools.reduce(jnp.maximum, [jnp.max(p, axis=0, keepdims=True) for p in parts]) for parts in allparts]
        return allparts, tops

    def second_stage(q_first, allparts, tops):
        k_first = max(0, q_first - BAND)
        q_at = slice(q_first, q_first + BLOCK)
        totals = [None] * per
        for i in range(len(allparts[0])):
            k_at = k_first + i * BLOCK
            for head in range(per):
                prob = jnp.exp(allparts[head][i] - tops[head]).astype(BF)
                part = mm(vt_ref[head, :, k_at : k_at + BLOCK], prob)
                totals[head] = part if totals[head] is None else totals[head] + part
        outs = []
        for head in range(per):
            total = totals[head]
            sums = total[head_dim : head_dim + 1, :]
            outs.append(total[:head_dim, :] / sums)
            lse_ref[0, head : head + 1, q_at] = tops[head] + jnp.log(sums)
        o_ref[q_at, :], ol_ref[q_at, :] = in_parts(jnp.concatenate(outs, axis=0).T, 2)

    firsts = list(range(0, length, BLOCK))
    ahead = first_stage(firsts[0])
    for i, q_first in enumerate(firsts):
        now = ahead
        if i + 1 < len(firsts):
            ahead = first_stage(firsts[i + 1])
        second_stage(q_first, *now)


def attn_fwd(projected, doc_col, head_dim, cost=0):
    length = projected.shape[0]
    width = projected.shape[1] // 3
    pair = 128
    pairs = width // pair
    per = pair // head_dim
    specs = [pl.BlockSpec((length, pair), functools.partial(lambda s, j: (0, s * pairs + j), s)) for s in range(3)]
    return call(
        functools.partial(attn_fwd_kernel, head_dim),
        (pairs,),
        [whole(doc_col.shape)] + specs,
        [pl.BlockSpec((length, pair), lambda j: (0, j))] * 2 + [pl.BlockSpec((1, per, length), lambda j: (j, 0, 0))],
        [
            jax.ShapeDtypeStruct((length, width), BF),
            pltpu.HBM((length, width), BF),
            pltpu.HBM((pairs, per, length), F32),
        ],
        scratch=[
            pltpu.VMEM((length, pair), BF),
            pltpu.VMEM((length, pair), BF),
            pltpu.VMEM((BLOCK, BLOCK), F32),
            pltpu.VMEM((per, head_dim + 16, length), BF),
            pltpu.VMEM((per, length, pair), BF),
            pltpu.VMEM((per, length, pair), BF),
        ],
        cost=cost,
    )(doc_col, projected, projected, projected)


def in_parts(x, count):
    parts = []
    for _ in range(count):
        parts.append(x.astype(BF))
        x = x - parts[-1].astype(F32)
    return parts


def attn_bwd_kernel(head_dim, col_ref, q_ref, k_ref, v_ref, o_ref, ol_ref, do_ref, lse_ref, g_ref, gt_ref,
                    fq_ref, fk_ref, tri_ref, qx, kx, vx, dox, qm, dom, dk_sum, dv_sum):
    length, pair = q_ref.shape
    scale = head_dim**-0.5
    per = pair // head_dim

    @pl.when(pl.program_id(0) == 0)
    def _():
        fill_masks(col_ref, fq_ref, fk_ref, tri_ref, head_dim)

    key_t = (k_ref[...] * BF(scale)).T
    query = q_ref[...] * BF(scale)
    grad = do_ref[...]
    lane = lax.broadcasted_iota(jnp.int32, (length, pair), 1)
    zero = jnp.zeros_like(query)
    one = jnp.ones_like(query)
    lse_rows = jnp.concatenate([lse_ref[0], jnp.zeros((8 - per, length), F32)], axis=0)
    lse_cols = lse_rows.T
    product = grad.astype(F32) * (o_ref[...].astype(F32) + ol_ref[...].astype(F32))
    for head in range(per):
        inside = lanes_of(query.shape, head, head_dim)
        slots = [lane == (1 - head) * head_dim + head_dim // 2 + i for i in range(PARTS)]
        some = functools.reduce(jnp.logical_or, slots)
        delta = jnp.sum(jnp.where(inside, product, 0.0), axis=1, keepdims=True)

        def spread(column, rest):
            for slot, part in zip(slots, in_parts(-column, PARTS)):
                rest = jnp.where(slot, part, rest)
            return rest

        qm[head] = jnp.where(inside, query, zero)
        dom[head] = jnp.where(inside, grad, zero)
        qx[head] = jnp.where(inside, query, spread(lse_cols[:, head : head + 1], fq_ref[...]))
        kx[head] = jnp.where(inside, k_ref[...], jnp.where(some, one, fk_ref[...]))
        vx[head] = jnp.where(inside, v_ref[...], jnp.where(some, one, zero))
        dox[head] = jnp.where(inside, grad, spread(delta, zero))
    dk_sum[...] = jnp.zeros_like(dk_sum)
    dv_sum[...] = jnp.zeros_like(dv_sum)
    for q_first in range(0, length, BLOCK):
        q_at = slice(q_first, q_first + BLOCK)
        dq_parts = [None] * per
        for k_first in range(max(0, q_first - BAND), q_first + BLOCK, BLOCK):
            k_at = slice(k_first, k_first + BLOCK)
            scores = [mm_nt(kx[h, k_at, :], qx[h, q_at, :]) for h in range(per)]
            prob_grads = [mm_nt(vx[h, k_at, :], dox[h, q_at, :]) for h in range(per)]
            if k_first == q_first:
                scores = [s + tri_ref[...] for s in scores]
            probs = [jnp.exp(s) for s in scores]
            score_grads = [(p * d).astype(BF) for p, d in zip(probs, prob_grads)]
            probs = [p.astype(BF) for p in probs]
            dv_sum[k_at, :] += mm(
                jnp.concatenate(probs, axis=1), jnp.concatenate([dom[h, q_at, :] for h in range(per)], axis=0)
            )
            dk_sum[k_at, :] += mm(
                jnp.concatenate(score_grads, axis=1), jnp.concatenate([qm[h, q_at, :] for h in range(per)], axis=0)
            )
            for h in range(per):
                one = mm(key_t[h * head_dim : (h + 1) * head_dim, k_at], score_grads[h])
                dq_parts[h] = one if dq_parts[h] is None else dq_parts[h] + one
        dq_t = jnp.concatenate(dq_parts, axis=0)
        gt_ref[0, :, q_at] = dq_t.astype(BF)
        g_ref[0, q_at, :] = dq_t.T.astype(BF)
    for i, ref in ((1, dk_sum), (2, dv_sum)):
        low = ref[...].astype(BF)
        g_ref[i] = low
        gt_ref[i] = low.T


def attn_bwd(projected, mixed_heads, mixed_low, grad_heads, log_total, doc_col, head_dim, first, steps, held=(), after=(), cost=0):
    length = projected.shape[0]
    width = projected.shape[1] // 3
    pair = 128
    pairs = width // pair
    per = pair // head_dim
    specs = [
        pl.BlockSpec((length, pair), functools.partial(lambda s, j: (0, s * pairs + first + j), s)) for s in range(3)
    ]
    held = list(held)
    count = len(held)
    kernel = functools.partial(attn_bwd_kernel, head_dim)
    one = pl.BlockSpec((length, pair), lambda j: (0, first + j))
    return call(
        lambda *refs: kernel(*refs[:8], *refs[8 + count :]),
        (steps,),
        [whole(doc_col.shape)] + specs + [one, one, one, pl.BlockSpec((1, per, length), lambda j: (first + j, 0, 0))]
        + [pl.BlockSpec(memory_space=pltpu.HBM)] * count,
        [
            pl.BlockSpec((3, length, pair), lambda j: (0, 0, first + j)),
            pl.BlockSpec((3, pair, length), lambda j: (0, first + j, 0)),
        ],
        [pltpu.HBM((3, length, width), BF), pltpu.HBM((3, width, length), BF)],
        scratch=[
            pltpu.VMEM((length, pair), BF),
            pltpu.VMEM((length, pair), BF),
            pltpu.VMEM((BLOCK, BLOCK), F32),
        ]
        + [pltpu.VMEM((per, length, pair), BF)] * 6
        + [pltpu.VMEM((length, pair), F32)] * 2,
        aliases={8 + i: i for i in range(count)},
        after=after,
        cost=cost,
    )(doc_col, *[far(a) for a in (projected, projected, projected, mixed_heads, mixed_low, grad_heads, log_total)], *held)


def middle_kernel(x_ref, h_ref, w_ref, g_ref, b_ref, *refs):
    m_ref, s_ref = refs[-2:]
    middle = x_ref[...].astype(F32) + mm(h_ref[...], w_ref[...])
    m_ref[...] = middle
    unit, _inverse = normalize(middle)
    s_ref[...] = (unit * g_ref[1:2, :] + b_ref[1:2, :]).astype(BF)


def make_middle(tokens, mixed_heads, w_attn_out, gains, biases, first, count, held=(), after=(), cost=0):
    rows, dim = tokens.shape
    tile = min(count, 448)
    at = first // tile
    block = pl.BlockSpec((tile, dim), lambda i: (at + i, 0))
    held = list(held)
    return call(
        middle_kernel,
        (count // tile,),
        [block, block, whole(w_attn_out.shape), whole(gains.shape), whole(biases.shape)]
        + [pl.BlockSpec(memory_space=pltpu.HBM)] * len(held),
        [block, pl.BlockSpec((tile, dim), lambda i: (i, 0))],
        [pltpu.HBM((rows, dim), F32), jax.ShapeDtypeStruct((count, dim), BF)],
        aliases={5: 0} if held else None,
        after=after,
        cost=cost,
    )(far(tokens), mixed_heads, far(w_attn_out), far(gains), far(biases), *held)


def dispatch_kernel(slots, added, *refs):
    o_refs = refs[4 + added :]
    count = slots * (o_refs[0].shape[0] // (2 * slots)) * len(o_refs)
    for side in range(2):
        place, rows = refs[side], refs[2 + side]
        slot = lax.broadcasted_iota(jnp.int32, (count, rows.shape[0]), 0)
        low = mm(jnp.where(slot == place[...], 1.0, 0.0).astype(BF), rows[...]).astype(BF)
        for i, ref in enumerate(o_refs):
            each = count // len(o_refs)
            at = slice(side * each, (side + 1) * each)
            part = low[i * each : (i + 1) * each]
            ref[at, :] = part + refs[4 + i][at, :] if added else part


def dispatch_rows(places, rows, positions, slots, added=(), after=(), cost=0):
    dim = rows[0].shape[1]
    count = positions if slots % 16 == 0 else 1
    shape = (2 * slots * (positions // count), dim)
    return call(
        functools.partial(dispatch_kernel, slots, len(added)),
        (1,),
        [whole(a.shape) for a in [*places, *rows]] + [whole(shape)] * len(added),
        [whole(shape)] * count,
        [jax.ShapeDtypeStruct(shape, BF)] * count,
        after=after,
        cost=cost,
    )(*places, *rows, *added)


def separate(out, positions, slots):
    if len(out) > 1:
        return out
    sides = out[0].reshape(2, positions, slots, out[0].shape[1])
    return [sides[:, p].reshape(2 * slots, out[0].shape[1]) for p in range(positions)]


def fill(joined_ref, block_refs):
    at = 0
    for ref in block_refs:
        joined_ref[at : at + ref.shape[0], :] = ref[...]
        at += ref.shape[0]


def pick_rows(place, back):
    slot = lax.broadcasted_iota(jnp.int32, (place.shape[0], back.shape[0]), 1)
    return mm(jnp.where(slot == place, 1.0, 0.0).astype(BF), back)


def mixed_kernel(count, place_ref, m_ref, *refs):
    o_ref, joined_ref = refs[count:]

    @pl.when(pl.program_id(0) == 0)
    def _():
        fill(joined_ref, refs[:count])

    o_ref[...] = (m_ref[...] + pick_rows(place_ref[...], joined_ref[...])).astype(BF)


def make_mixed(place_col, middle, back, after=(), cost=0):
    rows, dim = middle.shape
    tile = 256
    total = sum(n for _, n in back)
    block = pl.BlockSpec((tile, dim), lambda i: (i, 0))
    return call(
        functools.partial(mixed_kernel, len(back)),
        (rows // tile,),
        [pl.BlockSpec((tile, 1), lambda i: (i, 0)), block] + [whole((n, dim)) for _, n in back],
        block,
        jax.ShapeDtypeStruct((rows, dim), BF),
        scratch=[pltpu.VMEM((total, dim), BF)],
        after=after,
        cost=cost,
    )(place_col, far(middle), *[far(b) for b, _ in back])


def second_back_kernel(count, place_ref, m_ref, c_ref, w_ref, g_ref, *refs):
    gm_ref, gat_ref, gh_ref, sums_ref, joined_ref = refs[count:]

    @pl.when(pl.program_id(0) == 0)
    def _():
        fill(joined_ref, refs[:count])

    grad_sent = pick_rows(place_ref[...], joined_ref[...])
    unit, inverse = normalize(m_ref[...])
    grad_middle = c_ref[...].astype(F32) + norm_back(unit, inverse, g_ref[1:2, :], grad_sent)
    gm_ref[...] = grad_middle
    grad_attn = grad_middle.astype(BF)
    gat_ref[...] = grad_attn.T
    gh_ref[...] = mm_nt(grad_attn, w_ref[...]).astype(BF)
    sums = jnp.concatenate(
        [jnp.sum(grad_sent * unit, axis=0, keepdims=True), jnp.sum(grad_sent, axis=0, keepdims=True)], axis=0
    )

    @pl.when(pl.program_id(0) == 0)
    def _():
        sums_ref[...] = sums

    @pl.when(pl.program_id(0) > 0)
    def _():
        sums_ref[...] += sums


def second_back(place_col, middle, cotangent, back, w_attn_out, gains, after=(), cost=0):
    rows, dim = middle.shape
    tile = 256
    total = sum(n for _, n in back)
    block = pl.BlockSpec((tile, dim), lambda i: (i, 0))
    return call(
        functools.partial(second_back_kernel, len(back)),
        (rows // tile,),
        [pl.BlockSpec((tile, 1), lambda i: (i, 0)), block, block, whole(w_attn_out.shape), whole(gains.shape)]
        + [whole((n, dim)) for _, n in back],
        [block, pl.BlockSpec((dim, tile), lambda i: (0, i)), block, whole((2, dim))],
        [
            pltpu.HBM((rows, dim), F32),
            pltpu.HBM((dim, rows), BF),
            pltpu.HBM((rows, dim), BF),
            jax.ShapeDtypeStruct((2, dim), F32),
        ],
        scratch=[pltpu.VMEM((total, dim), BF)],
        after=after,
        cost=cost,
    )(place_col, far(middle), far(cotangent), far(w_attn_out), far(gains), *[far(b) for b, _ in back])


def first_back_kernel(x_ref, gm_ref, d_ref, w_ref, g_ref, dx_ref, sums_ref):
    dim = x_ref.shape[1]
    grad_normed = mm_nt(d_ref[0], w_ref[:, :dim])
    grad_normed += mm_nt(d_ref[1], w_ref[:, dim : 2 * dim])
    grad_normed += mm_nt(d_ref[2], w_ref[:, 2 * dim :])
    unit, inverse = normalize(x_ref[...].astype(F32))
    dx_ref[...] = gm_ref[...] + norm_back(unit, inverse, g_ref[0:1, :], grad_normed)
    sums = jnp.concatenate(
        [jnp.sum(grad_normed * unit, axis=0, keepdims=True), jnp.sum(grad_normed, axis=0, keepdims=True)], axis=0
    )

    @pl.when(pl.program_id(0) == 0)
    def _():
        sums_ref[...] = sums

    @pl.when(pl.program_id(0) > 0)
    def _():
        sums_ref[...] += sums


def first_back(tokens, grad_middle, grads, w_qkv, gains, after=(), cost=0):
    rows, dim = tokens.shape
    tile = 256
    block = pl.BlockSpec((tile, dim), lambda i: (i, 0))
    return call(
        first_back_kernel,
        (rows // tile,),
        [
            block,
            block,
            pl.BlockSpec((3, tile, dim), lambda i: (0, i, 0)),
            whole(w_qkv.shape),
            whole(gains.shape),
        ],
        [block, whole((2, dim))],
        [jax.ShapeDtypeStruct((rows, dim), F32), jax.ShapeDtypeStruct((2, dim), F32)],
        after=after,
        cost=cost,
    )(far(tokens), far(grad_middle), far(grads), far(w_qkv), far(gains))


def grad_hidden_kernel(count, wo_ref, *refs):
    gh_ref, joined_ref = refs[-2:]

    @pl.when(pl.program_id(0) == 0)
    def _():
        fill(joined_ref, refs[:count])

    gh_ref[...] = mm_nt(joined_ref[...], wo_ref[...]).astype(BF)


def grad_hidden(grads, w_out, first, total, held=(), after=(), cost=0):
    rows = sum(g.shape[0] for g in grads)
    units, dim = w_out.shape
    tile = 1024
    at = first // rows
    held = list(held)
    return call(
        functools.partial(grad_hidden_kernel, len(grads)),
        (units // tile,),
        [pl.BlockSpec((tile, dim), lambda j: (j, 0))]
        + [whole(g.shape) for g in grads]
        + [pl.BlockSpec(memory_space=pltpu.HBM)] * len(held),
        pl.BlockSpec((rows, tile), lambda j: (at, j)),
        pltpu.HBM((total, units), BF),
        scratch=[pltpu.VMEM((rows, dim), BF)],
        aliases={1 + len(grads) + i: i for i in range(len(held))},
        after=after,
        cost=cost,
    )(far(w_out), *grads, *held)


def expert_kernel(count, aliased, wi_ref, gh_ref, *refs):
    blocks = refs[:count]
    outs = refs[count + aliased :]
    h_ref, gp_ref = outs[:2]
    gr_refs = outs[2:-2]
    joined_ref, gr_sum = outs[-2:]
    step = pl.program_id(0)

    @pl.when(step == 0)
    def _():
        fill(joined_ref, blocks)
        gr_sum[...] = jnp.zeros_like(gr_sum)

    slope = 0.7978845608028654

    def preact_of(first):
        return mm(joined_ref[...], wi_ref[:, first : first + SUB])

    def add_rows_grad(first):
        cols = slice(first, first + SUB)
        gr_sum[...] += mm_nt(gp_ref[:, cols], wi_ref[:, cols])

    firsts = list(range(0, wi_ref.shape[1], SUB))
    ahead = preact_of(firsts[0])
    for i, first in enumerate(firsts):
        preact = ahead
        if i + 1 < len(firsts):
            ahead = preact_of(firsts[i + 1])
        if i > 0:
            add_rows_grad(firsts[i - 1])
        cols = slice(first, first + SUB)
        square = preact * preact
        tanh = jnp.tanh(preact * (slope + (slope * 0.044715) * square))
        half = 0.5 + 0.5 * tanh
        hidden = preact * half
        gate = half + hidden * (1.0 - tanh) * (slope + (3.0 * slope * 0.044715) * square)
        h_ref[:, cols] = hidden.astype(BF)
        gp_ref[:, cols] = (gate * gh_ref[:, cols].astype(F32)).astype(BF)
    add_rows_grad(firsts[-1])

    @pl.when(step == pl.num_programs(0) - 1)
    def _():
        at = 0
        for ref in gr_refs:
            ref[...] = gr_sum[at : at + ref.shape[0], :].astype(BF)
            at += ref.shape[0]


def expert(blocks, gh, w_in, first, held=(), out_rows=None, after=(), cost=0):
    count = sum(b.shape[0] for b in blocks)
    dim, units = w_in.shape
    tile = 2048
    at = first // count
    act = pl.BlockSpec((count, tile), lambda j: (at, j))
    shape = pltpu.HBM(gh.shape, BF)
    held = list(held)
    pieces = out_rows or [b.shape[0] for b in blocks]
    return call(
        functools.partial(expert_kernel, len(blocks), len(held)),
        (units // tile,),
        [pl.BlockSpec((dim, tile), lambda j: (0, j)), act]
        + [whole(b.shape) for b in blocks]
        + [pl.BlockSpec(memory_space=pltpu.HBM)] * len(held),
        [act, act] + [whole((n, dim)) for n in pieces],
        [shape, shape] + [pltpu.HBM((n, dim), BF) for n in pieces],
        scratch=[pltpu.VMEM((count, dim), BF), pltpu.VMEM((count, dim), F32)],
        aliases={2 + len(blocks) + i: i for i in range(len(held))},
        after=after,
        cost=cost,
    )(w_in, gh, *blocks, *held)


def turn_kernel(count, *refs):
    o_ref, joined_ref = refs[count:]
    fill(joined_ref, refs[:count])
    o_ref[...] = joined_ref[...].T


def turned(blocks, after=(), cost=0):
    total = sum(b.shape[0] for b in blocks)
    dim = blocks[0].shape[1]
    return call(
        functools.partial(turn_kernel, len(blocks)),
        (1,),
        [whole(b.shape) for b in blocks],
        whole((dim, total)),
        pltpu.HBM((dim, total), BF),
        scratch=[pltpu.VMEM((total, dim), BF)],
        after=after,
        cost=cost,
    )(*blocks)


def produced_kernel(h_ref, wo_ref, *refs):
    o_refs, total_ref = refs[:-1], refs[-1]
    step = pl.program_id(0)
    part = mm(h_ref[...], wo_ref[...])

    @pl.when(step == 0)
    def _():
        total_ref[...] = part

    @pl.when(step > 0)
    def _():
        total_ref[...] += part

    @pl.when(step == pl.num_programs(0) - 1)
    def _():
        at = 0
        for ref in o_refs:
            ref[...] = total_ref[at : at + ref.shape[0], :].astype(BF)
            at += ref.shape[0]


def make_produced(hidden, w_out, pieces, after=(), cost=0):
    rows, units = hidden.shape
    dim = w_out.shape[1]
    tile = 1024
    return call(
        produced_kernel,
        (units // tile,),
        [pl.BlockSpec((rows, tile), lambda j: (0, j)), pl.BlockSpec((tile, dim), lambda j: (j, 0))],
        [whole((n, dim)) for n in pieces],
        [jax.ShapeDtypeStruct((n, dim), BF) for n in pieces],
        scratch=[pltpu.VMEM((rows, dim), F32)],
        after=after,
        cost=cost,
    )(hidden, w_out)


def halves_kernel(count, slots, *refs):
    o_ref = refs[-1]
    for i in range(count):
        o_ref[i * slots : (i + 1) * slots, :] = refs[i][...]


def second_halves(blocks, slots, after=(), cost=0):
    dim = blocks[0].shape[1]
    count = len(blocks)
    return call(
        functools.partial(halves_kernel, count, slots),
        (1,),
        [pl.BlockSpec((slots, dim), lambda i: (1, 0))] * count,
        whole((count * slots, dim)),
        jax.ShapeDtypeStruct((count * slots, dim), BF),
        after=after,
        cost=cost,
    )(*blocks)


def add_kernel(count, *refs):
    outs = refs[2 * count :]
    rows = refs[0].shape[1]
    for i in range(count):
        o_ref, at = outs[i // 2], i % 2
        o_ref[at, :rows, :] = (refs[2 * i][0].astype(F32) + refs[2 * i + 1][0].astype(F32)).astype(BF)
        o_ref[at, rows:, :] = jnp.zeros((o_ref.shape[1] - rows, o_ref.shape[2]), BF)


def add_second(pairs, after=(), cost=0):
    _, rows, cols = pairs[0][0].shape
    steps = rows // TILE
    each = TILE + SPARE
    count = len(pairs)
    block = pl.BlockSpec((1, TILE, cols), lambda i: (1, i, 0))
    return call(
        functools.partial(add_kernel, count),
        (steps,),
        [block] * (2 * count),
        [pl.BlockSpec((2, each, cols), lambda i: (0, i, 0))] * (count // 2),
        [pltpu.HBM((2, steps * each, cols), BF)] * (count // 2),
        after=after,
        cost=cost,
    )(*[far(a) for pair in pairs for a in pair])


def stack_kernel(a_ref, b_ref, o_ref):
    o_ref[0:1, :] = a_ref[0:1, :]
    o_ref[1:2, :] = b_ref[0:1, :]
    o_ref[2:3, :] = a_ref[1:2, :]
    o_ref[3:4, :] = b_ref[1:2, :]


def stack_sums(first, second, after=(), cost=0):
    _, dim = first.shape
    return call(
        stack_kernel,
        (1,),
        [whole(first.shape), whole(second.shape)],
        whole((4, dim)),
        jax.ShapeDtypeStruct((4, dim), F32),
        after=after,
        cost=cost,
    )(first, second)


def weights_kernel(count, puts, table_ref, l_ref, r_ref, *refs):
    half = l_ref.shape[0] // 2
    outs = refs[count:]

    for step, (first, last) in enumerate(puts):

        @pl.when(pl.program_id(0) == step)
        def _(first=first, last=last):
            outs[first][0] = mm(l_ref[:half, :], r_ref[...]).astype(BF)
            outs[last][0] = mm(l_ref[half:, :], r_ref[...]).astype(BF)


def weight_parts(left, right, table, count=4, held=(), after=(), cost=0):
    dim, depth = left.shape
    quarter = right.shape[1] // 4
    half = pltpu.HBM((2, dim // 2, quarter), BF)
    held = list(held)

    def part(until):
        return pl.BlockSpec((1, dim // 2, quarter), lambda i, t: (jnp.where(i <= until, 1, 0), 0, 0))

    if held:
        puts, specs = [(0, 1)], [part(-1), part(-1)]
    else:
        puts, specs = [(0, 1), (0, 3), (2, 1), (2, 3)][:count], [part(0), part(1), part(2), part(2)]
    steps = len(puts)
    return call(
        functools.partial(weights_kernel, len(held), puts),
        (steps,),
        [whole(left.shape), pl.BlockSpec((depth, quarter), lambda i, t: (0, t[i + (3 if held else 0)]))]
        + [pl.BlockSpec(memory_space=pltpu.HBM)] * len(held),
        specs,
        [half] * len(specs),
        prefetch=1,
        aliases={3 + i: i for i in range(len(held))},
        after=after,
        cost=cost,
    )(table, far(left), right, *held)


def joint_kernel(bit_ref, g_ref, ga_ref, n_ref, h_ref, *out_refs):
    low = bit_ref[0] == 0
    for side in range(2):
        keep_ref, send_ref = out_refs[2 * side : 2 * side + 2]
        own = 2 * keep_ref.shape[0]
        cols = keep_ref.shape[2]
        at = slice(side * cols, (side + 1) * cols)
        qkv_part = mm(g_ref[...], n_ref[:, at]).reshape(own, g_ref.shape[0] // own, cols)
        out_part = mm(ga_ref[...], h_ref[:, at]).reshape(own, ga_ref.shape[0] // own, cols)
        both = jnp.concatenate([qkv_part, out_part], axis=1).astype(BF)
        both = both.reshape(own // 2, 2, *both.shape[1:])
        keep_ref[...] = jnp.where(low, both[:, 0], both[:, 1])
        send_ref[...] = jnp.where(low, both[:, 1], both[:, 0])


def joint(grads_t, grad_attn_t, normed, mixed_heads, bit, owners, after=(), cost=0):
    rows, dim = normed.shape
    steps = 4
    cols = dim // 2
    own = owners // steps
    qkv_rows = grads_t.shape[0] // steps
    out_rows = grad_attn_t.shape[0] // steps
    each = (qkv_rows + out_rows) // own
    block = pl.BlockSpec((own // 2, each, cols), lambda i, _: (i, 0, 0))
    return call(
        joint_kernel,
        (steps,),
        [
            pl.BlockSpec((qkv_rows, rows), lambda i, _: (i, 0)),
            pl.BlockSpec((out_rows, rows), lambda i, _: (i, 0)),
            whole((rows, dim)),
            whole((rows, dim)),
        ],
        [block] * 4,
        [pltpu.HBM((owners // 2, each, cols), BF)] * 4,
        prefetch=1,
        after=after,
        cost=cost,
    )(bit, far(grads_t), far(grad_attn_t), far(normed), far(mixed_heads))


def add_split_kernel(shapes, *refs):
    refs = refs[len(shapes) :]
    at = 4 * sum(shapes)
    for parts in shapes:
        keep_ref, send_ref = refs[at : at + 2]
        at += 2
        cols = refs[0].shape[-1]
        for i in range(parts):
            mine_keep, got_keep, mine_send, got_send = refs[:4]
            refs = refs[4:]
            at -= 4
            some = slice(i * cols, (i + 1) * cols)
            keep_ref[..., some] = (mine_keep[...].astype(F32) + got_keep[...].astype(F32)).astype(BF)
            send_ref[..., some] = (mine_send[...].astype(F32) + got_send[...].astype(F32)).astype(BF)


def add_split(sets, after=(), cost=0):
    in_specs, out_specs, out_shape, args, shapes = [], [], [], [], []
    for number, (pairs, bit, inner) in enumerate(sets):
        count, rows, cols = pairs[0][0].shape
        outer = count // (2 * inner)
        inner_each = min(inner, 4)
        outer_each = min(outer, 4 // inner_each)
        inner_steps = inner // inner_each
        steps = outer // outer_each * inner_steps
        block = (outer_each, None, inner_each, rows, cols)

        def spec(flip, number=number, inner_steps=inner_steps, block=block):
            return pl.BlockSpec(
                block, lambda i, *b: (i // inner_steps, b[number][0] ^ flip, i % inner_steps, 0, 0)
            )

        in_specs += [spec(0), spec(0), spec(1), spec(1)] * len(pairs)
        out_specs += [
            pl.BlockSpec(
                (outer_each, inner_each, rows, len(pairs) * cols),
                lambda i, *b, inner_steps=inner_steps: (i // inner_steps, i % inner_steps, 0, 0),
            )
        ] * 2
        out_shape += [jax.ShapeDtypeStruct((outer, inner, rows, len(pairs) * cols), BF)] * 2
        shape = (outer, 2, inner, rows, cols)
        args += [a.reshape(shape) for mine, got in pairs for a in (mine, got, mine, got)]
        shapes.append(len(pairs))
    results = call(
        functools.partial(add_split_kernel, shapes),
        (steps,),
        in_specs,
        out_specs,
        out_shape,
        prefetch=len(sets),
        after=after,
        cost=cost,
    )(*[bit for _, bit, _ in sets], *args)
    results = [r.reshape(-1, *r.shape[2:]) for r in results]
    return [results[i : i + 2] for i in range(0, len(results), 2)]


def add_rows_kernel(count, *refs):
    total = refs[0][...]
    for i in range(1, count):
        total += refs[i][...]
    refs[count][...] = total


def add_rows(values, after=(), cost=0):
    shape = values[0].shape
    return call(
        functools.partial(add_rows_kernel, len(values)),
        (1,),
        [whole(shape)] * len(values),
        whole(shape),
        jax.ShapeDtypeStruct(shape, F32),
        after=after,
        cost=cost,
    )(*values)


def finish_kernel(turn, *refs):
    o_ref = refs[-1]
    rows = refs[0].shape[1]
    total = refs[0][0].astype(F32) + refs[1][0].astype(F32) + refs[2][0, :rows].astype(F32)
    o_ref[...] = total.T if turn else total


def finish(keep, got, last, which, turn, side, held=None, after=(), cost=0):
    _, rows, cols = keep.shape
    tile = TILE
    block = pl.BlockSpec((1, tile, cols), lambda i: (0, i, 0))
    steps = rows // tile
    shape = (cols, 2 * rows) if turn else (2 * rows, cols)
    out = (
        pl.BlockSpec((cols, tile), lambda i: (0, side * steps + i))
        if turn
        else pl.BlockSpec((tile, cols), lambda i: (side * steps + i, 0))
    )
    more = [] if held is None else [held]
    count = len(more)

    def body(*refs):
        finish_kernel(turn, *refs[:3], refs[3 + count])

    return call(
        body,
        (steps,),
        [block] * 2
        + [pl.BlockSpec((1, tile + SPARE, cols), lambda i: (which, i, 0))]
        + [pl.BlockSpec(memory_space=pltpu.HBM)] * count,
        out,
        pltpu.HBM(shape, F32),
        aliases={3: 0} if more else None,
        after=after,
        cost=cost,
    )(far(keep), far(got), far(last), *more)


def swap(value, axis, mask):
    size = lax.axis_size(axis)
    return lax.ppermute(value, axis, [(i, i ^ mask) for i in range(size)])


def bit_of(axis, mask):
    return jnp.where((lax.axis_index(axis) & mask) > 0, 1, 0).astype(jnp.int32).reshape(1)


def bits_of(size):
    return [1 << i for i in range(size.bit_length() - 1)]


def on_device(
    tokens,
    norm_gains,
    norm_biases,
    w_qkv,
    w_attn_out,
    w_in,
    w_out,
    segment_ids,
    expert_ids,
    slots,
    cotangent,
):
    ORDER.clear()
    tok, dim = tokens.shape
    head_dim = dim // HEADS
    wide = lax.axis_size("wide")
    narrow = lax.axis_size("narrow")
    units = w_in.shape[2]
    me_wide = lax.axis_index("wide")
    me_narrow = lax.axis_index("narrow")
    capacity = tok * 9 // (8 * wide)
    w_in = w_in[0]
    w_out = w_out[0]
    zs = wide // 2
    slots_all = zs * capacity
    groups = [list(range(i, i + zs // 4)) for i in range(0, zs, zs // 4)]
    apart = capacity % 16 == 0

    def joinable(blocks):
        return blocks if apart else [jnp.concatenate(blocks, axis=0)]

    def by_position(pieces):
        return list(pieces) if apart else [q for p in pieces for q in jnp.split(p, p.shape[0] // (2 * capacity))]

    def piece_rows(group):
        return [2 * capacity] * len(group) if apart else [2 * capacity * len(group)]

    away = expert_ids ^ me_wide
    kept = slots < capacity
    base = (away >> 1) * capacity + slots
    core = away & 1
    nowhere = 2 * slots_all
    place_own = jnp.where(kept & (core == 0), base, nowhere).astype(jnp.int32)[None, :]
    place_sent = jnp.where(kept & (core == 1), base, nowhere).astype(jnp.int32)[None, :]
    places = [place_own, swap(place_sent, "wide", 1)]
    place_col = jnp.where(kept, core * slots_all + base, nowhere).astype(jnp.int32)[:, None]
    doc_col = segment_ids.reshape(tok, 1)

    def exchange(blocks, positions):
        return [swap(blocks[z], "wide", 2 * z) if z else blocks[z] for z in positions]

    def bring_back(blocks, cost=0):
        if not apart:
            theirs = jnp.concatenate([b[capacity:] for b in blocks], axis=0)
            own = [(jnp.concatenate([b[:capacity] for b in blocks], axis=0), slots_all)]
        else:
            theirs = second_halves(blocks, capacity, cost=cost)
            own = [(b, capacity) for b in blocks]
        return own + [(swap(theirs, "wide", 1), slots_all)]

    cotangent_other = swap(cotangent, "wide", 1)
    normed = first_norm(tokens, norm_gains, norm_biases)
    sent_grads = dispatch_rows(places, [cotangent, cotangent_other], zs, capacity)
    expert_grads = exchange(separate(sent_grads, zs, capacity), range(zs))

    projected = project(normed, w_qkv)
    mixed_heads, mixed_low, log_total = attn_fwd(projected, doc_col, head_dim)
    many = tok - LAST_ROWS
    middle_of = functools.partial(make_middle, tokens, mixed_heads, w_attn_out, norm_gains, norm_biases)
    middle, sent_first = middle_of(0, many)
    other_first = swap(sent_first, "wide", 1)
    gh = grad_hidden(joinable(expert_grads[: zs // 2]), w_out, 0, 2 * slots_all)
    middle, sent_last = middle_of(many, LAST_ROWS, [middle], after=expert_grads, cost=COST_MIDDLE)
    other_last = swap(sent_last, "wide", 1)
    sent_rows = dispatch_rows([p[:, :many] for p in places], [sent_first, other_first], zs, capacity)
    sent_rows = dispatch_rows([p[:, many:] for p in places], [sent_last, other_last], zs, capacity, sent_rows)
    expert_rows = exchange(separate(sent_rows, zs, capacity), range(zs))

    gh = grad_hidden(joinable(expert_grads[zs // 2 :]), w_out, slots_all, 2 * slots_all, [gh])
    grads_t = turned(joinable(expert_grads))
    held = ()
    back_grads = []
    for group in groups:
        blocks = joinable([expert_rows[z] for z in group])
        outs = expert(blocks, gh, w_in, 2 * group[0] * capacity, held, piece_rows(group))
        held = outs[:2]
        pieces = by_position(outs[2:])
        back_grads += exchange({z: pieces[i] for i, z in enumerate(group)}, group)
    hidden, grad_preact = held

    masks = [(1, 2), (2, 1)]
    sides = range(2)
    table = jnp.array([3, 1, 2, 0], jnp.int32) ^ me_narrow

    def first_step(send):
        return [swap(send[side], "narrow", masks[side][0]) for side in sides]

    send_a, send_b, *keep_out = weight_parts(grads_t, hidden, table, 3)
    got_out = first_step([send_a, send_b])
    keep_out = weight_parts(grads_t, hidden, table, 1, keep_out)
    produced = make_produced(hidden, w_out, piece_rows(range(zs)))
    back_rows = exchange(by_position(produced), range(zs))
    rows_t = turned(joinable(expert_rows))
    send_a, send_b, *keep_in = weight_parts(rows_t, grad_preact, table)
    got_in = first_step([send_a, send_b])
    back_grads = bring_back(back_grads, COST_GATE)
    grad_middle, grad_attn_t, grad_heads, sums_two = second_back(
        place_col, middle, cotangent, back_grads, w_attn_out, norm_gains, after=got_out
    )
    attn = functools.partial(
        attn_bwd, projected, mixed_heads, mixed_low, grad_heads, log_total, doc_col, head_dim
    )
    pairs = dim // 128
    held = attn(0, PAIRS_FIRST)
    again = add_second(
        [pair for side in sides for pair in ((keep_out[side], got_out[side]), (keep_in[side], got_in[side]))]
    )
    last = [swap(again[side], "narrow", masks[side][1]) for side in sides]
    grads, grads_all_t = attn(PAIRS_FIRST, pairs - PAIRS_FIRST, held)
    back_rows = bring_back(back_rows)
    grads_all_t = grads_all_t.reshape(3 * dim, tok)

    owners = narrow * wide
    own_qkv = 3 * dim // owners
    n_bits = bits_of(narrow)
    w_bits = bits_of(wide)
    names = [("narrow", b) for b in reversed(n_bits)] + [("wide", b) for b in reversed(w_bits)]
    core_bit = ("wide", 1)
    near = ("wide", w_bits[1])
    orders = [[near, ("narrow", 1), ("narrow", 2)], [("narrow", 1), ("narrow", 2), near]]
    bits = {name: bit_of(*name) for name in names}
    kept_a, sent_a, kept_b, sent_b = joint(
        grads_all_t, grad_attn_t, normed, mixed_heads, bits[core_bit], owners
    )
    got_a, got_b = [swap(sent, *core_bit) for sent in (sent_a, sent_b)]
    state = [(kept_a, got_a, names[:-1]), (kept_b, got_b, names[:-1])]

    def one_step(number, after=()):
        steps = [orders[side][number] for side in sides]
        places_left = [state[side][2].index(steps[side]) for side in sides]
        results = add_split(
            [
                ([state[side][:2]], bits[steps[side]], 1 << (len(state[side][2]) - 1 - places_left[side]))
                for side in sides
            ],
            after=after,
        )
        for side, (kept, sent) in enumerate(results):
            left = list(state[side][2])
            left.remove(steps[side])
            state[side] = (kept, swap(sent, *steps[side]), left)

    rounds = [("narrow", n_bits)] + [("wide", w_bits[i : i + 2]) for i in range(0, len(w_bits), 2)]

    def send_sums(number):
        axis, some = rounds[number]
        others = sorted({sum(c) for c in itertools.product(*[(0, b) for b in some])} - {0})
        return [swap(sums, axis, m) for m in others]

    mixed = make_mixed(place_col, middle, back_rows, cost=9)
    one_step(0, last)
    d_tokens, sums_one = first_back(tokens, grad_middle, grads, w_qkv, norm_gains, cost=12)
    sums = stack_sums(sums_one, sums_two)
    sums_got = send_sums(0)
    sums = add_rows([sums, *sums_got])
    one_step(1)
    sums_got = send_sums(1)
    d_w_out = finish(keep_out[0], got_out[0], last[0], 0, True, 0)
    d_w_out = finish(keep_out[1], got_out[1], last[1], 0, True, 1, d_w_out)
    sums = add_rows([sums, *sums_got])
    one_step(2)
    for number in range(2, len(rounds)):
        sums_got = send_sums(number)
        if number == 2:
            d_w_in = finish(keep_in[0], got_in[0], last[0], 1, False, 0)
            d_w_in = finish(keep_in[1], got_in[1], last[1], 1, False, 1, d_w_in)
        sums = add_rows([sums, *sums_got])
    pairs = [state[side][:2] for side in sides]
    left = state[0][2]
    for step in [("wide", b) for b in w_bits[2:]]:
        at = left.index(step)
        [(kept, sent)] = add_split([(pairs, bits[step], 1 << (len(left) - 1 - at))])
        pairs = [(kept, swap(sent, *step))]
        left = left[:at] + left[at + 1 :]
    value = pairs[0][0][0].astype(F32) + pairs[0][1][0].astype(F32)
    d_w_qkv = value[:own_qkv].T
    d_w_attn_out = value[own_qkv:].T
    own = dim // owners
    sums = lax.dynamic_slice_in_dim(sums, (me_narrow * wide + me_wide) * own, own, 1)
    return (mixed, d_tokens, sums[:2], sums[2:], d_w_qkv, d_w_attn_out, d_w_in[None], d_w_out[None])


def solution(mesh):
    placed = (
        P(("narrow", "wide"), None),
        P(),
        P(),
        P(),
        P(),
        P("wide", None, None),
        P("wide", None, None),
        P(("narrow", "wide"), None),
        P(("narrow", "wide")),
        P(("narrow", "wide")),
        P(("narrow", "wide"), None),
    )
    return jax.shard_map(
        on_device,
        mesh=mesh,
        in_specs=placed,
        out_specs=(
            P(("narrow", "wide"), None),
            P(("narrow", "wide"), None),
            P(None, ("narrow", "wide")),
            P(None, ("narrow", "wide")),
            P(None, ("narrow", "wide")),
            P(None, ("narrow", "wide")),
            P("wide", None, "narrow"),
            P("wide", "narrow", None),
        ),
        check_vma=False,
    )
```

```python
import functools
import itertools

import jax
import jax.numpy as jnp
from jax import lax
from jax.experimental import pallas as pl
from jax.experimental.pallas import tpu as pltpu
from jax.sharding import PartitionSpec as P

HEADS = 16
EPSILON = 1e-05
NEGATIVE = -1e30
BAND = 512
BLOCK = 256
SUB = 512
TILE = 256
SPARE = 16
PARTS = 3
F32 = jnp.float32
BF = jnp.bfloat16
LAST_ROWS = 128
COST_GATE = 6
COST_MIDDLE = 25
PAIRS_FIRST = 5
VMEM_BYTES = 48 * 1024 * 1024


def mm(a, b):
    return lax.dot_general(a, b, (((1,), (0,)), ((), ())), preferred_element_type=F32)


def mm_nt(a, b):
    return lax.dot_general(a, b, (((1,), (1,)), ((), ())), preferred_element_type=F32)


def mm_tn(a, b):
    return lax.dot_general(a, b, (((0,), (0,)), ((), ())), preferred_element_type=F32)


ORDER = []


def call(kernel, grid, in_specs, out_specs, out_shape, scratch=(), prefetch=0, aliases=None, after=(), cost=0):
    count = prefetch + len(in_specs)
    extra = len(after) + len(ORDER)
    order = list(ORDER)
    several = isinstance(out_specs, list)
    outs = len(out_specs) if several else 1

    def body(*refs):
        rest = refs[count + extra :]
        kernel(*refs[:count], *rest[:outs], *rest[outs + 1 :])
        rest[outs][...] = jnp.zeros_like(rest[outs])

    run = pl.pallas_call(
        body,
        grid_spec=pltpu.PrefetchScalarGridSpec(
            num_scalar_prefetch=prefetch,
            grid=grid,
            in_specs=list(in_specs)
            + [pl.BlockSpec(memory_space=pltpu.HBM)] * len(after)
            + [pl.BlockSpec(memory_space=pl.ANY)] * len(ORDER),
            out_specs=[*(out_specs if several else [out_specs]), whole((8, 128))],
            scratch_shapes=list(scratch),
        ),
        out_shape=[*(out_shape if several else [out_shape]), jax.ShapeDtypeStruct((8, 128), F32)],
        input_output_aliases=aliases or {},
        compiler_params=pltpu.CompilerParams(vmem_limit_bytes=VMEM_BYTES),
        cost_estimate=pl.CostEstimate(flops=1 + int(cost * 1.15e9), bytes_accessed=0, transcendentals=0),
    )

    def apply(*args):
        *results, token = run(*args, *[far(a) for a in after], *order)
        ORDER[:] = [token]
        return results if several else results[0]

    return apply


def far(value):
    return pltpu.with_memory_space_constraint(value, pltpu.HBM)


def whole(shape):
    return pl.BlockSpec(shape, lambda *_: (0,) * len(shape))


def normalize(stream):
    average = jnp.mean(stream, axis=-1, keepdims=True)
    centered = stream - average
    inverse = lax.rsqrt(jnp.mean(centered * centered, axis=-1, keepdims=True) + EPSILON)
    return centered * inverse, inverse


def norm_back(unit, inverse, gain, grad):
    scaled = grad * gain
    first = jnp.mean(scaled, axis=-1, keepdims=True)
    second = jnp.mean(scaled * unit, axis=-1, keepdims=True)
    return inverse * (scaled - first - unit * second)


def first_norm_kernel(x_ref, g_ref, b_ref, n_ref):
    unit, _inverse = normalize(x_ref[...].astype(F32))
    n_ref[...] = (unit * g_ref[0:1, :] + b_ref[0:1, :]).astype(BF)


def first_norm(tokens, gains, biases, after=(), cost=0):
    rows, dim = tokens.shape
    block = pl.BlockSpec((256, dim), lambda i: (i, 0))
    return call(
        first_norm_kernel,
        (rows // 256,),
        [block, whole(gains.shape), whole(biases.shape)],
        block,
        pltpu.HBM((rows, dim), BF),
        after=after,
        cost=cost,
    )(far(tokens), far(gains), far(biases))


def project_kernel(n_ref, w_ref, p_ref):
    p_ref[...] = mm(n_ref[...], w_ref[...]).astype(BF)


def project(normed, w_qkv, after=(), cost=0):
    rows, dim = normed.shape
    cols = w_qkv.shape[1]
    tile = 768
    return call(
        project_kernel,
        (cols // tile,),
        [whole((rows, dim)), pl.BlockSpec((dim, tile), lambda j: (0, j))],
        pl.BlockSpec((rows, tile), lambda j: (0, j)),
        jax.ShapeDtypeStruct((rows, cols), BF),
        after=after,
        cost=cost,
    )(far(normed), far(w_qkv))


def fill_masks(col_ref, fq_ref, fk_ref, tri_ref, head_dim):
    length = col_ref.shape[0]
    doc = lax.broadcasted_iota(jnp.int32, fq_ref.shape, 1) % head_dim
    same = doc == col_ref[...]
    fq_ref[...] = jnp.where(same, 1.0, 0.0).astype(BF)
    fk_ref[...] = jnp.where(same, 0.0, NEGATIVE).astype(BF)
    key_pos = lax.broadcasted_iota(jnp.int32, tri_ref.shape, 0)
    query_pos = lax.broadcasted_iota(jnp.int32, tri_ref.shape, 1)
    tri_ref[...] = jnp.where(key_pos <= query_pos, 0.0, NEGATIVE).astype(F32)


def lanes_of(shape, head, head_dim):
    lane = lax.broadcasted_iota(jnp.int32, shape, 1)
    return (lane >= head * head_dim) & (lane < (head + 1) * head_dim)


def attn_fwd_kernel(head_dim, col_ref, q_ref, k_ref, v_ref, o_ref, ol_ref, lse_ref, fq_ref, fk_ref, tri_ref, vt_ref, qh_ref, kh_ref):
    length, pair = q_ref.shape
    scale = head_dim**-0.5
    per = pair // head_dim

    @pl.when(pl.program_id(0) == 0)
    def _():
        fill_masks(col_ref, fq_ref, fk_ref, tri_ref, head_dim)
        vt_ref[...] = jnp.ones_like(vt_ref)

    value_t = v_ref[...].T
    query = q_ref[...] * BF(scale)
    for head in range(per):
        inside = lanes_of(query.shape, head, head_dim)
        vt_ref[head, :head_dim, :] = value_t[head * head_dim : (head + 1) * head_dim, :]
        qh_ref[head] = jnp.where(inside, query, fq_ref[...])
        kh_ref[head] = jnp.where(inside, k_ref[...], fk_ref[...])
    def first_stage(q_first):
        k_first = max(0, q_first - BAND)
        allparts = [[] for _ in range(per)]
        for k_at in range(k_first, q_first + BLOCK, BLOCK):
            for head in range(per):
                scores = mm_nt(kh_ref[head, k_at : k_at + BLOCK, :], qh_ref[head, q_first : q_first + BLOCK, :])
                if k_at == q_first:
                    scores = scores + tri_ref[...]
                allparts[head].append(scores)
        tops = [functools.reduce(jnp.maximum, [jnp.max(p, axis=0, keepdims=True) for p in parts]) for parts in allparts]
        return allparts, tops

    def second_stage(q_first, allparts, tops):
        k_first = max(0, q_first - BAND)
        q_at = slice(q_first, q_first + BLOCK)
        totals = [None] * per
        for i in range(len(allparts[0])):
            k_at = k_first + i * BLOCK
            for head in range(per):
                prob = jnp.exp(allparts[head][i] - tops[head]).astype(BF)
                part = mm(vt_ref[head, :, k_at : k_at + BLOCK], prob)
                totals[head] = part if totals[head] is None else totals[head] + part
        outs = []
        for head in range(per):
            total = totals[head]
            sums = total[head_dim : head_dim + 1, :]
            outs.append(total[:head_dim, :] / sums)
            lse_ref[0, head : head + 1, q_at] = tops[head] + jnp.log(sums)
        o_ref[q_at, :], ol_ref[q_at, :] = in_parts(jnp.concatenate(outs, axis=0).T, 2)

    firsts = list(range(0, length, BLOCK))
    ahead = first_stage(firsts[0])
    for i, q_first in enumerate(firsts):
        now = ahead
        if i + 1 < len(firsts):
            ahead = first_stage(firsts[i + 1])
        second_stage(q_first, *now)


def attn_fwd(projected, doc_col, head_dim, cost=0):
    length = projected.shape[0]
    width = projected.shape[1] // 3
    pair = 128
    pairs = width // pair
    per = pair // head_dim
    specs = [pl.BlockSpec((length, pair), functools.partial(lambda s, j: (0, s * pairs + j), s)) for s in range(3)]
    return call(
        functools.partial(attn_fwd_kernel, head_dim),
        (pairs,),
        [whole(doc_col.shape)] + specs,
        [pl.BlockSpec((length, pair), lambda j: (0, j))] * 2 + [pl.BlockSpec((1, per, length), lambda j: (j, 0, 0))],
        [
            jax.ShapeDtypeStruct((length, width), BF),
            pltpu.HBM((length, width), BF),
            pltpu.HBM((pairs, per, length), F32),
        ],
        scratch=[
            pltpu.VMEM((length, pair), BF),
            pltpu.VMEM((length, pair), BF),
            pltpu.VMEM((BLOCK, BLOCK), F32),
            pltpu.VMEM((per, head_dim + 16, length), BF),
            pltpu.VMEM((per, length, pair), BF),
            pltpu.VMEM((per, length, pair), BF),
        ],
        cost=cost,
    )(doc_col, projected, projected, projected)


def in_parts(x, count):
    parts = []
    for _ in range(count):
        parts.append(x.astype(BF))
        x = x - parts[-1].astype(F32)
    return parts


def attn_bwd_kernel(head_dim, col_ref, q_ref, k_ref, v_ref, o_ref, ol_ref, do_ref, lse_ref, g_ref, gt_ref,
                    fq_ref, fk_ref, tri_ref, qx, kx, vx, dox, qm, dom, dk_sum, dv_sum):
    length, pair = q_ref.shape
    scale = head_dim**-0.5
    per = pair // head_dim

    @pl.when(pl.program_id(0) == 0)
    def _():
        fill_masks(col_ref, fq_ref, fk_ref, tri_ref, head_dim)

    key_t = (k_ref[...] * BF(scale)).T
    query = q_ref[...] * BF(scale)
    grad = do_ref[...]
    lane = lax.broadcasted_iota(jnp.int32, (length, pair), 1)
    zero = jnp.zeros_like(query)
    one = jnp.ones_like(query)
    lse_rows = jnp.concatenate([lse_ref[0], jnp.zeros((8 - per, length), F32)], axis=0)
    lse_cols = lse_rows.T
    product = grad.astype(F32) * (o_ref[...].astype(F32) + ol_ref[...].astype(F32))
    for head in range(per):
        inside = lanes_of(query.shape, head, head_dim)
        slots = [lane == (1 - head) * head_dim + head_dim // 2 + i for i in range(PARTS)]
        some = functools.reduce(jnp.logical_or, slots)
        delta = jnp.sum(jnp.where(inside, product, 0.0), axis=1, keepdims=True)

        def spread(column, rest):
            for slot, part in zip(slots, in_parts(-column, PARTS)):
                rest = jnp.where(slot, part, rest)
            return rest

        qm[head] = jnp.where(inside, query, zero)
        dom[head] = jnp.where(inside, grad, zero)
        qx[head] = jnp.where(inside, query, spread(lse_cols[:, head : head + 1], fq_ref[...]))
        kx[head] = jnp.where(inside, k_ref[...], jnp.where(some, one, fk_ref[...]))
        vx[head] = jnp.where(inside, v_ref[...], jnp.where(some, one, zero))
        dox[head] = jnp.where(inside, grad, spread(delta, zero))
    dk_sum[...] = jnp.zeros_like(dk_sum)
    dv_sum[...] = jnp.zeros_like(dv_sum)
    for q_first in range(0, length, BLOCK):
        q_at = slice(q_first, q_first + BLOCK)
        dq_parts = [None] * per
        for k_first in range(max(0, q_first - BAND), q_first + BLOCK, BLOCK):
            k_at = slice(k_first, k_first + BLOCK)
            scores = [mm_nt(kx[h, k_at, :], qx[h, q_at, :]) for h in range(per)]
            prob_grads = [mm_nt(vx[h, k_at, :], dox[h, q_at, :]) for h in range(per)]
            if k_first == q_first:
                scores = [s + tri_ref[...] for s in scores]
            probs = [jnp.exp(s) for s in scores]
            score_grads = [(p * d).astype(BF) for p, d in zip(probs, prob_grads)]
            probs = [p.astype(BF) for p in probs]
            dv_sum[k_at, :] += mm(
                jnp.concatenate(probs, axis=1), jnp.concatenate([dom[h, q_at, :] for h in range(per)], axis=0)
            )
            dk_sum[k_at, :] += mm(
                jnp.concatenate(score_grads, axis=1), jnp.concatenate([qm[h, q_at, :] for h in range(per)], axis=0)
            )
            for h in range(per):
                one = mm(key_t[h * head_dim : (h + 1) * head_dim, k_at], score_grads[h])
                dq_parts[h] = one if dq_parts[h] is None else dq_parts[h] + one
        dq_t = jnp.concatenate(dq_parts, axis=0)
        gt_ref[0, :, q_at] = dq_t.astype(BF)
        g_ref[0, q_at, :] = dq_t.T.astype(BF)
    for i, ref in ((1, dk_sum), (2, dv_sum)):
        low = ref[...].astype(BF)
        g_ref[i] = low
        gt_ref[i] = low.T


def attn_bwd(projected, mixed_heads, mixed_low, grad_heads, log_total, doc_col, head_dim, first, steps, held=(), after=(), cost=0):
    length = projected.shape[0]
    width = projected.shape[1] // 3
    pair = 128
    pairs = width // pair
    per = pair // head_dim
    specs = [
        pl.BlockSpec((length, pair), functools.partial(lambda s, j: (0, s * pairs + first + j), s)) for s in range(3)
    ]
    held = list(held)
    count = len(held)
    kernel = functools.partial(attn_bwd_kernel, head_dim)
    one = pl.BlockSpec((length, pair), lambda j: (0, first + j))
    return call(
        lambda *refs: kernel(*refs[:8], *refs[8 + count :]),
        (steps,),
        [whole(doc_col.shape)] + specs + [one, one, one, pl.BlockSpec((1, per, length), lambda j: (first + j, 0, 0))]
        + [pl.BlockSpec(memory_space=pltpu.HBM)] * count,
        [
            pl.BlockSpec((3, length, pair), lambda j: (0, 0, first + j)),
            pl.BlockSpec((3, pair, length), lambda j: (0, first + j, 0)),
        ],
        [pltpu.HBM((3, length, width), BF), pltpu.HBM((3, width, length), BF)],
        scratch=[
            pltpu.VMEM((length, pair), BF),
            pltpu.VMEM((length, pair), BF),
            pltpu.VMEM((BLOCK, BLOCK), F32),
        ]
        + [pltpu.VMEM((per, length, pair), BF)] * 6
        + [pltpu.VMEM((length, pair), F32)] * 2,
        aliases={8 + i: i for i in range(count)},
        after=after,
        cost=cost,
    )(doc_col, *[far(a) for a in (projected, projected, projected, mixed_heads, mixed_low, grad_heads, log_total)], *held)


def middle_kernel(x_ref, h_ref, w_ref, g_ref, b_ref, *refs):
    m_ref, s_ref = refs[-2:]
    middle = x_ref[...].astype(F32) + mm(h_ref[...], w_ref[...])
    m_ref[...] = middle
    unit, _inverse = normalize(middle)
    s_ref[...] = (unit * g_ref[1:2, :] + b_ref[1:2, :]).astype(BF)


def make_middle(tokens, mixed_heads, w_attn_out, gains, biases, first, count, held=(), after=(), cost=0):
    rows, dim = tokens.shape
    tile = min(count, 448)
    at = first // tile
    block = pl.BlockSpec((tile, dim), lambda i: (at + i, 0))
    held = list(held)
    return call(
        middle_kernel,
        (count // tile,),
        [block, block, whole(w_attn_out.shape), whole(gains.shape), whole(biases.shape)]
        + [pl.BlockSpec(memory_space=pltpu.HBM)] * len(held),
        [block, pl.BlockSpec((tile, dim), lambda i: (i, 0))],
        [pltpu.HBM((rows, dim), F32), jax.ShapeDtypeStruct((count, dim), BF)],
        aliases={5: 0} if held else None,
        after=after,
        cost=cost,
    )(far(tokens), mixed_heads, far(w_attn_out), far(gains), far(biases), *held)


def dispatch_kernel(slots, added, *refs):
    o_refs = refs[4 + added :]
    count = slots * (o_refs[0].shape[0] // (2 * slots)) * len(o_refs)
    for side in range(2):
        place, rows = refs[side], refs[2 + side]
        slot = lax.broadcasted_iota(jnp.int32, (count, rows.shape[0]), 0)
        low = mm(jnp.where(slot == place[...], 1.0, 0.0).astype(BF), rows[...]).astype(BF)
        for i, ref in enumerate(o_refs):
            each = count // len(o_refs)
            at = slice(side * each, (side + 1) * each)
            part = low[i * each : (i + 1) * each]
            ref[at, :] = part + refs[4 + i][at, :] if added else part


def dispatch_rows(places, rows, positions, slots, added=(), after=(), cost=0):
    dim = rows[0].shape[1]
    count = positions if slots % 16 == 0 else 1
    shape = (2 * slots * (positions // count), dim)
    return call(
        functools.partial(dispatch_kernel, slots, len(added)),
        (1,),
        [whole(a.shape) for a in [*places, *rows]] + [whole(shape)] * len(added),
        [whole(shape)] * count,
        [jax.ShapeDtypeStruct(shape, BF)] * count,
        after=after,
        cost=cost,
    )(*places, *rows, *added)


def dispatch_side_kernel(positions, place_ref, x_ref, *refs):
    o_refs = refs[-positions:]
    slots = o_refs[0].shape[0]
    slot = lax.broadcasted_iota(jnp.int32, (positions * slots, x_ref.shape[0]), 0)
    low = mm(jnp.where(slot == place_ref[...], 1.0, 0.0).astype(BF), x_ref[...]).astype(BF)
    for i, ref in enumerate(o_refs):
        ref[...] = low[i * slots : (i + 1) * slots]


def dispatch_side(place, rows, positions, slots, side, held=(), after=(), cost=0):
    dim = rows.shape[1]
    held = list(held)
    return call(
        functools.partial(dispatch_side_kernel, positions),
        (1,),
        [whole(place.shape), whole(rows.shape)] + [pl.BlockSpec(memory_space=pltpu.HBM)] * len(held),
        [pl.BlockSpec((slots, dim), lambda i: (side, 0))] * positions,
        [pltpu.HBM((2 * slots, dim), BF)] * positions,
        aliases={2 + i: i for i in range(len(held))},
        after=after,
        cost=cost,
    )(place, rows, *held)


def separate(out, positions, slots):
    if len(out) > 1:
        return out
    sides = out[0].reshape(2, positions, slots, out[0].shape[1])
    return [sides[:, p].reshape(2 * slots, out[0].shape[1]) for p in range(positions)]


def fill(joined_ref, block_refs):
    at = 0
    for ref in block_refs:
        joined_ref[at : at + ref.shape[0], :] = ref[...]
        at += ref.shape[0]


def pick_rows(place, back):
    slot = lax.broadcasted_iota(jnp.int32, (place.shape[0], back.shape[0]), 1)
    return mm(jnp.where(slot == place, 1.0, 0.0).astype(BF), back)


def mixed_kernel(count, place_ref, m_ref, *refs):
    o_ref, joined_ref = refs[count:]

    @pl.when(pl.program_id(0) == 0)
    def _():
        fill(joined_ref, refs[:count])

    o_ref[...] = (m_ref[...] + pick_rows(place_ref[...], joined_ref[...])).astype(BF)


def make_mixed(place_col, middle, back, after=(), cost=0):
    rows, dim = middle.shape
    tile = 256
    total = sum(n for _, n in back)
    block = pl.BlockSpec((tile, dim), lambda i: (i, 0))
    return call(
        functools.partial(mixed_kernel, len(back)),
        (rows // tile,),
        [pl.BlockSpec((tile, 1), lambda i: (i, 0)), block] + [whole((n, dim)) for _, n in back],
        block,
        jax.ShapeDtypeStruct((rows, dim), BF),
        scratch=[pltpu.VMEM((total, dim), BF)],
        after=after,
        cost=cost,
    )(place_col, far(middle), *[far(b) for b, _ in back])


def second_back_kernel(count, place_ref, m_ref, c_ref, w_ref, g_ref, *refs):
    gm_ref, gat_ref, gh_ref, sums_ref, joined_ref = refs[count:]

    @pl.when(pl.program_id(0) == 0)
    def _():
        fill(joined_ref, refs[:count])

    grad_sent = pick_rows(place_ref[...], joined_ref[...])
    unit, inverse = normalize(m_ref[...])
    grad_middle = c_ref[...].astype(F32) + norm_back(unit, inverse, g_ref[1:2, :], grad_sent)
    gm_ref[...] = grad_middle
    grad_attn = grad_middle.astype(BF)
    gat_ref[...] = grad_attn.T
    gh_ref[...] = mm_nt(grad_attn, w_ref[...]).astype(BF)
    sums = jnp.concatenate(
        [jnp.sum(grad_sent * unit, axis=0, keepdims=True), jnp.sum(grad_sent, axis=0, keepdims=True)], axis=0
    )

    @pl.when(pl.program_id(0) == 0)
    def _():
        sums_ref[...] = sums

    @pl.when(pl.program_id(0) > 0)
    def _():
        sums_ref[...] += sums


def second_back(place_col, middle, cotangent, back, w_attn_out, gains, after=(), cost=0):
    rows, dim = middle.shape
    tile = 256
    total = sum(n for _, n in back)
    block = pl.BlockSpec((tile, dim), lambda i: (i, 0))
    return call(
        functools.partial(second_back_kernel, len(back)),
        (rows // tile,),
        [pl.BlockSpec((tile, 1), lambda i: (i, 0)), block, block, whole(w_attn_out.shape), whole(gains.shape)]
        + [whole((n, dim)) for _, n in back],
        [block, pl.BlockSpec((dim, tile), lambda i: (0, i)), block, whole((2, dim))],
        [
            pltpu.HBM((rows, dim), F32),
            pltpu.HBM((dim, rows), BF),
            pltpu.HBM((rows, dim), BF),
            jax.ShapeDtypeStruct((2, dim), F32),
        ],
        scratch=[pltpu.VMEM((total, dim), BF)],
        after=after,
        cost=cost,
    )(place_col, far(middle), far(cotangent), far(w_attn_out), far(gains), *[far(b) for b, _ in back])


def first_back_kernel(x_ref, gm_ref, d_ref, w_ref, g_ref, dx_ref, sums_ref):
    dim = x_ref.shape[1]
    grad_normed = mm_nt(d_ref[0], w_ref[:, :dim])
    grad_normed += mm_nt(d_ref[1], w_ref[:, dim : 2 * dim])
    grad_normed += mm_nt(d_ref[2], w_ref[:, 2 * dim :])
    unit, inverse = normalize(x_ref[...].astype(F32))
    dx_ref[...] = gm_ref[...] + norm_back(unit, inverse, g_ref[0:1, :], grad_normed)
    sums = jnp.concatenate(
        [jnp.sum(grad_normed * unit, axis=0, keepdims=True), jnp.sum(grad_normed, axis=0, keepdims=True)], axis=0
    )

    @pl.when(pl.program_id(0) == 0)
    def _():
        sums_ref[...] = sums

    @pl.when(pl.program_id(0) > 0)
    def _():
        sums_ref[...] += sums


def first_back(tokens, grad_middle, grads, w_qkv, gains, after=(), cost=0):
    rows, dim = tokens.shape
    tile = 256
    block = pl.BlockSpec((tile, dim), lambda i: (i, 0))
    return call(
        first_back_kernel,
        (rows // tile,),
        [
            block,
            block,
            pl.BlockSpec((3, tile, dim), lambda i: (0, i, 0)),
            whole(w_qkv.shape),
            whole(gains.shape),
        ],
        [block, whole((2, dim))],
        [jax.ShapeDtypeStruct((rows, dim), F32), jax.ShapeDtypeStruct((2, dim), F32)],
        after=after,
        cost=cost,
    )(far(tokens), far(grad_middle), far(grads), far(w_qkv), far(gains))


def grad_hidden_kernel(count, wo_ref, *refs):
    gh_ref, joined_ref = refs[-2:]

    @pl.when(pl.program_id(0) == 0)
    def _():
        fill(joined_ref, refs[:count])

    gh_ref[...] = mm_nt(joined_ref[...], wo_ref[...]).astype(BF)


def grad_hidden(grads, w_out, first, total, held=(), after=(), cost=0):
    rows = sum(g.shape[0] for g in grads)
    units, dim = w_out.shape
    tile = 1024
    at = first // rows
    held = list(held)
    return call(
        functools.partial(grad_hidden_kernel, len(grads)),
        (units // tile,),
        [pl.BlockSpec((tile, dim), lambda j: (j, 0))]
        + [whole(g.shape) for g in grads]
        + [pl.BlockSpec(memory_space=pltpu.HBM)] * len(held),
        pl.BlockSpec((rows, tile), lambda j: (at, j)),
        pltpu.HBM((total, units), BF),
        scratch=[pltpu.VMEM((rows, dim), BF)],
        aliases={1 + len(grads) + i: i for i in range(len(held))},
        after=after,
        cost=cost,
    )(far(w_out), *grads, *held)


def expert_kernel(count, aliased, wi_ref, gh_ref, *refs):
    blocks = refs[:count]
    outs = refs[count + aliased :]
    h_ref, gp_ref = outs[:2]
    gr_refs = outs[2:-2]
    joined_ref, gr_sum = outs[-2:]
    step = pl.program_id(0)

    @pl.when(step == 0)
    def _():
        fill(joined_ref, blocks)
        gr_sum[...] = jnp.zeros_like(gr_sum)

    slope = 0.7978845608028654

    def preact_of(first):
        return mm(joined_ref[...], wi_ref[:, first : first + SUB])

    def add_rows_grad(first):
        cols = slice(first, first + SUB)
        gr_sum[...] += mm_nt(gp_ref[:, cols], wi_ref[:, cols])

    firsts = list(range(0, wi_ref.shape[1], SUB))
    ahead = preact_of(firsts[0])
    for i, first in enumerate(firsts):
        preact = ahead
        if i + 1 < len(firsts):
            ahead = preact_of(firsts[i + 1])
        if i > 0:
            add_rows_grad(firsts[i - 1])
        cols = slice(first, first + SUB)
        square = preact * preact
        tanh = jnp.tanh(preact * (slope + (slope * 0.044715) * square))
        half = 0.5 + 0.5 * tanh
        hidden = preact * half
        gate = half + hidden * (1.0 - tanh) * (slope + (3.0 * slope * 0.044715) * square)
        h_ref[:, cols] = hidden.astype(BF)
        gp_ref[:, cols] = (gate * gh_ref[:, cols].astype(F32)).astype(BF)
    add_rows_grad(firsts[-1])

    @pl.when(step == pl.num_programs(0) - 1)
    def _():
        at = 0
        for ref in gr_refs:
            ref[...] = gr_sum[at : at + ref.shape[0], :].astype(BF)
            at += ref.shape[0]


def expert(blocks, gh, w_in, first, held=(), out_rows=None, after=(), cost=0):
    count = sum(b.shape[0] for b in blocks)
    dim, units = w_in.shape
    tile = 2048
    at = first // count
    act = pl.BlockSpec((count, tile), lambda j: (at, j))
    shape = pltpu.HBM(gh.shape, BF)
    held = list(held)
    pieces = out_rows or [b.shape[0] for b in blocks]
    return call(
        functools.partial(expert_kernel, len(blocks), len(held)),
        (units // tile,),
        [pl.BlockSpec((dim, tile), lambda j: (0, j)), act]
        + [whole(b.shape) for b in blocks]
        + [pl.BlockSpec(memory_space=pltpu.HBM)] * len(held),
        [act, act] + [whole((n, dim)) for n in pieces],
        [shape, shape] + [pltpu.HBM((n, dim), BF) for n in pieces],
        scratch=[pltpu.VMEM((count, dim), BF), pltpu.VMEM((count, dim), F32)],
        aliases={2 + len(blocks) + i: i for i in range(len(held))},
        after=after,
        cost=cost,
    )(w_in, gh, *blocks, *held)


def turn_kernel(count, *refs):
    o_ref, joined_ref = refs[count:]
    fill(joined_ref, refs[:count])
    o_ref[...] = joined_ref[...].T


def turned(blocks, after=(), cost=0):
    total = sum(b.shape[0] for b in blocks)
    dim = blocks[0].shape[1]
    return call(
        functools.partial(turn_kernel, len(blocks)),
        (1,),
        [whole(b.shape) for b in blocks],
        whole((dim, total)),
        pltpu.HBM((dim, total), BF),
        scratch=[pltpu.VMEM((total, dim), BF)],
        after=after,
        cost=cost,
    )(*blocks)


def produced_kernel(h_ref, wo_ref, *refs):
    o_refs, total_ref = refs[:-1], refs[-1]
    step = pl.program_id(0)
    part = mm(h_ref[...], wo_ref[...])

    @pl.when(step == 0)
    def _():
        total_ref[...] = part

    @pl.when(step > 0)
    def _():
        total_ref[...] += part

    @pl.when(step == pl.num_programs(0) - 1)
    def _():
        at = 0
        for ref in o_refs:
            ref[...] = total_ref[at : at + ref.shape[0], :].astype(BF)
            at += ref.shape[0]


def make_produced(hidden, w_out, pieces, after=(), cost=0):
    rows, units = hidden.shape
    dim = w_out.shape[1]
    tile = 1024
    return call(
        produced_kernel,
        (units // tile,),
        [pl.BlockSpec((rows, tile), lambda j: (0, j)), pl.BlockSpec((tile, dim), lambda j: (j, 0))],
        [whole((n, dim)) for n in pieces],
        [jax.ShapeDtypeStruct((n, dim), BF) for n in pieces],
        scratch=[pltpu.VMEM((rows, dim), F32)],
        after=after,
        cost=cost,
    )(hidden, w_out)


def halves_kernel(count, slots, *refs):
    o_ref = refs[-1]
    for i in range(count):
        o_ref[i * slots : (i + 1) * slots, :] = refs[i][...]


def second_halves(blocks, slots, after=(), cost=0):
    dim = blocks[0].shape[1]
    count = len(blocks)
    return call(
        functools.partial(halves_kernel, count, slots),
        (1,),
        [pl.BlockSpec((slots, dim), lambda i: (1, 0))] * count,
        whole((count * slots, dim)),
        jax.ShapeDtypeStruct((count * slots, dim), BF),
        after=after,
        cost=cost,
    )(*blocks)


def add_kernel(count, *refs):
    outs = refs[2 * count :]
    rows = refs[0].shape[1]
    for i in range(count):
        o_ref, at = outs[i // 2], i % 2
        o_ref[at, :rows, :] = (refs[2 * i][0].astype(F32) + refs[2 * i + 1][0].astype(F32)).astype(BF)
        o_ref[at, rows:, :] = jnp.zeros((o_ref.shape[1] - rows, o_ref.shape[2]), BF)


def add_second(pairs, after=(), cost=0):
    _, rows, cols = pairs[0][0].shape
    steps = rows // TILE
    each = TILE + SPARE
    count = len(pairs)
    block = pl.BlockSpec((1, TILE, cols), lambda i: (1, i, 0))
    return call(
        functools.partial(add_kernel, count),
        (steps,),
        [block] * (2 * count),
        [pl.BlockSpec((2, each, cols), lambda i: (0, i, 0))] * (count // 2),
        [pltpu.HBM((2, steps * each, cols), BF)] * (count // 2),
        after=after,
        cost=cost,
    )(*[far(a) for pair in pairs for a in pair])


def stack_kernel(a_ref, b_ref, o_ref):
    o_ref[0:1, :] = a_ref[0:1, :]
    o_ref[1:2, :] = b_ref[0:1, :]
    o_ref[2:3, :] = a_ref[1:2, :]
    o_ref[3:4, :] = b_ref[1:2, :]


def stack_sums(first, second, after=(), cost=0):
    _, dim = first.shape
    return call(
        stack_kernel,
        (1,),
        [whole(first.shape), whole(second.shape)],
        whole((4, dim)),
        jax.ShapeDtypeStruct((4, dim), F32),
        after=after,
        cost=cost,
    )(first, second)


def weights_kernel(count, puts, table_ref, l_ref, r_ref, *refs):
    half = l_ref.shape[0] // 2
    outs = refs[count:]

    for step, (first, last) in enumerate(puts):

        @pl.when(pl.program_id(0) == step)
        def _(first=first, last=last):
            outs[first][0] = mm(l_ref[:half, :], r_ref[...]).astype(BF)
            outs[last][0] = mm(l_ref[half:, :], r_ref[...]).astype(BF)


def weight_parts(left, right, table, count=4, held=(), after=(), cost=0):
    dim, depth = left.shape
    quarter = right.shape[1] // 4
    half = pltpu.HBM((2, dim // 2, quarter), BF)
    held = list(held)

    def part(until):
        return pl.BlockSpec((1, dim // 2, quarter), lambda i, t: (jnp.where(i <= until, 1, 0), 0, 0))

    if held:
        puts, specs = [(0, 1)], [part(-1), part(-1)]
    else:
        puts, specs = [(0, 1), (0, 3), (2, 1), (2, 3)][:count], [part(0), part(1), part(2), part(2)]
    steps = len(puts)
    return call(
        functools.partial(weights_kernel, len(held), puts),
        (steps,),
        [whole(left.shape), pl.BlockSpec((depth, quarter), lambda i, t: (0, t[i + (3 if held else 0)]))]
        + [pl.BlockSpec(memory_space=pltpu.HBM)] * len(held),
        specs,
        [half] * len(specs),
        prefetch=1,
        aliases={3 + i: i for i in range(len(held))},
        after=after,
        cost=cost,
    )(table, far(left), right, *held)


def joint_kernel(bit_ref, g_ref, ga_ref, n_ref, h_ref, *out_refs):
    low = bit_ref[0] == 0
    for side in range(2):
        keep_ref, send_ref = out_refs[2 * side : 2 * side + 2]
        own = 2 * keep_ref.shape[0]
        cols = keep_ref.shape[2]
        at = slice(side * cols, (side + 1) * cols)
        qkv_part = mm(g_ref[...], n_ref[:, at]).reshape(own, g_ref.shape[0] // own, cols)
        out_part = mm(ga_ref[...], h_ref[:, at]).reshape(own, ga_ref.shape[0] // own, cols)
        both = jnp.concatenate([qkv_part, out_part], axis=1).astype(BF)
        both = both.reshape(own // 2, 2, *both.shape[1:])
        keep_ref[...] = jnp.where(low, both[:, 0], both[:, 1])
        send_ref[...] = jnp.where(low, both[:, 1], both[:, 0])


def joint(grads_t, grad_attn_t, normed, mixed_heads, bit, owners, after=(), cost=0):
    rows, dim = normed.shape
    steps = 4
    cols = dim // 2
    own = owners // steps
    qkv_rows = grads_t.shape[0] // steps
    out_rows = grad_attn_t.shape[0] // steps
    each = (qkv_rows + out_rows) // own
    block = pl.BlockSpec((own // 2, each, cols), lambda i, _: (i, 0, 0))
    return call(
        joint_kernel,
        (steps,),
        [
            pl.BlockSpec((qkv_rows, rows), lambda i, _: (i, 0)),
            pl.BlockSpec((out_rows, rows), lambda i, _: (i, 0)),
            whole((rows, dim)),
            whole((rows, dim)),
        ],
        [block] * 4,
        [pltpu.HBM((owners // 2, each, cols), BF)] * 4,
        prefetch=1,
        after=after,
        cost=cost,
    )(bit, far(grads_t), far(grad_attn_t), far(normed), far(mixed_heads))


def add_half_kernel(shapes, *refs):
    refs = refs[len(shapes) :]
    outs = refs[2 * sum(shapes) :]
    for parts, o_ref in zip(shapes, outs):
        cols = refs[0].shape[-1]
        for i in range(parts):
            mine, got = refs[:2]
            refs = refs[2:]
            o_ref[..., i * cols : (i + 1) * cols] = (mine[...].astype(F32) + got[...].astype(F32)).astype(BF)


def add_half(sets, flip, far_in=False, far_out=False, after=(), cost=0):
    in_specs, out_specs, out_shape, args, shapes = [], [], [], [], []
    for number, (pairs, bit, inner) in enumerate(sets):
        count, rows, cols = pairs[0][0].shape
        outer = count // (2 * inner)
        inner_each = min(inner, 4)
        outer_each = min(outer, 4 // inner_each)
        inner_steps = inner // inner_each
        steps = outer // outer_each * inner_steps

        def at_bit(i, *b, number=number, inner_steps=inner_steps):
            return (i // inner_steps, b[number][0] ^ flip, i % inner_steps, 0, 0)

        def at(i, *b, inner_steps=inner_steps):
            return (i // inner_steps, i % inner_steps, 0, 0)

        in_specs += [pl.BlockSpec((outer_each, None, inner_each, rows, cols), at_bit)] * (2 * len(pairs))
        out_specs.append(pl.BlockSpec((outer_each, inner_each, rows, len(pairs) * cols), at))
        out_shape.append((pltpu.HBM if far_out else jax.ShapeDtypeStruct)((outer, inner, rows, len(pairs) * cols), BF))
        for mine, got in pairs:
            mine, got = [a.reshape(outer, 2, inner, rows, cols) for a in (mine, got)]
            args += [far(mine) if far_in else mine, got]
        shapes.append(len(pairs))
    results = call(
        functools.partial(add_half_kernel, shapes),
        (steps,),
        in_specs,
        out_specs,
        out_shape,
        prefetch=len(sets),
        after=after,
        cost=cost,
    )(*[bit for _, bit, _ in sets], *args)
    return [r.reshape(-1, *r.shape[2:]) for r in results]


def add_rows_kernel(count, *refs):
    total = refs[0][...]
    for i in range(1, count):
        total += refs[i][...]
    refs[count][...] = total


def add_rows(values, after=(), cost=0):
    shape = values[0].shape
    return call(
        functools.partial(add_rows_kernel, len(values)),
        (1,),
        [whole(shape)] * len(values),
        whole(shape),
        jax.ShapeDtypeStruct(shape, F32),
        after=after,
        cost=cost,
    )(*values)


def finish_kernel(turn, *refs):
    o_ref = refs[-1]
    rows = refs[0].shape[1]
    total = refs[0][0].astype(F32) + refs[1][0].astype(F32) + refs[2][0, :rows].astype(F32)
    o_ref[...] = total.T if turn else total


def finish(keep, got, last, which, turn, side, held=None, after=(), cost=0):
    _, rows, cols = keep.shape
    tile = TILE
    block = pl.BlockSpec((1, tile, cols), lambda i: (0, i, 0))
    steps = rows // tile
    shape = (cols, 2 * rows) if turn else (2 * rows, cols)
    out = (
        pl.BlockSpec((cols, tile), lambda i: (0, side * steps + i))
        if turn
        else pl.BlockSpec((tile, cols), lambda i: (side * steps + i, 0))
    )
    more = [] if held is None else [held]
    count = len(more)

    def body(*refs):
        finish_kernel(turn, *refs[:3], refs[3 + count])

    return call(
        body,
        (steps,),
        [block] * 2
        + [pl.BlockSpec((1, tile + SPARE, cols), lambda i: (which, i, 0))]
        + [pl.BlockSpec(memory_space=pltpu.HBM)] * count,
        out,
        pltpu.HBM(shape, F32),
        aliases={3: 0} if more else None,
        after=after,
        cost=cost,
    )(far(keep), far(got), far(last), *more)


def swap(value, axis, mask):
    size = lax.axis_size(axis)
    return lax.ppermute(value, axis, [(i, i ^ mask) for i in range(size)])


def bit_of(axis, mask):
    return jnp.where((lax.axis_index(axis) & mask) > 0, 1, 0).astype(jnp.int32).reshape(1)


def bits_of(size):
    return [1 << i for i in range(size.bit_length() - 1)]


def on_device(
    tokens,
    norm_gains,
    norm_biases,
    w_qkv,
    w_attn_out,
    w_in,
    w_out,
    segment_ids,
    expert_ids,
    slots,
    cotangent,
):
    ORDER.clear()
    tok, dim = tokens.shape
    head_dim = dim // HEADS
    wide = lax.axis_size("wide")
    narrow = lax.axis_size("narrow")
    units = w_in.shape[2]
    me_wide = lax.axis_index("wide")
    me_narrow = lax.axis_index("narrow")
    capacity = tok * 9 // (8 * wide)
    w_in = w_in[0]
    w_out = w_out[0]
    zs = wide // 2
    slots_all = zs * capacity
    groups = [list(range(i, i + zs // 4)) for i in range(0, zs, zs // 4)]
    apart = capacity % 16 == 0

    def joinable(blocks):
        return blocks if apart else [jnp.concatenate(blocks, axis=0)]

    def by_position(pieces):
        return list(pieces) if apart else [q for p in pieces for q in jnp.split(p, p.shape[0] // (2 * capacity))]

    def piece_rows(group):
        return [2 * capacity] * len(group) if apart else [2 * capacity * len(group)]

    away = expert_ids ^ me_wide
    kept = slots < capacity
    base = (away >> 1) * capacity + slots
    core = away & 1
    nowhere = 2 * slots_all
    place_own = jnp.where(kept & (core == 0), base, nowhere).astype(jnp.int32)[None, :]
    place_sent = jnp.where(kept & (core == 1), base, nowhere).astype(jnp.int32)[None, :]
    places = [place_own, swap(place_sent, "wide", 1)]
    place_col = jnp.where(kept, core * slots_all + base, nowhere).astype(jnp.int32)[:, None]
    doc_col = segment_ids.reshape(tok, 1)

    def exchange(blocks, positions):
        return [swap(blocks[z], "wide", 2 * z) if z else blocks[z] for z in positions]

    def bring_back(blocks, cost=0):
        if not apart:
            theirs = jnp.concatenate([b[capacity:] for b in blocks], axis=0)
            own = [(jnp.concatenate([b[:capacity] for b in blocks], axis=0), slots_all)]
        else:
            theirs = second_halves(blocks, capacity, cost=cost)
            own = [(b, capacity) for b in blocks]
        return own + [(swap(theirs, "wide", 1), slots_all)]

    cotangent_other = swap(cotangent, "wide", 1)
    if apart:
        sent_grads = dispatch_side(places[0], far(cotangent), zs, capacity, 0)
        sent_grads = dispatch_side(places[1], cotangent_other, zs, capacity, 1, sent_grads)
    else:
        sent_grads = dispatch_rows(places, [cotangent, cotangent_other], zs, capacity)
    expert_grads = exchange(separate(sent_grads, zs, capacity), range(zs))
    normed = first_norm(tokens, norm_gains, norm_biases)

    projected = project(normed, w_qkv)
    mixed_heads, mixed_low, log_total = attn_fwd(projected, doc_col, head_dim)
    many = tok - LAST_ROWS
    middle_of = functools.partial(make_middle, tokens, mixed_heads, w_attn_out, norm_gains, norm_biases)
    middle, sent_first = middle_of(0, many)
    other_first = swap(sent_first, "wide", 1)
    gh = grad_hidden(joinable(expert_grads[: zs // 2]), w_out, 0, 2 * slots_all)
    middle, sent_last = middle_of(many, LAST_ROWS, [middle], after=expert_grads, cost=COST_MIDDLE)
    other_last = swap(sent_last, "wide", 1)
    sent_rows = dispatch_rows([p[:, :many] for p in places], [sent_first, other_first], zs, capacity)
    sent_rows = dispatch_rows([p[:, many:] for p in places], [sent_last, other_last], zs, capacity, sent_rows)
    expert_rows = exchange(separate(sent_rows, zs, capacity), range(zs))

    gh = grad_hidden(joinable(expert_grads[zs // 2 :]), w_out, slots_all, 2 * slots_all, [gh])
    grads_t = turned(joinable(expert_grads))
    held = ()
    back_grads = []
    for group in groups:
        blocks = joinable([expert_rows[z] for z in group])
        outs = expert(blocks, gh, w_in, 2 * group[0] * capacity, held, piece_rows(group))
        held = outs[:2]
        pieces = by_position(outs[2:])
        back_grads += exchange({z: pieces[i] for i, z in enumerate(group)}, group)
    hidden, grad_preact = held

    masks = [(1, 2), (2, 1)]
    sides = range(2)
    table = jnp.array([3, 1, 2, 0], jnp.int32) ^ me_narrow

    def first_step(send):
        return [swap(send[side], "narrow", masks[side][0]) for side in sides]

    send_a, send_b, *keep_out = weight_parts(grads_t, hidden, table, 3)
    got_out = first_step([send_a, send_b])
    keep_out = weight_parts(grads_t, hidden, table, 1, keep_out)
    produced = make_produced(hidden, w_out, piece_rows(range(zs)))
    back_rows = exchange(by_position(produced), range(zs))
    rows_t = turned(joinable(expert_rows))
    send_a, send_b, *keep_in = weight_parts(rows_t, grad_preact, table)
    got_in = first_step([send_a, send_b])
    back_grads = bring_back(back_grads, COST_GATE)
    grad_middle, grad_attn_t, grad_heads, sums_two = second_back(
        place_col, middle, cotangent, back_grads, w_attn_out, norm_gains, after=got_out
    )
    attn = functools.partial(
        attn_bwd, projected, mixed_heads, mixed_low, grad_heads, log_total, doc_col, head_dim
    )
    pairs = dim // 128
    held = attn(0, PAIRS_FIRST)
    again = add_second(
        [pair for side in sides for pair in ((keep_out[side], got_out[side]), (keep_in[side], got_in[side]))]
    )
    last = [swap(again[side], "narrow", masks[side][1]) for side in sides]
    grads, grads_all_t = attn(PAIRS_FIRST, pairs - PAIRS_FIRST, held)
    back_rows = bring_back(back_rows)
    grads_all_t = grads_all_t.reshape(3 * dim, tok)

    owners = narrow * wide
    own_qkv = 3 * dim // owners
    n_bits = bits_of(narrow)
    w_bits = bits_of(wide)
    names = [("narrow", b) for b in reversed(n_bits)] + [("wide", b) for b in reversed(w_bits)]
    core_bit = ("wide", 1)
    near = ("wide", w_bits[1])
    orders = [[near, ("narrow", 1), ("narrow", 2)], [("narrow", 1), ("narrow", 2), near]]
    bits = {name: bit_of(*name) for name in names}
    kept_a, sent_a, kept_b, sent_b = joint(
        grads_all_t, grad_attn_t, normed, mixed_heads, bits[core_bit], owners
    )
    got_a, got_b = [swap(sent, *core_bit) for sent in (sent_a, sent_b)]
    state = [(kept_a, got_a, names[:-1]), (kept_b, got_b, names[:-1])]

    def one_step(number, after=()):
        steps = [orders[side][number] for side in sides]
        places_left = [state[side][2].index(steps[side]) for side in sides]
        sets = [
            ([state[side][:2]], bits[steps[side]], 1 << (len(state[side][2]) - 1 - places_left[side]))
            for side in sides
        ]
        got = [swap(sent, *steps[side]) for side, sent in enumerate(add_half(sets, 1, number < 2, after=after))]
        for side, kept in enumerate(add_half(sets, 0, number < 2, number == 0, cost=12)):
            left = list(state[side][2])
            left.remove(steps[side])
            state[side] = (kept, got[side], left)

    rounds = [("narrow", n_bits)] + [("wide", w_bits[i : i + 2]) for i in range(0, len(w_bits), 2)]

    def send_sums(number):
        axis, some = rounds[number]
        others = sorted({sum(c) for c in itertools.product(*[(0, b) for b in some])} - {0})
        return [swap(sums, axis, m) for m in others]

    mixed = make_mixed(place_col, middle, back_rows, cost=9)
    one_step(0, last)
    d_tokens, sums_one = first_back(tokens, grad_middle, grads, w_qkv, norm_gains)
    one_step(1)
    sums = stack_sums(sums_one, sums_two)
    sums_got = send_sums(0)
    d_w_out = finish(keep_out[0], got_out[0], last[0], 0, True, 0)
    d_w_out = finish(keep_out[1], got_out[1], last[1], 0, True, 1, d_w_out)
    sums = add_rows([sums, *sums_got])
    one_step(2)
    sums_got = send_sums(1)
    d_w_in = finish(keep_in[0], got_in[0], last[0], 1, False, 0)
    d_w_in = finish(keep_in[1], got_in[1], last[1], 1, False, 1, d_w_in)
    sums = add_rows([sums, *sums_got])
    pairs = [state[side][:2] for side in sides]
    left = state[0][2]
    for number, step in enumerate((("wide", b) for b in w_bits[2:]), 2):
        at = left.index(step)
        sets = [(pairs, bits[step], 1 << (len(left) - 1 - at))]
        got = swap(add_half(sets, 1)[0], *step)
        pairs = [(add_half(sets, 0)[0], got)]
        left = left[:at] + left[at + 1 :]
        sums_got = send_sums(number) if number < len(rounds) else []
        sums = add_rows([sums, *sums_got])
    value = pairs[0][0][0].astype(F32) + pairs[0][1][0].astype(F32)
    d_w_qkv = value[:own_qkv].T
    d_w_attn_out = value[own_qkv:].T
    own = dim // owners
    sums = lax.dynamic_slice_in_dim(sums, (me_narrow * wide + me_wide) * own, own, 1)
    return (mixed, d_tokens, sums[:2], sums[2:], d_w_qkv, d_w_attn_out, d_w_in[None], d_w_out[None])


def solution(mesh):
    placed = (
        P(("narrow", "wide"), None),
        P(),
        P(),
        P(),
        P(),
        P("wide", None, None),
        P("wide", None, None),
        P(("narrow", "wide"), None),
        P(("narrow", "wide")),
        P(("narrow", "wide")),
        P(("narrow", "wide"), None),
    )
    return jax.shard_map(
        on_device,
        mesh=mesh,
        in_specs=placed,
        out_specs=(
            P(("narrow", "wide"), None),
            P(("narrow", "wide"), None),
            P(None, ("narrow", "wide")),
            P(None, ("narrow", "wide")),
            P(None, ("narrow", "wide")),
            P(None, ("narrow", "wide")),
            P("wide", None, "narrow"),
            P("wide", "narrow", None),
        ),
        check_vma=False,
    )
```

```python
import functools
import itertools

import jax
import jax.numpy as jnp
from jax import lax
from jax.experimental import pallas as pl
from jax.experimental.pallas import tpu as pltpu
from jax.sharding import PartitionSpec as P

HEADS = 16
EPSILON = 1e-05
NEGATIVE = -1e30
BAND = 512
BLOCK = 256
SUB = 512
TILE = 256
SPARE = 16
PARTS = 3
F32 = jnp.float32
BF = jnp.bfloat16
LAST_ROWS = 128
COST_GATE = 6
COST_MIDDLE = 25
PAIRS_FIRST = 5
VMEM_BYTES = 48 * 1024 * 1024


def mm(a, b):
    return lax.dot_general(a, b, (((1,), (0,)), ((), ())), preferred_element_type=F32)


def mm_nt(a, b):
    return lax.dot_general(a, b, (((1,), (1,)), ((), ())), preferred_element_type=F32)


def mm_tn(a, b):
    return lax.dot_general(a, b, (((0,), (0,)), ((), ())), preferred_element_type=F32)


ORDER = []


def call(kernel, grid, in_specs, out_specs, out_shape, scratch=(), prefetch=0, aliases=None, after=(), cost=0):
    count = prefetch + len(in_specs)
    extra = len(after) + len(ORDER)
    order = list(ORDER)
    several = isinstance(out_specs, list)
    outs = len(out_specs) if several else 1

    def body(*refs):
        rest = refs[count + extra :]
        kernel(*refs[:count], *rest[:outs], *rest[outs + 1 :])
        rest[outs][...] = jnp.zeros_like(rest[outs])

    run = pl.pallas_call(
        body,
        grid_spec=pltpu.PrefetchScalarGridSpec(
            num_scalar_prefetch=prefetch,
            grid=grid,
            in_specs=list(in_specs)
            + [pl.BlockSpec(memory_space=pltpu.HBM)] * len(after)
            + [pl.BlockSpec(memory_space=pl.ANY)] * len(ORDER),
            out_specs=[*(out_specs if several else [out_specs]), whole((8, 128))],
            scratch_shapes=list(scratch),
        ),
        out_shape=[*(out_shape if several else [out_shape]), jax.ShapeDtypeStruct((8, 128), F32)],
        input_output_aliases=aliases or {},
        compiler_params=pltpu.CompilerParams(vmem_limit_bytes=VMEM_BYTES),
        cost_estimate=pl.CostEstimate(flops=1 + int(cost * 1.15e9), bytes_accessed=0, transcendentals=0),
    )

    def apply(*args):
        *results, token = run(*args, *[far(a) for a in after], *order)
        ORDER[:] = [token]
        return results if several else results[0]

    return apply


def far(value):
    return pltpu.with_memory_space_constraint(value, pltpu.HBM)


def whole(shape):
    return pl.BlockSpec(shape, lambda *_: (0,) * len(shape))


def normalize(stream):
    average = jnp.mean(stream, axis=-1, keepdims=True)
    centered = stream - average
    inverse = lax.rsqrt(jnp.mean(centered * centered, axis=-1, keepdims=True) + EPSILON)
    return centered * inverse, inverse


def norm_back(unit, inverse, gain, grad):
    scaled = grad * gain
    first = jnp.mean(scaled, axis=-1, keepdims=True)
    second = jnp.mean(scaled * unit, axis=-1, keepdims=True)
    return inverse * (scaled - first - unit * second)


def first_norm_kernel(x_ref, g_ref, b_ref, n_ref):
    unit, _inverse = normalize(x_ref[...].astype(F32))
    n_ref[...] = (unit * g_ref[0:1, :] + b_ref[0:1, :]).astype(BF)


def first_norm(tokens, gains, biases, after=(), cost=0):
    rows, dim = tokens.shape
    block = pl.BlockSpec((256, dim), lambda i: (i, 0))
    return call(
        first_norm_kernel,
        (rows // 256,),
        [block, whole(gains.shape), whole(biases.shape)],
        block,
        pltpu.HBM((rows, dim), BF),
        after=after,
        cost=cost,
    )(far(tokens), far(gains), far(biases))


def project_kernel(n_ref, w_ref, p_ref):
    p_ref[...] = mm(n_ref[...], w_ref[...]).astype(BF)


def project(normed, w_qkv, after=(), cost=0):
    rows, dim = normed.shape
    cols = w_qkv.shape[1]
    tile = 768
    return call(
        project_kernel,
        (cols // tile,),
        [whole((rows, dim)), pl.BlockSpec((dim, tile), lambda j: (0, j))],
        pl.BlockSpec((rows, tile), lambda j: (0, j)),
        jax.ShapeDtypeStruct((rows, cols), BF),
        after=after,
        cost=cost,
    )(far(normed), far(w_qkv))


def fill_masks(col_ref, fq_ref, fk_ref, tri_ref, head_dim):
    length = col_ref.shape[0]
    doc = lax.broadcasted_iota(jnp.int32, fq_ref.shape, 1) % head_dim
    same = doc == col_ref[...]
    fq_ref[...] = jnp.where(same, 1.0, 0.0).astype(BF)
    fk_ref[...] = jnp.where(same, 0.0, NEGATIVE).astype(BF)
    key_pos = lax.broadcasted_iota(jnp.int32, tri_ref.shape, 0)
    query_pos = lax.broadcasted_iota(jnp.int32, tri_ref.shape, 1)
    tri_ref[...] = jnp.where(key_pos <= query_pos, 0.0, NEGATIVE).astype(F32)


def lanes_of(shape, head, head_dim):
    lane = lax.broadcasted_iota(jnp.int32, shape, 1)
    return (lane >= head * head_dim) & (lane < (head + 1) * head_dim)


def attn_fwd_kernel(head_dim, col_ref, q_ref, k_ref, v_ref, o_ref, ol_ref, lse_ref, fq_ref, fk_ref, tri_ref, vt_ref, qh_ref, kh_ref):
    length, pair = q_ref.shape
    scale = head_dim**-0.5
    per = pair // head_dim

    @pl.when(pl.program_id(0) == 0)
    def _():
        fill_masks(col_ref, fq_ref, fk_ref, tri_ref, head_dim)
        vt_ref[...] = jnp.ones_like(vt_ref)

    value_t = v_ref[...].T
    query = q_ref[...] * BF(scale)
    for head in range(per):
        inside = lanes_of(query.shape, head, head_dim)
        vt_ref[head, :head_dim, :] = value_t[head * head_dim : (head + 1) * head_dim, :]
        qh_ref[head] = jnp.where(inside, query, fq_ref[...])
        kh_ref[head] = jnp.where(inside, k_ref[...], fk_ref[...])
    def first_stage(q_first):
        k_first = max(0, q_first - BAND)
        allparts = [[] for _ in range(per)]
        for k_at in range(k_first, q_first + BLOCK, BLOCK):
            for head in range(per):
                scores = mm_nt(kh_ref[head, k_at : k_at + BLOCK, :], qh_ref[head, q_first : q_first + BLOCK, :])
                if k_at == q_first:
                    scores = scores + tri_ref[...]
                allparts[head].append(scores)
        tops = [functools.reduce(jnp.maximum, [jnp.max(p, axis=0, keepdims=True) for p in parts]) for parts in allparts]
        return allparts, tops

    def second_stage(q_first, allparts, tops):
        k_first = max(0, q_first - BAND)
        q_at = slice(q_first, q_first + BLOCK)
        totals = [None] * per
        for i in range(len(allparts[0])):
            k_at = k_first + i * BLOCK
            for head in range(per):
                prob = jnp.exp(allparts[head][i] - tops[head]).astype(BF)
                part = mm(vt_ref[head, :, k_at : k_at + BLOCK], prob)
                totals[head] = part if totals[head] is None else totals[head] + part
        outs = []
        for head in range(per):
            total = totals[head]
            sums = total[head_dim : head_dim + 1, :]
            outs.append(total[:head_dim, :] / sums)
            lse_ref[0, head : head + 1, q_at] = tops[head] + jnp.log(sums)
        o_ref[q_at, :], ol_ref[q_at, :] = in_parts(jnp.concatenate(outs, axis=0).T, 2)

    firsts = list(range(0, length, BLOCK))
    ahead = first_stage(firsts[0])
    for i, q_first in enumerate(firsts):
        now = ahead
        if i + 1 < len(firsts):
            ahead = first_stage(firsts[i + 1])
        second_stage(q_first, *now)


def attn_fwd(projected, doc_col, head_dim, cost=0):
    length = projected.shape[0]
    width = projected.shape[1] // 3
    pair = 128
    pairs = width // pair
    per = pair // head_dim
    specs = [pl.BlockSpec((length, pair), functools.partial(lambda s, j: (0, s * pairs + j), s)) for s in range(3)]
    return call(
        functools.partial(attn_fwd_kernel, head_dim),
        (pairs,),
        [whole(doc_col.shape)] + specs,
        [pl.BlockSpec((length, pair), lambda j: (0, j))] * 2 + [pl.BlockSpec((1, per, length), lambda j: (j, 0, 0))],
        [
            jax.ShapeDtypeStruct((length, width), BF),
            pltpu.HBM((length, width), BF),
            pltpu.HBM((pairs, per, length), F32),
        ],
        scratch=[
            pltpu.VMEM((length, pair), BF),
            pltpu.VMEM((length, pair), BF),
            pltpu.VMEM((BLOCK, BLOCK), F32),
            pltpu.VMEM((per, head_dim + 16, length), BF),
            pltpu.VMEM((per, length, pair), BF),
            pltpu.VMEM((per, length, pair), BF),
        ],
        cost=cost,
    )(doc_col, projected, projected, projected)


def in_parts(x, count):
    parts = []
    for _ in range(count):
        parts.append(x.astype(BF))
        x = x - parts[-1].astype(F32)
    return parts


def attn_bwd_kernel(head_dim, col_ref, q_ref, k_ref, v_ref, o_ref, ol_ref, do_ref, lse_ref, g_ref, gt_ref,
                    fq_ref, fk_ref, tri_ref, qx, kx, vx, dox, qm, dom, dk_sum, dv_sum):
    length, pair = q_ref.shape
    scale = head_dim**-0.5
    per = pair // head_dim

    @pl.when(pl.program_id(0) == 0)
    def _():
        fill_masks(col_ref, fq_ref, fk_ref, tri_ref, head_dim)

    key_t = (k_ref[...] * BF(scale)).T
    query = q_ref[...] * BF(scale)
    grad = do_ref[...]
    lane = lax.broadcasted_iota(jnp.int32, (length, pair), 1)
    zero = jnp.zeros_like(query)
    one = jnp.ones_like(query)
    lse_rows = jnp.concatenate([lse_ref[0], jnp.zeros((8 - per, length), F32)], axis=0)
    lse_cols = lse_rows.T
    product = grad.astype(F32) * (o_ref[...].astype(F32) + ol_ref[...].astype(F32))
    for head in range(per):
        inside = lanes_of(query.shape, head, head_dim)
        slots = [lane == (1 - head) * head_dim + head_dim // 2 + i for i in range(PARTS)]
        some = functools.reduce(jnp.logical_or, slots)
        delta = jnp.sum(jnp.where(inside, product, 0.0), axis=1, keepdims=True)

        def spread(column, rest):
            for slot, part in zip(slots, in_parts(-column, PARTS)):
                rest = jnp.where(slot, part, rest)
            return rest

        qm[head] = jnp.where(inside, query, zero)
        dom[head] = jnp.where(inside, grad, zero)
        qx[head] = jnp.where(inside, query, spread(lse_cols[:, head : head + 1], fq_ref[...]))
        kx[head] = jnp.where(inside, k_ref[...], jnp.where(some, one, fk_ref[...]))
        vx[head] = jnp.where(inside, v_ref[...], jnp.where(some, one, zero))
        dox[head] = jnp.where(inside, grad, spread(delta, zero))
    dk_sum[...] = jnp.zeros_like(dk_sum)
    dv_sum[...] = jnp.zeros_like(dv_sum)
    for q_first in range(0, length, BLOCK):
        q_at = slice(q_first, q_first + BLOCK)
        dq_parts = [None] * per
        for k_first in range(max(0, q_first - BAND), q_first + BLOCK, BLOCK):
            k_at = slice(k_first, k_first + BLOCK)
            scores = [mm_nt(kx[h, k_at, :], qx[h, q_at, :]) for h in range(per)]
            prob_grads = [mm_nt(vx[h, k_at, :], dox[h, q_at, :]) for h in range(per)]
            if k_first == q_first:
                scores = [s + tri_ref[...] for s in scores]
            probs = [jnp.exp(s) for s in scores]
            score_grads = [(p * d).astype(BF) for p, d in zip(probs, prob_grads)]
            probs = [p.astype(BF) for p in probs]
            dv_sum[k_at, :] += mm(
                jnp.concatenate(probs, axis=1), jnp.concatenate([dom[h, q_at, :] for h in range(per)], axis=0)
            )
            dk_sum[k_at, :] += mm(
                jnp.concatenate(score_grads, axis=1), jnp.concatenate([qm[h, q_at, :] for h in range(per)], axis=0)
            )
            for h in range(per):
                one = mm(key_t[h * head_dim : (h + 1) * head_dim, k_at], score_grads[h])
                dq_parts[h] = one if dq_parts[h] is None else dq_parts[h] + one
        dq_t = jnp.concatenate(dq_parts, axis=0)
        gt_ref[0, :, q_at] = dq_t.astype(BF)
        g_ref[0, q_at, :] = dq_t.T.astype(BF)
    for i, ref in ((1, dk_sum), (2, dv_sum)):
        low = ref[...].astype(BF)
        g_ref[i] = low
        gt_ref[i] = low.T


def attn_bwd(projected, mixed_heads, mixed_low, grad_heads, log_total, doc_col, head_dim, first, steps, held=(), after=(), cost=0):
    length = projected.shape[0]
    width = projected.shape[1] // 3
    pair = 128
    pairs = width // pair
    per = pair // head_dim
    specs = [
        pl.BlockSpec((length, pair), functools.partial(lambda s, j: (0, s * pairs + first + j), s)) for s in range(3)
    ]
    held = list(held)
    count = len(held)
    kernel = functools.partial(attn_bwd_kernel, head_dim)
    one = pl.BlockSpec((length, pair), lambda j: (0, first + j))
    return call(
        lambda *refs: kernel(*refs[:8], *refs[8 + count :]),
        (steps,),
        [whole(doc_col.shape)] + specs + [one, one, one, pl.BlockSpec((1, per, length), lambda j: (first + j, 0, 0))]
        + [pl.BlockSpec(memory_space=pltpu.HBM)] * count,
        [
            pl.BlockSpec((3, length, pair), lambda j: (0, 0, first + j)),
            pl.BlockSpec((3, pair, length), lambda j: (0, first + j, 0)),
        ],
        [pltpu.HBM((3, length, width), BF), pltpu.HBM((3, width, length), BF)],
        scratch=[
            pltpu.VMEM((length, pair), BF),
            pltpu.VMEM((length, pair), BF),
            pltpu.VMEM((BLOCK, BLOCK), F32),
        ]
        + [pltpu.VMEM((per, length, pair), BF)] * 6
        + [pltpu.VMEM((length, pair), F32)] * 2,
        aliases={8 + i: i for i in range(count)},
        after=after,
        cost=cost,
    )(doc_col, *[far(a) for a in (projected, projected, projected, mixed_heads, mixed_low, grad_heads, log_total)], *held)


def middle_kernel(x_ref, h_ref, w_ref, g_ref, b_ref, *refs):
    m_ref, s_ref = refs[-2:]
    middle = x_ref[...].astype(F32) + mm(h_ref[...], w_ref[...])
    m_ref[...] = middle
    unit, _inverse = normalize(middle)
    s_ref[...] = (unit * g_ref[1:2, :] + b_ref[1:2, :]).astype(BF)


def make_middle(tokens, mixed_heads, w_attn_out, gains, biases, first, count, held=(), after=(), cost=0):
    rows, dim = tokens.shape
    tile = min(count, 448)
    at = first // tile
    block = pl.BlockSpec((tile, dim), lambda i: (at + i, 0))
    held = list(held)
    return call(
        middle_kernel,
        (count // tile,),
        [block, block, whole(w_attn_out.shape), whole(gains.shape), whole(biases.shape)]
        + [pl.BlockSpec(memory_space=pltpu.HBM)] * len(held),
        [block, pl.BlockSpec((tile, dim), lambda i: (i, 0))],
        [pltpu.HBM((rows, dim), F32), jax.ShapeDtypeStruct((count, dim), BF)],
        aliases={5: 0} if held else None,
        after=after,
        cost=cost,
    )(far(tokens), mixed_heads, far(w_attn_out), far(gains), far(biases), *held)


def dispatch_kernel(slots, added, *refs):
    o_refs = refs[4 + added :]
    count = slots * (o_refs[0].shape[0] // (2 * slots)) * len(o_refs)
    for side in range(2):
        place, rows = refs[side], refs[2 + side]
        slot = lax.broadcasted_iota(jnp.int32, (count, rows.shape[0]), 0)
        low = mm(jnp.where(slot == place[...], 1.0, 0.0).astype(BF), rows[...]).astype(BF)
        for i, ref in enumerate(o_refs):
            each = count // len(o_refs)
            at = slice(side * each, (side + 1) * each)
            part = low[i * each : (i + 1) * each]
            ref[at, :] = part + refs[4 + i][at, :] if added else part


def dispatch_rows(places, rows, positions, slots, added=(), after=(), cost=0):
    dim = rows[0].shape[1]
    count = positions if slots % 16 == 0 else 1
    shape = (2 * slots * (positions // count), dim)
    return call(
        functools.partial(dispatch_kernel, slots, len(added)),
        (1,),
        [whole(a.shape) for a in [*places, *rows]] + [whole(shape)] * len(added),
        [whole(shape)] * count,
        [jax.ShapeDtypeStruct(shape, BF)] * count,
        after=after,
        cost=cost,
    )(*places, *rows, *added)


def dispatch_side_kernel(positions, place_ref, x_ref, *refs):
    o_refs = refs[-positions:]
    slots = o_refs[0].shape[0]
    slot = lax.broadcasted_iota(jnp.int32, (positions * slots, x_ref.shape[0]), 0)
    low = mm(jnp.where(slot == place_ref[...], 1.0, 0.0).astype(BF), x_ref[...]).astype(BF)
    for i, ref in enumerate(o_refs):
        ref[...] = low[i * slots : (i + 1) * slots]


def dispatch_side(place, rows, positions, slots, side, held=(), after=(), cost=0):
    dim = rows.shape[1]
    held = list(held)
    return call(
        functools.partial(dispatch_side_kernel, positions),
        (1,),
        [whole(place.shape), whole(rows.shape)] + [pl.BlockSpec(memory_space=pltpu.HBM)] * len(held),
        [pl.BlockSpec((slots, dim), lambda i: (side, 0))] * positions,
        [pltpu.HBM((2 * slots, dim), BF)] * positions,
        aliases={2 + i: i for i in range(len(held))},
        after=after,
        cost=cost,
    )(place, rows, *held)


def separate(out, positions, slots):
    if len(out) > 1:
        return out
    sides = out[0].reshape(2, positions, slots, out[0].shape[1])
    return [sides[:, p].reshape(2 * slots, out[0].shape[1]) for p in range(positions)]


def fill(joined_ref, block_refs):
    at = 0
    for ref in block_refs:
        joined_ref[at : at + ref.shape[0], :] = ref[...]
        at += ref.shape[0]


def pick_rows(place, back):
    slot = lax.broadcasted_iota(jnp.int32, (place.shape[0], back.shape[0]), 1)
    return mm(jnp.where(slot == place, 1.0, 0.0).astype(BF), back)


def mixed_kernel(count, place_ref, m_ref, *refs):
    o_ref, joined_ref = refs[count:]

    @pl.when(pl.program_id(0) == 0)
    def _():
        fill(joined_ref, refs[:count])

    o_ref[...] = (m_ref[...] + pick_rows(place_ref[...], joined_ref[...])).astype(BF)


def make_mixed(place_col, middle, back, after=(), cost=0):
    rows, dim = middle.shape
    tile = 256
    total = sum(n for _, n in back)
    block = pl.BlockSpec((tile, dim), lambda i: (i, 0))
    return call(
        functools.partial(mixed_kernel, len(back)),
        (rows // tile,),
        [pl.BlockSpec((tile, 1), lambda i: (i, 0)), block] + [whole((n, dim)) for _, n in back],
        block,
        jax.ShapeDtypeStruct((rows, dim), BF),
        scratch=[pltpu.VMEM((total, dim), BF)],
        after=after,
        cost=cost,
    )(place_col, far(middle), *[far(b) for b, _ in back])


def second_back_kernel(count, place_ref, m_ref, c_ref, w_ref, g_ref, *refs):
    gm_ref, gat_ref, gh_ref, sums_ref, joined_ref = refs[count:]

    @pl.when(pl.program_id(0) == 0)
    def _():
        fill(joined_ref, refs[:count])

    grad_sent = pick_rows(place_ref[...], joined_ref[...])
    unit, inverse = normalize(m_ref[...])
    grad_middle = c_ref[...].astype(F32) + norm_back(unit, inverse, g_ref[1:2, :], grad_sent)
    gm_ref[...] = grad_middle
    grad_attn = grad_middle.astype(BF)
    gat_ref[...] = grad_attn.T
    gh_ref[...] = mm_nt(grad_attn, w_ref[...]).astype(BF)
    sums = jnp.concatenate(
        [jnp.sum(grad_sent * unit, axis=0, keepdims=True), jnp.sum(grad_sent, axis=0, keepdims=True)], axis=0
    )

    @pl.when(pl.program_id(0) == 0)
    def _():
        sums_ref[...] = sums

    @pl.when(pl.program_id(0) > 0)
    def _():
        sums_ref[...] += sums


def second_back(place_col, middle, cotangent, back, w_attn_out, gains, after=(), cost=0):
    rows, dim = middle.shape
    tile = 256
    total = sum(n for _, n in back)
    block = pl.BlockSpec((tile, dim), lambda i: (i, 0))
    return call(
        functools.partial(second_back_kernel, len(back)),
        (rows // tile,),
        [pl.BlockSpec((tile, 1), lambda i: (i, 0)), block, block, whole(w_attn_out.shape), whole(gains.shape)]
        + [whole((n, dim)) for _, n in back],
        [block, pl.BlockSpec((dim, tile), lambda i: (0, i)), block, whole((2, dim))],
        [
            pltpu.HBM((rows, dim), F32),
            pltpu.HBM((dim, rows), BF),
            pltpu.HBM((rows, dim), BF),
            jax.ShapeDtypeStruct((2, dim), F32),
        ],
        scratch=[pltpu.VMEM((total, dim), BF)],
        after=after,
        cost=cost,
    )(place_col, far(middle), far(cotangent), far(w_attn_out), far(gains), *[far(b) for b, _ in back])


def first_back_kernel(x_ref, gm_ref, d_ref, w_ref, g_ref, dx_ref, sums_ref):
    dim = x_ref.shape[1]
    grad_normed = mm_nt(d_ref[0], w_ref[:, :dim])
    grad_normed += mm_nt(d_ref[1], w_ref[:, dim : 2 * dim])
    grad_normed += mm_nt(d_ref[2], w_ref[:, 2 * dim :])
    unit, inverse = normalize(x_ref[...].astype(F32))
    dx_ref[...] = gm_ref[...] + norm_back(unit, inverse, g_ref[0:1, :], grad_normed)
    sums = jnp.concatenate(
        [jnp.sum(grad_normed * unit, axis=0, keepdims=True), jnp.sum(grad_normed, axis=0, keepdims=True)], axis=0
    )

    @pl.when(pl.program_id(0) == 0)
    def _():
        sums_ref[...] = sums

    @pl.when(pl.program_id(0) > 0)
    def _():
        sums_ref[...] += sums


def first_back(tokens, grad_middle, grads, w_qkv, gains, after=(), cost=0):
    rows, dim = tokens.shape
    tile = 256
    block = pl.BlockSpec((tile, dim), lambda i: (i, 0))
    return call(
        first_back_kernel,
        (rows // tile,),
        [
            block,
            block,
            pl.BlockSpec((3, tile, dim), lambda i: (0, i, 0)),
            whole(w_qkv.shape),
            whole(gains.shape),
        ],
        [block, whole((2, dim))],
        [jax.ShapeDtypeStruct((rows, dim), F32), jax.ShapeDtypeStruct((2, dim), F32)],
        after=after,
        cost=cost,
    )(far(tokens), far(grad_middle), far(grads), far(w_qkv), far(gains))


def grad_hidden_kernel(count, wo_ref, *refs):
    gh_ref, joined_ref = refs[-2:]

    @pl.when(pl.program_id(0) == 0)
    def _():
        fill(joined_ref, refs[:count])

    gh_ref[...] = mm_nt(joined_ref[...], wo_ref[...]).astype(BF)


def grad_hidden(grads, w_out, first, total, held=(), after=(), cost=0):
    rows = sum(g.shape[0] for g in grads)
    units, dim = w_out.shape
    tile = 1024
    at = first // rows
    held = list(held)
    return call(
        functools.partial(grad_hidden_kernel, len(grads)),
        (units // tile,),
        [pl.BlockSpec((tile, dim), lambda j: (j, 0))]
        + [whole(g.shape) for g in grads]
        + [pl.BlockSpec(memory_space=pltpu.HBM)] * len(held),
        pl.BlockSpec((rows, tile), lambda j: (at, j)),
        pltpu.HBM((total, units), BF),
        scratch=[pltpu.VMEM((rows, dim), BF)],
        aliases={1 + len(grads) + i: i for i in range(len(held))},
        after=after,
        cost=cost,
    )(far(w_out), *grads, *held)


def expert_kernel(count, aliased, wi_ref, gh_ref, *refs):
    blocks = refs[:count]
    outs = refs[count + aliased :]
    h_ref, gp_ref = outs[:2]
    gr_refs = outs[2:-2]
    joined_ref, gr_sum = outs[-2:]
    step = pl.program_id(0)

    @pl.when(step == 0)
    def _():
        fill(joined_ref, blocks)
        gr_sum[...] = jnp.zeros_like(gr_sum)

    slope = 0.7978845608028654

    def preact_of(first):
        return mm(joined_ref[...], wi_ref[:, first : first + SUB])

    def add_rows_grad(first):
        cols = slice(first, first + SUB)
        gr_sum[...] += mm_nt(gp_ref[:, cols], wi_ref[:, cols])

    firsts = list(range(0, wi_ref.shape[1], SUB))
    ahead = preact_of(firsts[0])
    for i, first in enumerate(firsts):
        preact = ahead
        if i + 1 < len(firsts):
            ahead = preact_of(firsts[i + 1])
        if i > 0:
            add_rows_grad(firsts[i - 1])
        cols = slice(first, first + SUB)
        square = preact * preact
        tanh = jnp.tanh(preact * (slope + (slope * 0.044715) * square))
        half = 0.5 + 0.5 * tanh
        hidden = preact * half
        gate = half + hidden * (1.0 - tanh) * (slope + (3.0 * slope * 0.044715) * square)
        h_ref[:, cols] = hidden.astype(BF)
        gp_ref[:, cols] = (gate * gh_ref[:, cols].astype(F32)).astype(BF)
    add_rows_grad(firsts[-1])

    @pl.when(step == pl.num_programs(0) - 1)
    def _():
        at = 0
        for ref in gr_refs:
            ref[...] = gr_sum[at : at + ref.shape[0], :].astype(BF)
            at += ref.shape[0]


def expert(blocks, gh, w_in, first, held=(), out_rows=None, after=(), cost=0):
    count = sum(b.shape[0] for b in blocks)
    dim, units = w_in.shape
    tile = 2048
    at = first // count
    act = pl.BlockSpec((count, tile), lambda j: (at, j))
    shape = pltpu.HBM(gh.shape, BF)
    held = list(held)
    pieces = out_rows or [b.shape[0] for b in blocks]
    return call(
        functools.partial(expert_kernel, len(blocks), len(held)),
        (units // tile,),
        [pl.BlockSpec((dim, tile), lambda j: (0, j)), act]
        + [whole(b.shape) for b in blocks]
        + [pl.BlockSpec(memory_space=pltpu.HBM)] * len(held),
        [act, act] + [whole((n, dim)) for n in pieces],
        [shape, shape] + [pltpu.HBM((n, dim), BF) for n in pieces],
        scratch=[pltpu.VMEM((count, dim), BF), pltpu.VMEM((count, dim), F32)],
        aliases={2 + len(blocks) + i: i for i in range(len(held))},
        after=after,
        cost=cost,
    )(w_in, gh, *blocks, *held)


def turn_kernel(count, *refs):
    o_ref, joined_ref = refs[count:]
    fill(joined_ref, refs[:count])
    o_ref[...] = joined_ref[...].T


def turned(blocks, after=(), cost=0):
    total = sum(b.shape[0] for b in blocks)
    dim = blocks[0].shape[1]
    return call(
        functools.partial(turn_kernel, len(blocks)),
        (1,),
        [whole(b.shape) for b in blocks],
        whole((dim, total)),
        pltpu.HBM((dim, total), BF),
        scratch=[pltpu.VMEM((total, dim), BF)],
        after=after,
        cost=cost,
    )(*blocks)


def produced_kernel(h_ref, wo_ref, *refs):
    o_refs, total_ref = refs[:-1], refs[-1]
    step = pl.program_id(0)
    part = mm(h_ref[...], wo_ref[...])

    @pl.when(step == 0)
    def _():
        total_ref[...] = part

    @pl.when(step > 0)
    def _():
        total_ref[...] += part

    @pl.when(step == pl.num_programs(0) - 1)
    def _():
        at = 0
        for ref in o_refs:
            ref[...] = total_ref[at : at + ref.shape[0], :].astype(BF)
            at += ref.shape[0]


def make_produced(hidden, w_out, pieces, after=(), cost=0):
    rows, units = hidden.shape
    dim = w_out.shape[1]
    tile = 1024
    return call(
        produced_kernel,
        (units // tile,),
        [pl.BlockSpec((rows, tile), lambda j: (0, j)), pl.BlockSpec((tile, dim), lambda j: (j, 0))],
        [whole((n, dim)) for n in pieces],
        [jax.ShapeDtypeStruct((n, dim), BF) for n in pieces],
        scratch=[pltpu.VMEM((rows, dim), F32)],
        after=after,
        cost=cost,
    )(hidden, w_out)


def halves_kernel(count, slots, *refs):
    o_ref = refs[-1]
    for i in range(count):
        o_ref[i * slots : (i + 1) * slots, :] = refs[i][...]


def second_halves(blocks, slots, after=(), cost=0):
    dim = blocks[0].shape[1]
    count = len(blocks)
    return call(
        functools.partial(halves_kernel, count, slots),
        (1,),
        [pl.BlockSpec((slots, dim), lambda i: (1, 0))] * count,
        whole((count * slots, dim)),
        jax.ShapeDtypeStruct((count * slots, dim), BF),
        after=after,
        cost=cost,
    )(*blocks)


def add_kernel(count, *refs):
    outs = refs[2 * count :]
    rows = refs[0].shape[1]
    for i in range(count):
        o_ref, at = outs[i // 2], i % 2
        o_ref[at, :rows, :] = (refs[2 * i][0].astype(F32) + refs[2 * i + 1][0].astype(F32)).astype(BF)
        o_ref[at, rows:, :] = jnp.zeros((o_ref.shape[1] - rows, o_ref.shape[2]), BF)


def add_second(pairs, after=(), cost=0):
    _, rows, cols = pairs[0][0].shape
    steps = rows // TILE
    each = TILE + SPARE
    count = len(pairs)
    block = pl.BlockSpec((1, TILE, cols), lambda i: (1, i, 0))
    return call(
        functools.partial(add_kernel, count),
        (steps,),
        [block] * (2 * count),
        [pl.BlockSpec((2, each, cols), lambda i: (0, i, 0))] * (count // 2),
        [pltpu.HBM((2, steps * each, cols), BF)] * (count // 2),
        after=after,
        cost=cost,
    )(*[far(a) for pair in pairs for a in pair])


def stack_kernel(a_ref, b_ref, o_ref):
    o_ref[0:1, :] = a_ref[0:1, :]
    o_ref[1:2, :] = b_ref[0:1, :]
    o_ref[2:3, :] = a_ref[1:2, :]
    o_ref[3:4, :] = b_ref[1:2, :]


def stack_sums(first, second, after=(), cost=0):
    _, dim = first.shape
    return call(
        stack_kernel,
        (1,),
        [whole(first.shape), whole(second.shape)],
        whole((4, dim)),
        jax.ShapeDtypeStruct((4, dim), F32),
        after=after,
        cost=cost,
    )(first, second)


def weights_kernel(count, puts, table_ref, l_ref, r_ref, *refs):
    half = l_ref.shape[0] // 2
    outs = refs[count:]

    for step, (first, last) in enumerate(puts):

        @pl.when(pl.program_id(0) == step)
        def _(first=first, last=last):
            outs[first][0] = mm(l_ref[:half, :], r_ref[...]).astype(BF)
            outs[last][0] = mm(l_ref[half:, :], r_ref[...]).astype(BF)


def weight_parts(left, right, table, count=4, held=(), after=(), cost=0):
    dim, depth = left.shape
    quarter = right.shape[1] // 4
    half = pltpu.HBM((2, dim // 2, quarter), BF)
    held = list(held)

    def part(until):
        return pl.BlockSpec((1, dim // 2, quarter), lambda i, t: (jnp.where(i <= until, 1, 0), 0, 0))

    if held:
        puts, specs = [(0, 1)], [part(-1), part(-1)]
    else:
        puts, specs = [(0, 1), (0, 3), (2, 1), (2, 3)][:count], [part(0), part(1), part(2), part(2)]
    steps = len(puts)
    return call(
        functools.partial(weights_kernel, len(held), puts),
        (steps,),
        [whole(left.shape), pl.BlockSpec((depth, quarter), lambda i, t: (0, t[i + (3 if held else 0)]))]
        + [pl.BlockSpec(memory_space=pltpu.HBM)] * len(held),
        specs,
        [half] * len(specs),
        prefetch=1,
        aliases={3 + i: i for i in range(len(held))},
        after=after,
        cost=cost,
    )(table, far(left), right, *held)


def joint_kernel(bit_ref, g_ref, ga_ref, n_ref, h_ref, *out_refs):
    low = bit_ref[0] == 0
    for side in range(2):
        keep_ref, send_ref = out_refs[2 * side : 2 * side + 2]
        own = 2 * keep_ref.shape[0]
        cols = keep_ref.shape[2]
        at = slice(side * cols, (side + 1) * cols)
        qkv_part = mm(g_ref[...], n_ref[:, at]).reshape(own, g_ref.shape[0] // own, cols)
        out_part = mm(ga_ref[...], h_ref[:, at]).reshape(own, ga_ref.shape[0] // own, cols)
        both = jnp.concatenate([qkv_part, out_part], axis=1).astype(BF)
        both = both.reshape(own // 2, 2, *both.shape[1:])
        keep_ref[...] = jnp.where(low, both[:, 0], both[:, 1])
        send_ref[...] = jnp.where(low, both[:, 1], both[:, 0])


def joint(grads_t, grad_attn_t, normed, mixed_heads, bit, owners, after=(), cost=0):
    rows, dim = normed.shape
    steps = 4
    cols = dim // 2
    own = owners // steps
    qkv_rows = grads_t.shape[0] // steps
    out_rows = grad_attn_t.shape[0] // steps
    each = (qkv_rows + out_rows) // own
    block = pl.BlockSpec((own // 2, each, cols), lambda i, _: (i, 0, 0))
    return call(
        joint_kernel,
        (steps,),
        [
            pl.BlockSpec((qkv_rows, rows), lambda i, _: (i, 0)),
            pl.BlockSpec((out_rows, rows), lambda i, _: (i, 0)),
            whole((rows, dim)),
            whole((rows, dim)),
        ],
        [block] * 4,
        [pltpu.HBM((owners // 2, each, cols), BF)] * 4,
        prefetch=1,
        after=after,
        cost=cost,
    )(bit, far(grads_t), far(grad_attn_t), far(normed), far(mixed_heads))


def add_half_kernel(shapes, *refs):
    refs = refs[len(shapes) :]
    outs = refs[2 * sum(shapes) :]
    for parts, o_ref in zip(shapes, outs):
        cols = refs[0].shape[-1]
        for i in range(parts):
            mine, got = refs[:2]
            refs = refs[2:]
            o_ref[..., i * cols : (i + 1) * cols] = (mine[...].astype(F32) + got[...].astype(F32)).astype(BF)


def add_half(sets, flip, far_in=False, far_out=False, after=(), cost=0):
    in_specs, out_specs, out_shape, args, shapes = [], [], [], [], []
    for number, (pairs, bit, inner) in enumerate(sets):
        count, rows, cols = pairs[0][0].shape
        outer = count // (2 * inner)
        inner_each = min(inner, 4)
        outer_each = min(outer, 4 // inner_each)
        inner_steps = inner // inner_each
        steps = outer // outer_each * inner_steps

        def at_bit(i, *b, number=number, inner_steps=inner_steps):
            return (i // inner_steps, b[number][0] ^ flip, i % inner_steps, 0, 0)

        def at(i, *b, inner_steps=inner_steps):
            return (i // inner_steps, i % inner_steps, 0, 0)

        in_specs += [pl.BlockSpec((outer_each, None, inner_each, rows, cols), at_bit)] * (2 * len(pairs))
        out_specs.append(pl.BlockSpec((outer_each, inner_each, rows, len(pairs) * cols), at))
        out_shape.append((pltpu.HBM if far_out else jax.ShapeDtypeStruct)((outer, inner, rows, len(pairs) * cols), BF))
        for mine, got in pairs:
            mine, got = [a.reshape(outer, 2, inner, rows, cols) for a in (mine, got)]
            args += [far(mine) if far_in else mine, got]
        shapes.append(len(pairs))
    results = call(
        functools.partial(add_half_kernel, shapes),
        (steps,),
        in_specs,
        out_specs,
        out_shape,
        prefetch=len(sets),
        after=after,
        cost=cost,
    )(*[bit for _, bit, _ in sets], *args)
    return [r.reshape(-1, *r.shape[2:]) for r in results]


def add_rows_kernel(count, *refs):
    total = refs[0][...]
    for i in range(1, count):
        total += refs[i][...]
    refs[count][...] = total


def add_rows(values, after=(), cost=0):
    shape = values[0].shape
    return call(
        functools.partial(add_rows_kernel, len(values)),
        (1,),
        [whole(shape)] * len(values),
        whole(shape),
        jax.ShapeDtypeStruct(shape, F32),
        after=after,
        cost=cost,
    )(*values)


def finish_kernel(turn, *refs):
    o_ref = refs[-1]
    rows = refs[0].shape[1]
    total = refs[0][0].astype(F32) + refs[1][0].astype(F32) + refs[2][0, :rows].astype(F32)
    o_ref[...] = total.T if turn else total


def finish(keep, got, last, which, turn, side, held=None, after=(), cost=0):
    _, rows, cols = keep.shape
    tile = TILE
    block = pl.BlockSpec((1, tile, cols), lambda i: (0, i, 0))
    steps = rows // tile
    shape = (cols, 2 * rows) if turn else (2 * rows, cols)
    out = (
        pl.BlockSpec((cols, tile), lambda i: (0, side * steps + i))
        if turn
        else pl.BlockSpec((tile, cols), lambda i: (side * steps + i, 0))
    )
    more = [] if held is None else [held]
    count = len(more)

    def body(*refs):
        finish_kernel(turn, *refs[:3], refs[3 + count])

    return call(
        body,
        (steps,),
        [block] * 2
        + [pl.BlockSpec((1, tile + SPARE, cols), lambda i: (which, i, 0))]
        + [pl.BlockSpec(memory_space=pltpu.HBM)] * count,
        out,
        pltpu.HBM(shape, F32),
        aliases={3: 0} if more else None,
        after=after,
        cost=cost,
    )(far(keep), far(got), far(last), *more)


def swap(value, axis, mask):
    size = lax.axis_size(axis)
    return lax.ppermute(value, axis, [(i, i ^ mask) for i in range(size)])


def bit_of(axis, mask):
    return jnp.where((lax.axis_index(axis) & mask) > 0, 1, 0).astype(jnp.int32).reshape(1)


def bits_of(size):
    return [1 << i for i in range(size.bit_length() - 1)]


def on_device(
    tokens,
    norm_gains,
    norm_biases,
    w_qkv,
    w_attn_out,
    w_in,
    w_out,
    segment_ids,
    expert_ids,
    slots,
    cotangent,
):
    ORDER.clear()
    tok, dim = tokens.shape
    head_dim = dim // HEADS
    wide = lax.axis_size("wide")
    narrow = lax.axis_size("narrow")
    units = w_in.shape[2]
    me_wide = lax.axis_index("wide")
    me_narrow = lax.axis_index("narrow")
    capacity = tok * 9 // (8 * wide)
    w_in = w_in[0]
    w_out = w_out[0]
    zs = wide // 2
    slots_all = zs * capacity
    groups = [list(range(i, i + zs // 4)) for i in range(0, zs, zs // 4)]
    apart = capacity % 16 == 0

    def joinable(blocks):
        return blocks if apart else [jnp.concatenate(blocks, axis=0)]

    def by_position(pieces):
        return list(pieces) if apart else [q for p in pieces for q in jnp.split(p, p.shape[0] // (2 * capacity))]

    def piece_rows(group):
        return [2 * capacity] * len(group) if apart else [2 * capacity * len(group)]

    away = expert_ids ^ me_wide
    kept = slots < capacity
    base = (away >> 1) * capacity + slots
    core = away & 1
    nowhere = 2 * slots_all
    place_own = jnp.where(kept & (core == 0), base, nowhere).astype(jnp.int32)[None, :]
    place_sent = jnp.where(kept & (core == 1), base, nowhere).astype(jnp.int32)[None, :]
    places = [place_own, swap(place_sent, "wide", 1)]
    place_col = jnp.where(kept, core * slots_all + base, nowhere).astype(jnp.int32)[:, None]
    doc_col = segment_ids.reshape(tok, 1)

    def exchange(blocks, positions):
        return [swap(blocks[z], "wide", 2 * z) if z else blocks[z] for z in positions]

    def bring_back(blocks, cost=0):
        if not apart:
            theirs = jnp.concatenate([b[capacity:] for b in blocks], axis=0)
            own = [(jnp.concatenate([b[:capacity] for b in blocks], axis=0), slots_all)]
        else:
            theirs = second_halves(blocks, capacity, cost=cost)
            own = [(b, capacity) for b in blocks]
        return own + [(swap(theirs, "wide", 1), slots_all)]

    cotangent_other = swap(cotangent, "wide", 1)
    if apart:
        sent_grads = dispatch_side(places[0], far(cotangent), zs, capacity, 0)
        sent_grads = dispatch_side(places[1], cotangent_other, zs, capacity, 1, sent_grads)
    else:
        sent_grads = dispatch_rows(places, [cotangent, cotangent_other], zs, capacity)
    expert_grads = exchange(separate(sent_grads, zs, capacity), range(zs))
    normed = first_norm(tokens, norm_gains, norm_biases)

    projected = project(normed, w_qkv)
    mixed_heads, mixed_low, log_total = attn_fwd(projected, doc_col, head_dim)
    many = tok - LAST_ROWS
    middle_of = functools.partial(make_middle, tokens, mixed_heads, w_attn_out, norm_gains, norm_biases)
    middle, sent_first = middle_of(0, many)
    other_first = swap(sent_first, "wide", 1)
    gh = grad_hidden(joinable(expert_grads[: zs // 2]), w_out, 0, 2 * slots_all)
    middle, sent_last = middle_of(many, LAST_ROWS, [middle], after=expert_grads, cost=COST_MIDDLE)
    other_last = swap(sent_last, "wide", 1)
    sent_rows = dispatch_rows([p[:, :many] for p in places], [sent_first, other_first], zs, capacity)
    sent_rows = dispatch_rows([p[:, many:] for p in places], [sent_last, other_last], zs, capacity, sent_rows)
    expert_rows = exchange(separate(sent_rows, zs, capacity), range(zs))

    gh = grad_hidden(joinable(expert_grads[zs // 2 :]), w_out, slots_all, 2 * slots_all, [gh])
    grads_t = turned(joinable(expert_grads))
    held = ()
    back_grads = []
    for group in groups:
        blocks = joinable([expert_rows[z] for z in group])
        outs = expert(blocks, gh, w_in, 2 * group[0] * capacity, held, piece_rows(group))
        held = outs[:2]
        pieces = by_position(outs[2:])
        back_grads += exchange({z: pieces[i] for i, z in enumerate(group)}, group)
    hidden, grad_preact = held

    masks = [(1, 2), (2, 1)]
    sides = range(2)
    table = jnp.array([3, 1, 2, 0], jnp.int32) ^ me_narrow

    def first_step(send):
        return [swap(send[side], "narrow", masks[side][0]) for side in sides]

    send_a, send_b, *keep_out = weight_parts(grads_t, hidden, table, 3)
    got_out = first_step([send_a, send_b])
    keep_out = weight_parts(grads_t, hidden, table, 1, keep_out)
    produced = make_produced(hidden, w_out, piece_rows(range(zs)))
    back_rows = exchange(by_position(produced), range(zs))
    rows_t = turned(joinable(expert_rows))
    send_a, send_b, *keep_in = weight_parts(rows_t, grad_preact, table)
    got_in = first_step([send_a, send_b])
    back_grads = bring_back(back_grads, COST_GATE)
    grad_middle, grad_attn_t, grad_heads, sums_two = second_back(
        place_col, middle, cotangent, back_grads, w_attn_out, norm_gains, after=got_out
    )
    attn = functools.partial(
        attn_bwd, projected, mixed_heads, mixed_low, grad_heads, log_total, doc_col, head_dim
    )
    pairs = dim // 128
    held = attn(0, PAIRS_FIRST)
    again = add_second(
        [pair for side in sides for pair in ((keep_out[side], got_out[side]), (keep_in[side], got_in[side]))]
    )
    last = [swap(again[side], "narrow", masks[side][1]) for side in sides]
    grads, grads_all_t = attn(PAIRS_FIRST, pairs - PAIRS_FIRST, held)
    back_rows = bring_back(back_rows)
    grads_all_t = grads_all_t.reshape(3 * dim, tok)

    owners = narrow * wide
    own_qkv = 3 * dim // owners
    n_bits = bits_of(narrow)
    w_bits = bits_of(wide)
    names = [("narrow", b) for b in reversed(n_bits)] + [("wide", b) for b in reversed(w_bits)]
    core_bit = ("wide", 1)
    near = ("wide", w_bits[1])
    orders = [[near, ("narrow", 1), ("narrow", 2)], [("narrow", 1), ("narrow", 2), near]]
    bits = {name: bit_of(*name) for name in names}
    kept_a, sent_a, kept_b, sent_b = joint(
        grads_all_t, grad_attn_t, normed, mixed_heads, bits[core_bit], owners
    )
    got_a, got_b = [swap(sent, *core_bit) for sent in (sent_a, sent_b)]
    state = [(kept_a, got_a, names[:-1]), (kept_b, got_b, names[:-1])]

    def one_step(number, after=()):
        steps = [orders[side][number] for side in sides]
        places_left = [state[side][2].index(steps[side]) for side in sides]
        sets = [
            ([state[side][:2]], bits[steps[side]], 1 << (len(state[side][2]) - 1 - places_left[side]))
            for side in sides
        ]
        got = [swap(sent, *steps[side]) for side, sent in enumerate(add_half(sets, 1, number < 2, after=after))]
        for side, kept in enumerate(add_half(sets, 0, number < 2, number == 0, cost=12)):
            left = list(state[side][2])
            left.remove(steps[side])
            state[side] = (kept, got[side], left)

    rounds = [("narrow", n_bits)] + [("wide", w_bits[i : i + 2]) for i in range(0, len(w_bits), 2)]

    def send_sums(number):
        axis, some = rounds[number]
        others = sorted({sum(c) for c in itertools.product(*[(0, b) for b in some])} - {0})
        return [swap(sums, axis, m) for m in others]

    mixed = make_mixed(place_col, middle, back_rows, cost=9)
    one_step(0, last)
    d_tokens, sums_one = first_back(tokens, grad_middle, grads, w_qkv, norm_gains)
    one_step(1)
    sums = stack_sums(sums_one, sums_two)
    sums_got = send_sums(0)
    d_w_out = finish(keep_out[0], got_out[0], last[0], 0, True, 0)
    sums = add_rows([sums, *sums_got])
    one_step(2)
    sums_got = send_sums(1)
    d_w_out = finish(keep_out[1], got_out[1], last[1], 0, True, 1, d_w_out)
    d_w_in = finish(keep_in[0], got_in[0], last[0], 1, False, 0)
    sums = add_rows([sums, *sums_got])
    pairs = [state[side][:2] for side in sides]
    left = state[0][2]
    for number, step in enumerate((("wide", b) for b in w_bits[2:]), 2):
        at = left.index(step)
        sets = [(pairs, bits[step], 1 << (len(left) - 1 - at))]
        got = swap(add_half(sets, 1)[0], *step)
        pairs = [(add_half(sets, 0)[0], got)]
        left = left[:at] + left[at + 1 :]
        sums_got = send_sums(number) if number < len(rounds) else []
        if number == 2:
            d_w_in = finish(keep_in[1], got_in[1], last[1], 1, False, 1, d_w_in)
        sums = add_rows([sums, *sums_got])
    value = pairs[0][0][0].astype(F32) + pairs[0][1][0].astype(F32)
    d_w_qkv = value[:own_qkv].T
    d_w_attn_out = value[own_qkv:].T
    own = dim // owners
    sums = lax.dynamic_slice_in_dim(sums, (me_narrow * wide + me_wide) * own, own, 1)
    return (mixed, d_tokens, sums[:2], sums[2:], d_w_qkv, d_w_attn_out, d_w_in[None], d_w_out[None])


def solution(mesh):
    placed = (
        P(("narrow", "wide"), None),
        P(),
        P(),
        P(),
        P(),
        P("wide", None, None),
        P("wide", None, None),
        P(("narrow", "wide"), None),
        P(("narrow", "wide")),
        P(("narrow", "wide")),
        P(("narrow", "wide"), None),
    )
    return jax.shard_map(
        on_device,
        mesh=mesh,
        in_specs=placed,
        out_specs=(
            P(("narrow", "wide"), None),
            P(("narrow", "wide"), None),
            P(None, ("narrow", "wide")),
            P(None, ("narrow", "wide")),
            P(None, ("narrow", "wide")),
            P(None, ("narrow", "wide")),
            P("wide", None, "narrow"),
            P("wide", "narrow", None),
        ),
        check_vma=False,
    )
```
